32 devices in a mesh: seq: 8 (over y, x, core), grp: 4 (over z).
Axes of the slice: x: 2, y: 2, z: 4, core: 2. Of those that a mesh axis runs over, the one named last changes fastest.
Arguments:
- tokens: bfloat16 [8, 2048, 1024], P('grp', 'seq'), may hold values from -6 to 6
- cotangent: bfloat16 [8, 2048, 1024], P('grp', 'seq'), may hold values from -6 to 6
- norm_gain: float32 [1024], replicated, may hold values from 0.5 to 1.5
- in_weight: bfloat16 [1024, 4096], replicated, may hold values from -0.1875 to 0.1875
- conv_weight: float32 [4, 2048], replicated, may hold values from -3 to 3
- conv_bias: float32 [2048], replicated, may hold values from -3 to 3
- select_weight: bfloat16 [2048, 96], replicated, may hold values from -0.125 to 0.125
- rate_weight: bfloat16 [64, 2048], replicated, may hold values from -0.75 to 0.75
- rate_bias: float32 [2048], replicated, may hold values from -5 to -2
- decay_log: float32 [2048, 16], replicated, may hold values from -9 to 2
- skip_gain: float32 [2048], replicated, may hold values from 0.5 to 1.5
- out_weight: bfloat16 [2048, 1024], replicated, may hold values from -0.375 to 0.375
Outputs:
- block_out: bfloat16 [8, 2048, 1024], P('grp', 'seq')
- tokens_grad: bfloat16 [8, 2048, 1024], P('grp', 'seq')
- norm_gain_grad: float32 [1024], P(('seq', 'grp'))
- in_weight_grad: float32 [1024, 4096], P(('seq', 'grp'))
- conv_weight_grad: float32 [4, 2048], P(None, ('seq', 'grp'))
- conv_bias_grad: float32 [2048], P(('seq', 'grp'))
- select_weight_grad: float32 [2048, 96], P(('seq', 'grp'))
- rate_weight_grad: float32 [64, 2048], P(None, ('seq', 'grp'))
- rate_bias_grad: float32 [2048], P(('seq', 'grp'))
- decay_log_grad: float32 [2048, 16], P(('seq', 'grp'))
- skip_gain_grad: float32 [2048], P(('seq', 'grp'))
- out_weight_grad: float32 [2048, 1024], P(('seq', 'grp'))
The draws below stay inside these ranges and needn't reach their ends.
All inputs are finite; a program needn't handle non-finite values.
Results may differ from the reference program's by a relative error of at most 0.0083.
Values may be sent and summed in bfloat16 or wider, within the bound.
No kernel may reach another device: no remote copies, remote signals or barrier semaphores. Data moves between devices by JAX's collectives and lax.ppermute only.
A program may use at most 256 MiB of HBM per device.

```python
import math
from functools import partial
import jax
import jax.numpy as jnp
from jax import lax

D = 1024
DI = 2048
DS = 16
R = 64
KCONV = 4
LENGTH = 2048
BATCH = 8


def shared_rates(key):
    return jnp.exp(jax.random.uniform(key, (DI,), jnp.float32, math.log(0.01), math.log(0.1)))


def draw_rate_bias(key, part):
    base = shared_rates(key)
    return jnp.log(jnp.expm1(base))


def draw_decay_log(key, part):
    base = shared_rates(key)
    key = jax.random.fold_in(key, 23)
    pick_key, spread_key = jax.random.split(key)
    share = 0.5
    spread = jnp.exp(jax.random.uniform(spread_key, (DI, DS), jnp.float32, -math.log(2.0), math.log(2.0)))
    quick = jax.random.uniform(pick_key, (DI, 1), jnp.float32) < share
    rate = jnp.where(quick, 1.0 / (30.0 * base[:, None]), 1.0 / (4.0 * LENGTH * base[:, None]))
    return jnp.log(rate * spread)


def block_scale(key, dims, cuts, least, largest):
    def one(axis_at, blocks):
        heights = jax.random.uniform(jax.random.fold_in(jax.random.fold_in(key, 6), axis_at), (blocks,), jnp.float32, least / len(cuts), largest / len(cuts))
        return jnp.repeat(jnp.exp(heights), dims[axis_at] // blocks).reshape((-1,) + (1,) * (len(dims) - axis_at - 1))

    loudness = one(*cuts[0])
    for cut in cuts[1:]:
        loudness = loudness * one(*cut)
    return loudness


def noise(stream_key, dims, width, reach, shards=(), kind=jnp.bfloat16):
    drawn = jax.random.normal(stream_key, dims, jnp.float32) * width
    if len(shards) > 0:
        drawn = block_scale(stream_key, dims, shards, -0.22, 0.18) * drawn
    return jnp.clip(drawn, min=-reach, max=reach).astype(kind)


def setup_inputs(seed: int = 0) -> dict:
    seeds = jax.random.split(jax.random.key(seed), 13)
    return {
        "tokens": noise(seeds[0], (BATCH, LENGTH, D), 1.0, 6.0, ((0, 4), (1, 8))),
        "cotangent": noise(seeds[1], (BATCH, LENGTH, D), 1.0, 6.0, ((0, 4), (1, 8))),
        "norm_gain": jnp.clip(1.0 + 0.1 * jax.random.normal(seeds[2], (D,), jnp.float32), 0.5, 1.5),
        "in_weight": noise(seeds[3], (D, 2 * DI), D ** -0.5, 0.1875),
        "conv_weight": noise(seeds[4], (KCONV, DI), KCONV ** -0.5, 3.0, (), jnp.float32),
        "conv_bias": noise(seeds[5], (DI,), 0.5, 3.0, (), jnp.float32),
        "select_weight": noise(seeds[6], (DI, R + 2 * DS), DI ** -0.5, 0.125),
        "rate_weight": noise(seeds[7], (R, DI), R ** -0.5, 0.75),
        "rate_bias": draw_rate_bias(jax.random.fold_in(seeds[12], 71), 0),
        "decay_log": draw_decay_log(jax.random.fold_in(seeds[12], 71), 0),
        "skip_gain": jnp.clip(jax.random.uniform(seeds[10], (DI,), jnp.float32, 0.5, 1.5), 0.5, 1.5),
        "out_weight": noise(seeds[11], (DI, D), (DI // 8) ** -0.5, 0.375),
    }


epsilon = 1e-05

@jax.custom_vjp
def low(v):
    return lax.optimization_barrier(v.astype(jnp.bfloat16)).astype(jnp.float32)

@jax.custom_vjp
def low_back(v):
    return v

def low_keep(v):
    return (low(v), None)

def low_pass(kept, grad):
    return (grad,)

def back_keep(v):
    return (v, None)

def back_low(kept, grad):
    return (low(grad),)
low.defvjp(low_keep, low_pass)
low_back.defvjp(back_keep, back_low)

def matmul(left, right):
    return jnp.dot(left, right, precision=lax.Precision.HIGHEST, preferred_element_type=jnp.float32)

def silu(values):
    return values * jax.nn.sigmoid(values)

def scan_block(decay_rates, state, pieces):

    def advance(hidden, token_row):
        step_row, input_row, in_row, out_row = token_row
        hidden = jnp.exp(step_row[:, None] * decay_rates) * hidden + (step_row * input_row)[:, None] * in_row[None, :]
        return (hidden, lax.optimization_barrier(jnp.sum(hidden * out_row[None, :], axis=1)))
    return lax.scan(advance, state, pieces)

def selective(step_sizes, inputs, in_gate, out_gate, decay_rates):
    length = step_sizes.shape[0]
    block_span = math.gcd(length, 64)
    pieces = tuple((piece.reshape(length // block_span, block_span, piece.shape[1]) for piece in (step_sizes, inputs, in_gate, out_gate)))
    start_state = jnp.zeros(decay_rates.shape, jnp.float32)
    final_state, outputs = lax.scan(jax.checkpoint(partial(scan_block, decay_rates)), start_state, pieces)
    return outputs.reshape(length, step_sizes.shape[1])

def layer(tokens, norm_gain, in_weight, conv_weight, conv_bias, select_weight, rate_weight, rate_bias, decay_log, skip_gain, out_weight):
    length = tokens.shape[0]
    inner_width = out_weight.shape[0]
    rank_width = rate_weight.shape[0]
    state_width = decay_log.shape[1]
    taps = conv_weight.shape[0]
    scale = lax.rsqrt(lax.optimization_barrier(jnp.mean(tokens * tokens, axis=1, keepdims=True)) + epsilon)
    normed = low(tokens * scale * norm_gain)
    in_mix = low_back(matmul(normed, in_weight))
    inner_part = low(in_mix[:, :inner_width])
    gate_half = in_mix[:, inner_width:]
    padded = jnp.concatenate([jnp.zeros((taps - 1, inner_width), jnp.float32), inner_part], axis=0)
    conv_pre = conv_bias
    for offset in range(taps):
        conv_pre = conv_pre + conv_weight[offset] * padded[offset:offset + length]
    conv_out = low(silu(conv_pre))
    projected = low_back(matmul(conv_out, select_weight))
    rank_part = low(projected[:, :rank_width])
    in_gate = projected[:, rank_width:rank_width + state_width]
    out_gate = projected[:, rank_width + state_width:]
    step_sizes = jax.nn.softplus(low_back(matmul(rank_part, rate_weight)) + rate_bias)
    decay_rates = -jnp.exp(decay_log)
    scanned = selective(step_sizes, conv_out, in_gate, out_gate, decay_rates)
    gated = low((scanned + skip_gain * conv_out) * silu(gate_half))
    return tokens + matmul(gated, out_weight)

def reference(tokens, cotangent, norm_gain, in_weight, conv_weight, conv_bias, select_weight, rate_weight, rate_bias, decay_log, skip_gain, out_weight):
    weights = (norm_gain.astype(jnp.float32), in_weight.astype(jnp.float32), conv_weight.astype(jnp.float32), conv_bias.astype(jnp.float32), select_weight.astype(jnp.float32), rate_weight.astype(jnp.float32), rate_bias.astype(jnp.float32), decay_log.astype(jnp.float32), skip_gain.astype(jnp.float32), out_weight.astype(jnp.float32))

    def per_sequence(totals, pair):
        row_in, row_grad = pair
        result, pullback = jax.vjp(lambda inputs, params: layer(inputs, *params), row_in.astype(jnp.float32), weights)
        input_grad, param_grads = pullback(row_grad.astype(jnp.float32))
        totals = jax.tree.map(jnp.add, totals, param_grads)
        return (totals, (result.astype(jnp.bfloat16), input_grad.astype(jnp.bfloat16)))
    start_totals = jax.tree.map(jnp.zeros_like, weights)
    totals, (outputs, grads) = lax.scan(per_sequence, start_totals, (tokens, cotangent))
    return (outputs, grads, totals[0], totals[1], totals[2], totals[3], totals[4], totals[5], totals[6], totals[7], totals[8], totals[9])
```

```python
import functools
import math

import jax
import jax.numpy as jnp
from jax import lax
from jax.experimental import pallas as pl
from jax.experimental.pallas import tpu as pltpu
from jax.sharding import PartitionSpec as P

epsilon = 1e-05


f32=jnp.float32; bf16=jnp.bfloat16
LOG2E=1.4426950408889634
N=16; T=16

def merged_kernel(dl_ref, x_ref, g_ref, bb_ref, cb_ref, bdb_ref, bdc_ref, a_ref, hin_ref, lin_ref, e_ref, s_ref,
                  sc_ref, sg_ref, wt_ref, ing_ref, outg_ref, dlog_ref,
                  ur_ref, dr_ref, gr_ref, ub_ref, gb_ref, hb_ref, ab_ref, qb_ref, qd_ref, *, nseq, length, cb):
    rows=nseq*length; nl=cb//128; nch=length//T
    j=pl.program_id(0)
    a2=a_ref[...]*LOG2E
    def lane(l): return slice(l*128,(l+1)*128)
    d_all=dl_ref[...]
    u=d_all*x_ref[...].astype(f32)
    for l in range(nl):
        ur_ref[l]=u[:,lane(l)]
        dr_ref[l]=d_all[:,lane(l)]
        gr_ref[l]=g_ref[:,lane(l)]
    ub_ref[...]=u.astype(bf16)
    gb_ref[...]=g_ref[...].astype(bf16)
    abf=a_ref[...].astype(bf16)
    @pl.when(j==0)
    def _():
        ing_ref[...]=jnp.zeros_like(ing_ref)
        outg_ref[...]=jnp.zeros_like(outg_ref)
    def fwd(ci, h):
        h=[list(x) for x in h]
        for s in range(nseq):
            base=pl.multiple_of(s*length+ci*T,T)
            for k in range(T):
                t=base+k
                bt=bb_ref[t]
                for l in range(nl):
                    d=dr_ref[l,pl.ds(t,1),:]
                    uu=ur_ref[l,pl.ds(t,1),:]
                    f=jnp.exp2(d*a2[:,lane(l)])
                    h[s][l]=f*h[s][l]+uu*bt
                    hb_ref[pl.ds(pl.multiple_of(t*N,N),N),lane(l)]=h[s][l].astype(bf16)
        for s in range(nseq):
            base=pl.multiple_of(s*length+ci*T,T)
            hc=hb_ref[pl.ds(pl.multiple_of(base*N,T*N),T*N),:]
            sc_ref[pl.ds(base,T),:]=jnp.dot(bdc_ref[pl.ds(base,T),:],hc,preferred_element_type=f32)
            outg_ref[pl.ds(base,T),:]+=lax.dot_general(gb_ref[pl.ds(base,T),:],hc,(((1,),(1,)),((),())),preferred_element_type=f32)
        return tuple(tuple(x) for x in h)
    h0=tuple(tuple(hin_ref[s][:,lane(l)] for l in range(nl)) for s in range(nseq))
    lax.fori_loop(0,nch,fwd,h0)
    def bwd(cj, c):
        lam,dlog=c
        lam=[list(x) for x in lam]
        ci=nch-1-cj
        for s in range(nseq):
            base=pl.multiple_of(s*length+ci*T,T)
            for k in reversed(range(T)):
                t=base+k
                ct=cb_ref[t]
                for l in range(nl):
                    d=jnp.broadcast_to(dr_ref[l,pl.ds(t,1),:],(N,128))
                    gg=gr_ref[l,pl.ds(t,1),:]
                    f=jnp.exp2(d*a2[:,lane(l)])
                    a=gg*ct+lam[s][l]
                    lam[s][l]=f*a
                    if k==0:
                        tp=jnp.maximum(t-1, s*length)
                        hp=hb_ref[pl.ds(pl.multiple_of(tp*N,N),N),lane(l)]
                        hp=jnp.where(ci==0, hin_ref[s][:,lane(l)].astype(bf16), hp)
                    else:
                        hp=hb_ref[pl.ds(pl.multiple_of((t-1)*N,N),N),lane(l)]
                    q=lam[s][l].astype(bf16)*hp*abf[:,lane(l)]
                    r=s*T*N+k*N
                    ab_ref[r:r+N,lane(l)]=a.astype(bf16)
                    qb_ref[r:r+N,lane(l)]=q
                    qd_ref[r:r+N,lane(l)]=q*d.astype(bf16)
        for s in range(nseq):
            base=pl.multiple_of(s*length+ci*T,T)
            ac=ab_ref[s*T*N:(s+1)*T*N,:]
            w=jnp.dot(bdb_ref[pl.ds(base,T),:],ac,preferred_element_type=f32)
            qs=jnp.dot(s_ref[...],qb_ref[s*T*N:(s+1)*T*N,:],preferred_element_type=f32)
            dlog=dlog+jnp.dot(e_ref[...],qd_ref[s*T*N:(s+1)*T*N,:],preferred_element_type=f32)
            sg_ref[pl.ds(base,T),:]=qs+w*x_ref[pl.ds(base,T),:].astype(f32)
            wt_ref[pl.ds(base,T),:]=w*dl_ref[pl.ds(base,T),:]
            ing_ref[pl.ds(base,T),:]+=lax.dot_general(ub_ref[pl.ds(base,T),:],ac,(((1,),(1,)),((),())),preferred_element_type=f32)
        return (tuple(tuple(x) for x in lam),dlog)
    l0=tuple(tuple(lin_ref[s][:,lane(l)] for l in range(nl)) for s in range(nseq))
    _,dlog=lax.fori_loop(0,nch,bwd,(l0,jnp.zeros((N,cb),f32)))
    dlog_ref[...]=dlog

def merged(dl,x,g,B,C,A,hin,lin,nseq,length,cb=256):
    rows,ch=dl.shape
    cols=jnp.arange(T*N)//N
    mask=(cols[None,:]==(jnp.arange(rows)%T)[:,None])
    bdb=jnp.where(mask,jnp.tile(B,(1,T)),0).astype(bf16)
    bdc=jnp.where(mask,jnp.tile(C,(1,T)),0).astype(bf16)
    bb=jnp.broadcast_to(B[:,:,None],(rows,N,128))
    cbb=jnp.broadcast_to(C[:,:,None],(rows,N,128))
    e=jnp.tile(jnp.eye(N,dtype=bf16),(1,T))
    s=jnp.repeat(jnp.eye(T,dtype=bf16),N,axis=1)
    colblk=lambda r: pl.BlockSpec((r,cb),lambda j:(0,j))
    st=pl.BlockSpec((nseq,N,cb),lambda j:(0,0,j))
    full=lambda a: pl.BlockSpec(a.shape,lambda j:(0,)*a.ndim, pipeline_mode=pl.Buffered(1))
    outs=(jax.ShapeDtypeStruct((rows,ch),f32),)*3+(jax.ShapeDtypeStruct((rows,T*N),f32),)*2+(jax.ShapeDtypeStruct((N,ch),f32),)
    acc=pl.BlockSpec((rows,T*N),lambda j:(0,0))
    sc,sg,wt,ing,outg,dlog=pl.pallas_call(
        functools.partial(merged_kernel,nseq=nseq,length=length,cb=cb),
        grid=(ch//cb,),
        in_specs=[colblk(rows)]*3+[full(bb),full(cbb),full(bdb),full(bdc),colblk(N),st,st,full(e),full(s)],
        out_specs=[colblk(rows)]*3+[acc,acc,colblk(N)],
        out_shape=outs,
        scratch_shapes=[pltpu.VMEM((cb//128,rows,128),f32)]*3+[pltpu.VMEM((rows,cb),bf16),pltpu.VMEM((rows,cb),bf16),
            pltpu.VMEM((rows*N,cb),bf16)]+[pltpu.VMEM((nseq*T*N,cb),bf16)]*3,
        compiler_params=pltpu.CompilerParams(vmem_limit_bytes=60*2**20,dimension_semantics=("arbitrary",)),
        name="merged",
    )(dl,x,g,bb,cbb,bdb,bdc,A,hin,lin,e,s)
    ext=lambda z: jnp.where(mask,z,0).reshape(rows,T,N).sum(1)
    return sc,sg,wt,ext(ing),ext(outg),dlog

def summary_kernel(dl_ref,x_ref,g_ref,bb_ref,cb_ref,a_ref,he_ref,sb_ref,w_ref,ur_ref,dr_ref,gr_ref,*,nseq,length,cb):
    nl=cb//128; nch=length//T
    a2=a_ref[...]*LOG2E
    def lane(l): return slice(l*128,(l+1)*128)
    d_all=dl_ref[...]
    u=d_all*x_ref[...].astype(f32)
    for l in range(nl):
        ur_ref[l]=u[:,lane(l)]
        dr_ref[l]=d_all[:,lane(l)]
        gr_ref[l]=g_ref[:,lane(l)]
    for s in range(nseq):
        w_ref[s:s+1,:]=jnp.sum(d_all[s*length:(s+1)*length],axis=0,keepdims=True)
    def fwd(ci,c):
        c=[[list(z) for z in y] for y in c]
        for s in range(nseq):
            base=pl.multiple_of(s*length+ci*T,T)
            for k in range(T):
                t=base+k
                bt=bb_ref[t]; ct=cb_ref[t]
                for l in range(nl):
                    h,p,sb=c[s][l]
                    d=dr_ref[l,pl.ds(t,1),:]
                    uu=ur_ref[l,pl.ds(t,1),:]
                    gg=gr_ref[l,pl.ds(t,1),:]
                    f=jnp.exp2(d*a2[:,lane(l)])
                    h=f*h+uu*bt
                    p=p*f
                    sb=sb+p*(gg*ct)
                    c[s][l]=[h,p,sb]
        return tuple(tuple(tuple(z) for z in y) for y in c)
    z=jnp.zeros((N,128),f32)
    c=lax.fori_loop(0,nch,fwd,tuple(tuple((z,z+1,z) for l in range(nl)) for s in range(nseq)))
    for s in range(nseq):
        for l in range(nl):
            he_ref[s,:,lane(l)]=c[s][l][0]
            sb_ref[s,:,lane(l)]=c[s][l][2]

def summary(dl,x,g,B,C,A,nseq,length,cb=256):
    rows,ch=dl.shape
    bb=jnp.broadcast_to(B[:,:,None],(rows,N,128))
    cbb=jnp.broadcast_to(C[:,:,None],(rows,N,128))
    colblk=lambda r: pl.BlockSpec((r,cb),lambda j:(0,j))
    st=pl.BlockSpec((nseq,N,cb),lambda j:(0,0,j))
    full=lambda a: pl.BlockSpec(a.shape,lambda j:(0,)*a.ndim, pipeline_mode=pl.Buffered(1))
    so=jax.ShapeDtypeStruct((nseq,N,ch),f32)
    return pl.pallas_call(
        functools.partial(summary_kernel,nseq=nseq,length=length,cb=cb),
        grid=(ch//cb,),
        in_specs=[colblk(rows)]*3+[full(bb),full(cbb),colblk(N)],
        out_specs=[st,st,colblk(nseq)],
        out_shape=(so,so,jax.ShapeDtypeStruct((nseq,ch),f32)),
        scratch_shapes=[pltpu.VMEM((cb//128,rows,128),f32)]*3,
        compiler_params=pltpu.CompilerParams(vmem_limit_bytes=60*2**20,dimension_semantics=("arbitrary",)),
        name="summary",
    )(dl,x,g,bb,cbb,A)


def flip_bit(axis, bit):
    return [(i, i ^ bit) for i in range(lax.axis_size(axis))]


def bits_of(axis):
    size = lax.axis_size(axis)
    return [1 << k for k in range(size.bit_length() - 1)]


def sum_shares(parts):
    seq_bits, grp_bits = bits_of("seq"), bits_of("grp")
    names = [("seq", b) for b in reversed(seq_bits)] + [("grp", b) for b in reversed(grp_bits)]
    order = [("seq", b) for b in seq_bits] + [("grp", b) for b in grp_bits]
    held = parts.reshape((2,) * len(names) + parts.shape[1:])
    for axis, bit in order:
        place = names.index((axis, bit))
        mine = (lax.axis_index(axis) // bit) % 2
        sent = lax.dynamic_index_in_dim(held, 1 - mine, place, keepdims=False).astype(jnp.bfloat16)
        kept = lax.dynamic_index_in_dim(held, mine, place, keepdims=False)
        got = lax.ppermute(sent, axis, flip_bit(axis, bit))
        held = kept + got.astype(jnp.float32)
        names.remove((axis, bit))
    return held


def exchange(whole, local_end, sent_back, rates):
    count, mine = lax.axis_size("seq"), lax.axis_index("seq")
    entering = jnp.zeros_like(local_end)
    leaving = jnp.zeros_like(sent_back)
    span_before = jnp.zeros_like(whole)
    span_after = jnp.zeros_like(whole)
    width = whole.shape[-1]
    for bit in bits_of("seq"):
        high = whole.astype(jnp.bfloat16)
        low = (whole - high.astype(jnp.float32)).astype(jnp.bfloat16)
        block = jnp.concatenate(
            [
                local_end.astype(jnp.bfloat16).reshape(-1, width),
                sent_back.astype(jnp.bfloat16).reshape(-1, width),
                high,
                low,
            ],
            axis=0,
        )
        got = lax.ppermute(block, "seq", flip_bit("seq", bit)).astype(jnp.float32)
        rows = local_end.shape[0] * local_end.shape[1]
        their_end = got[:rows].reshape(local_end.shape)
        their_back = got[rows : 2 * rows].reshape(local_end.shape)
        their_whole = got[2 * rows : 2 * rows + 2] + got[2 * rows + 2 :]
        upper = (mine // bit) % 2 == 1
        decay = lambda span: jnp.exp(span[:, None, :] * rates)
        entering = jnp.where(upper, decay(span_before) * their_end + entering, entering)
        leaving = jnp.where(upper, leaving, decay(span_after) * their_back + leaving)
        span_before = jnp.where(upper, span_before + their_whole, span_before)
        span_after = jnp.where(upper, span_after, span_after + their_whole)
        local_end = jnp.where(
            upper,
            decay(whole) * their_end + local_end,
            decay(their_whole) * local_end + their_end,
        )
        sent_back = jnp.where(
            upper,
            decay(their_whole) * sent_back + their_back,
            decay(whole) * their_back + sent_back,
        )
        whole = whole + their_whole
    return entering, leaving


def passed_along(block, axis, distance):
    devices = range(lax.axis_size(axis))
    route = [(i - distance, i) for i in devices if i - distance in devices]
    return lax.ppermute(block, axis, route)


def silu(values):
    return values * jax.nn.sigmoid(values)


def silu_slope(values):
    sigma = jax.nn.sigmoid(values)
    return sigma * (1.0 + values * (1.0 - sigma))


def contract_rows(left, right):
    return lax.dot_general(
        left, right, (((0,), (0,)), ((), ())), preferred_element_type=jnp.float32
    )


def times_transpose(left, right):
    return lax.dot_general(
        left, right, (((1,), (1,)), ((), ())), preferred_element_type=jnp.float32
    )


def shards(
    tokens,
    cotangent,
    norm_gain,
    in_weight,
    conv_weight,
    conv_bias,
    select_weight,
    rate_weight,
    rate_bias,
    decay_log,
    skip_gain,
    out_weight,
):
    seq_count, length, model_width = tokens.shape
    inner_width = out_weight.shape[0]
    rank_width = rate_weight.shape[0]
    state_width = decay_log.shape[1]
    taps = conv_weight.shape[0]
    row_count = seq_count * length
    share_count = lax.axis_size("seq") * lax.axis_size("grp")
    wide = lambda v: v.astype(jnp.float32)
    flat_tokens = wide(tokens.reshape(row_count, model_width))
    out_flat = cotangent.reshape(row_count, model_width)
    scale = lax.rsqrt(jnp.mean(flat_tokens * flat_tokens, axis=1, keepdims=True) + epsilon)
    normed = (flat_tokens * scale * norm_gain).astype(jnp.bfloat16)
    in_mix = jnp.dot(normed, in_weight, preferred_element_type=jnp.float32)
    inner_part = in_mix[:, :inner_width].astype(jnp.bfloat16).reshape(seq_count, length, inner_width)
    gate_half = in_mix[:, inner_width:]
    previous = passed_along(inner_part[:, length - taps + 1 :], "seq", 1)
    padded = wide(jnp.concatenate([previous, inner_part], axis=1))
    conv_pre = conv_bias
    for k in range(taps):
        conv_pre = conv_pre + conv_weight[k] * padded[:, k : k + length]
    conv_pre = conv_pre.reshape(row_count, inner_width)
    conv_out = silu(conv_pre).astype(jnp.bfloat16)
    projected = jnp.dot(conv_out, select_weight, preferred_element_type=jnp.float32)
    rank_part = projected[:, :rank_width].astype(jnp.bfloat16)
    in_gate = projected[:, rank_width : rank_width + state_width]
    out_gate = projected[:, rank_width + state_width :]
    rate_pre = jnp.dot(rank_part, rate_weight, preferred_element_type=jnp.float32) + rate_bias
    step_sizes = jax.nn.softplus(rate_pre)
    rates = -jnp.exp(decay_log).T
    gated_grad = times_transpose(out_flat, out_weight)
    gate_act = silu(gate_half)
    mixed_grad = gated_grad * gate_act
    local_end, sent_back, whole = summary(
        step_sizes, conv_out, mixed_grad, in_gate, out_gate, rates, seq_count, length
    )
    entering, leaving = exchange(whole, local_end, sent_back, rates)
    scanned, step_grad, input_grad, in_grad, out_grad, decay_grad = merged(
        step_sizes, conv_out, mixed_grad, in_gate, out_gate, rates, entering, leaving, seq_count, length
    )
    inputs = wide(conv_out)
    mixed_out = scanned + skip_gain * inputs
    gated = (mixed_out * gate_act).astype(jnp.bfloat16)
    block_out = (
        (flat_tokens + jnp.dot(gated, out_weight, preferred_element_type=jnp.float32))
        .astype(jnp.bfloat16)
        .reshape(tokens.shape)
    )
    out_weight_share = sum_shares(
        contract_rows(gated, out_flat).reshape(share_count, -1, model_width)
    )
    gate_grad = (gated_grad * mixed_out * silu_slope(gate_half)).astype(jnp.bfloat16)
    gate_share = sum_shares(contract_rows(normed, gate_grad).reshape(share_count, -1, inner_width))
    skip_grad = jnp.sum(mixed_grad * inputs, axis=0)
    rate_grad = step_grad * jax.nn.sigmoid(rate_pre)
    rate_bias_grad = jnp.sum(rate_grad, axis=0)
    rate_low = rate_grad.astype(jnp.bfloat16)
    rate_weight_grad = contract_rows(rank_part, rate_low)
    rank_grad = times_transpose(rate_low, rate_weight)
    projected_grad = jnp.concatenate([rank_grad, in_grad, out_grad], axis=1).astype(jnp.bfloat16)
    select_grad = contract_rows(projected_grad, conv_out)
    conv_grad = input_grad + skip_gain * mixed_grad + times_transpose(projected_grad, select_weight)
    pre_grad = (conv_grad * silu_slope(conv_pre)).reshape(seq_count, length, inner_width)
    conv_bias_grad = jnp.sum(pre_grad, axis=(0, 1))
    conv_weight_grad = jnp.stack(
        [jnp.sum(pre_grad * padded[:, k : k + length], axis=(0, 1)) for k in range(taps)]
    )
    heads = jnp.pad(pre_grad[:, : taps - 1], ((0, 0), (taps - 1, 0), (0, 0)))
    returned = sum(conv_weight[k] * heads[:, taps - 1 - k : 2 * (taps - 1) - k] for k in range(taps))
    returned = wide(passed_along(returned.astype(jnp.bfloat16), "seq", -1))
    tailed = jnp.pad(pre_grad, ((0, 0), (0, taps - 1), (0, 0)))
    inner_grad = sum(
        conv_weight[k] * tailed[:, taps - 1 - k : taps - 1 - k + length] for k in range(taps)
    )
    inner_grad = inner_grad.at[:, length - taps + 1 :].add(returned)
    inner_grad = inner_grad.reshape(row_count, inner_width).astype(jnp.bfloat16)
    inner_share = sum_shares(contract_rows(normed, inner_grad).reshape(share_count, -1, inner_width))
    normed_grad = times_transpose(inner_grad, in_weight[:, :inner_width]) + times_transpose(
        gate_grad, in_weight[:, inner_width:]
    )
    gain_grad = jnp.sum(normed_grad * flat_tokens * scale, axis=0)
    lifted = normed_grad * norm_gain
    dots = jnp.mean(lifted * flat_tokens, axis=1, keepdims=True)
    tokens_grad = (
        (wide(out_flat) + scale * lifted - flat_tokens * (scale * scale * scale) * dots)
        .astype(jnp.bfloat16)
        .reshape(tokens.shape)
    )
    gain_rows = model_width // share_count
    part_width = inner_width // share_count
    gain_row = jnp.pad(
        gain_grad.reshape(share_count, gain_rows), ((0, 0), (0, part_width - gain_rows))
    ).reshape(1, inner_width)
    small = jnp.concatenate(
        [
            select_grad,
            rate_weight_grad,
            decay_grad,
            conv_weight_grad,
            conv_bias_grad[None],
            rate_bias_grad[None],
            skip_grad[None],
            gain_row,
        ],
        axis=0,
    )
    small = small.reshape(small.shape[0], share_count, part_width).transpose(1, 0, 2)
    small = sum_shares(small)
    at = 0
    taken = []
    for size in (select_weight.shape[1], rank_width, state_width, taps, 1, 1, 1, 1):
        taken.append(small[at : at + size])
        at += size
    return (
        block_out,
        tokens_grad,
        taken[7][0, :gain_rows],
        jnp.concatenate([inner_share, gate_share], axis=1),
        taken[3],
        taken[4][0],
        taken[0].T,
        taken[1],
        taken[5][0],
        taken[2].T,
        taken[6][0],
        out_weight_share,
    )


def solution(mesh):
    sharded = P("grp", "seq", None)
    shares = ("seq", "grp")
    return jax.shard_map(
        shards,
        mesh=mesh,
        in_specs=(sharded, sharded) + (P(),) * 10,
        out_specs=(
            sharded,
            sharded,
            P(shares),
            P(shares, None),
            P(None, shares),
            P(shares),
            P(shares, None),
            P(None, shares),
            P(shares),
            P(shares, None),
            P(shares),
            P(shares, None),
        ),
        check_vma=False,
    )
```

```python
import functools
import math

import jax
import jax.numpy as jnp
from jax import lax
from jax.experimental import pallas as pl
from jax.experimental.pallas import tpu as pltpu
from jax.sharding import PartitionSpec as P

f32 = jnp.float32
bf16 = jnp.bfloat16
LOG2E = 1.4426950408889634
N = 16
T = 16
WIDTH = 512
NL = WIDTH // 128
VMEM = 60 * 2**20


def lane(l):
    return slice(l * 128, (l + 1) * 128)


def sigmoid(v):
    return 1.0 / (1.0 + jnp.exp(-v))


def joined(ref, rows):
    return jnp.concatenate([ref[l, rows, :] for l in range(NL)], axis=1)


def steps_of(rows):
    return pl.ds(pl.multiple_of(rows, T), T)


def state_of(t):
    return pl.ds(pl.multiple_of(t * N, N), N)


def rows_dot(left, right):
    return lax.dot_general(left, right, (((1,), (1,)), ((), ())), preferred_element_type=f32)


def state_end_kernel(proj_ref, rw_ref, rb_ref, x_ref, a2_ref, bb_ref, he_ref, w_ref, dl_ref, u_ref, *, nseq, length):
    rows = nseq * length

    def steps(i, _):
        r = pl.multiple_of(i * 64, 64)
        at = pl.ds(r, 64)
        low = proj_ref[at, : rw_ref.shape[0]].astype(bf16)
        pre = jnp.dot(low, rw_ref[...], preferred_element_type=f32) + rb_ref[...]
        d = jnp.maximum(pre, 0.0) + jnp.log(1.0 + jnp.exp(-jnp.abs(pre)))
        for l in range(NL):
            dl_ref[l, at, :] = d[:, lane(l)]
            u_ref[l, at, :] = d[:, lane(l)] * x_ref[l, at, :].astype(f32)
        return 0

    lax.fori_loop(0, rows // 64, steps, 0)
    for s in range(nseq):
        for l in range(NL):
            w_ref[s : s + 1, lane(l)] = jnp.sum(dl_ref[l, s * length : (s + 1) * length, :], axis=0, keepdims=True)

    def step(c, h):
        h = [list(v) for v in h]
        for k in range(T):
            for s in range(nseq):
                t = s * length + c * T + k
                bt = bb_ref[t]
                for l in range(NL):
                    f = jnp.exp2(dl_ref[l, pl.ds(t, 1), :] * a2_ref[:, lane(l)])
                    h[s][l] = f * h[s][l] + u_ref[l, pl.ds(t, 1), :] * bt
        return tuple(tuple(v) for v in h)

    z = jnp.zeros((N, 128), f32)
    h = lax.fori_loop(0, length // T, step, ((z,) * NL,) * nseq)
    for s in range(nseq):
        for l in range(NL):
            he_ref[s, :, lane(l)] = h[s][l]


def adjoint_end_kernel(dl_ref, g_ref, a2_ref, cb_ref, sb_ref, *, nseq, length):
    nch = length // T

    def step(m, lam):
        lam = [list(v) for v in lam]
        c = nch - 1 - m
        for k in reversed(range(T)):
            for s in range(nseq):
                t = s * length + c * T + k
                ct = cb_ref[t]
                for l in range(NL):
                    f = jnp.exp2(dl_ref[l, pl.ds(t, 1), :] * a2_ref[:, lane(l)])
                    lam[s][l] = f * (lam[s][l] + g_ref[l, pl.ds(t, 1), :] * ct)
        return tuple(tuple(v) for v in lam)

    z = jnp.zeros((N, 128), f32)
    lam = lax.fori_loop(0, nch, step, ((z,) * NL,) * nseq)
    for s in range(nseq):
        for l in range(NL):
            sb_ref[s, :, lane(l)] = lam[s][l]


def forward_kernel(
    dl_ref, u_ref, g_ref, ga_ref, gs_ref, x_ref, skip_ref, bb_ref, lc_ref, a2_ref, hin_ref,
    hb_ref, gated_ref, ggr_ref, outg_ref, sk_ref, *, nseq, length, unroll,
):
    nch = length // T
    skip = skip_ref[...]
    ones = jnp.ones((8, 128), bf16)

    @pl.when(pl.program_id(0) == 0)
    def _():
        outg_ref[...] = jnp.zeros_like(outg_ref)

    def chunk(c, h, acc):
        hbv, pov = {}, [[None] * T for _ in range(nseq)]
        for k in range(T):
            for s in range(nseq):
                t = s * length + c * T + k
                bt = bb_ref[t]
                po = None
                for l in range(NL):
                    g = jnp.broadcast_to(g_ref[l, pl.ds(t, 1), :], (N, 128)).astype(bf16)
                    f = jnp.exp2(dl_ref[l, pl.ds(t, 1), :] * a2_ref[:, lane(l)])
                    h[s][l] = f * h[s][l] + u_ref[l, pl.ds(t, 1), :] * bt
                    hb = h[s][l].astype(bf16)
                    hb_ref[state_of(t), lane(l)] = hb
                    hbv[k, s, l] = hb
                    po = hb * g if po is None else po + hb * g
                pov[s][k] = po
        lhs = jnp.concatenate([lc_ref[steps_of(s * length + c * T), :] for s in range(nseq)], axis=0)
        parts = []
        for l in range(0, NL, 2):
            rhs = jnp.concatenate(
                [
                    jnp.concatenate([hbv[k, s, l], hbv[k, s, l + 1]], axis=1)
                    for k in range(T) for s in range(nseq)
                ],
                axis=0,
            )
            parts.append(jnp.dot(lhs, rhs, preferred_element_type=f32))
        sc_all = jnp.concatenate(parts, axis=1)
        for s in range(nseq):
            og = rows_dot(ones, jnp.concatenate(pov[s], axis=0))
            outg_ref[pl.ds(s * nch + c, 1), :] += og[:1]
            at = steps_of(s * length + c * T)
            x = joined(x_ref, at).astype(f32)
            mo = sc_all[s * T : (s + 1) * T] + skip * x
            gated_ref[at, :] = (mo * joined(ga_ref, at)).astype(bf16)
            ggr_ref[at, :] = (mo * joined(gs_ref, at)).astype(bf16)
            acc = acc + joined(g_ref, at) * x
        return acc

    def step(i, carry):
        h, acc = carry
        h = [list(v) for v in h]
        for p in range(unroll):
            acc = chunk(i * unroll + p, h, acc)
        return tuple(tuple(v) for v in h), acc

    h0 = tuple(tuple(hin_ref[s, :, lane(l)] for l in range(NL)) for s in range(nseq))
    _, acc = lax.fori_loop(0, nch // unroll, step, (h0, jnp.zeros((T, WIDTH), f32)))
    sk_ref[...] = jnp.broadcast_to(jnp.sum(acc, axis=0, keepdims=True), sk_ref.shape)


def backward_kernel(
    dl_ref, u_ref, g_ref, x_ref, skip_ref, cb_ref, lb_ref, ls_ref, a_ref, a2_ref, lin_ref, hin_ref, hb_ref,
    rl_ref, cp_ref, ing_ref, dlog_ref, rb_ref, *, nseq, length, unroll,
):
    nch = length // T
    abf = a_ref[...].astype(bf16)
    skip = skip_ref[...]
    ones = jnp.ones((8, 128), bf16)

    @pl.when(pl.program_id(0) == 0)
    def _():
        ing_ref[...] = jnp.zeros_like(ing_ref)

    def chunk(c, lam, dlog, rb):
        pov = [[None] * T for _ in range(nseq)]
        dacc = [None] * NL
        vals = {}
        for k in reversed(range(T)):
            for s in range(nseq):
                t = s * length + c * T + k
                ct = cb_ref[t]
                po = None
                for l in range(NL):
                    d = jnp.broadcast_to(dl_ref[l, pl.ds(t, 1), :], (N, 128))
                    u = jnp.broadcast_to(u_ref[l, pl.ds(t, 1), :], (N, 128)).astype(bf16)
                    a = g_ref[l, pl.ds(t, 1), :] * ct + lam[s][l]
                    lam[s][l] = jnp.exp2(d * a2_ref[:, lane(l)]) * a
                    if k > 0:
                        hp = hb_ref[state_of(t - 1), lane(l)]
                    else:
                        hp = hb_ref[state_of(jnp.maximum(t - 1, 0)), lane(l)]
                        hp = jnp.where(c == 0, hin_ref[s, :, lane(l)].astype(bf16), hp)
                    q = lam[s][l].astype(bf16) * hp * abf[:, lane(l)]
                    ab = a.astype(bf16)
                    qd = q * d.astype(bf16)
                    vals[k, s, l] = (ab, q)
                    dacc[l] = qd if dacc[l] is None else dacc[l] + qd
                    po = ab * u if po is None else po + ab * u
                pov[s][k] = po
            if k % 8 == 0:
                for l in range(NL):
                    dlog[l] = dlog[l] + dacc[l].astype(f32)
                    dacc[l] = None
        lhs = jnp.concatenate(
            [lb_ref[steps_of(s * length + c * T), :] for s in range(nseq)] + [ls_ref[...]], axis=0
        )
        parts = []
        for l in range(0, NL, 2):
            rhs = jnp.concatenate(
                [
                    jnp.concatenate([vals[k, s, l][y], vals[k, s, l + 1][y]], axis=1)
                    for k in reversed(range(T)) for s in range(nseq) for y in range(2)
                ],
                axis=0,
            )
            parts.append(jnp.dot(lhs, rhs, preferred_element_type=f32))
        both = jnp.concatenate(parts, axis=1)
        for s in range(nseq):
            w = both[s * T : (s + 1) * T]
            qs = both[(nseq + s) * T : (nseq + s + 1) * T]
            ig = rows_dot(ones, jnp.concatenate(pov[s], axis=0))
            ing_ref[pl.ds(s * nch + c, 1), :] += ig[:1]
            at = steps_of(s * length + c * T)
            d = joined(dl_ref, at)
            rg = (qs + w * joined(x_ref, at).astype(f32)) * (1.0 - jnp.exp(-d))
            rb = rb + rg
            rl_ref[at, :] = rg.astype(bf16)
            cp_ref[at, :] = w * d + skip * joined(g_ref, at)
        return rb

    def step(m, carry):
        lam, dlog, rb = carry
        lam = [list(v) for v in lam]
        dlog = list(dlog)
        for p in range(unroll):
            rb = chunk(nch - 1 - (m * unroll + p), lam, dlog, rb)
        return tuple(tuple(v) for v in lam), tuple(dlog), rb

    l0 = tuple(tuple(lin_ref[s, :, lane(l)] for l in range(NL)) for s in range(nseq))
    z = jnp.zeros((N, 128), f32)
    _, dlog, rb = lax.fori_loop(0, nch // unroll, step, (l0, (z,) * NL, jnp.zeros((T, WIDTH), f32)))
    for l in range(NL):
        dlog_ref[:, lane(l)] = dlog[l]
    rb_ref[...] = jnp.broadcast_to(jnp.sum(rb, axis=0, keepdims=True), rb_ref.shape)


def block_of(rows):
    return pl.BlockSpec((rows, WIDTH), lambda j: (0, j))


def tiles_of(rows):
    return pl.BlockSpec((NL, rows, 128), lambda j: (j, 0, 0))


def states_of(nseq):
    return pl.BlockSpec((nseq, N, WIDTH), lambda j: (0, 0, j))


def whole(a):
    return pl.BlockSpec(a.shape, lambda j: (0,) * a.ndim, pipeline_mode=pl.Buffered(1))


def kernel_call(body, name, channels, operands, specs, out_specs, outs, flops, scratch=(), **options):
    moved = sum(a.size * a.dtype.itemsize for a in operands) + sum(
        math.prod(o.shape) * o.dtype.itemsize for o in outs
    )
    return pl.pallas_call(
        functools.partial(body, **options),
        grid=(channels // WIDTH,),
        in_specs=specs,
        out_specs=out_specs,
        out_shape=outs,
        scratch_shapes=scratch,
        compiler_params=pltpu.CompilerParams(vmem_limit_bytes=VMEM, dimension_semantics=("arbitrary",)),
        cost_estimate=pl.CostEstimate(flops=flops, bytes_accessed=moved, transcendentals=0),
        name=name,
    )(*operands)


def spread(values, nseq, length, kinds, reverse):
    rows = nseq * length
    width = T * nseq * kinds * N
    column = jnp.arange(width)
    pick = (column[None, :] % N == jnp.arange(N)[:, None]).astype(bf16)
    wide = jnp.dot(values.astype(bf16), pick, preferred_element_type=f32)
    return jnp.where(own_column(rows, length, width, nseq, kinds, 0, reverse), wide, 0.0).astype(bf16)


def own_column(rows, length, width, nseq, kinds, kind, reverse):
    row = lax.broadcasted_iota(jnp.int32, (rows, width), 0)
    column = lax.broadcasted_iota(jnp.int32, (rows, width), 1)
    step = column // (nseq * kinds * N)
    if reverse:
        step = T - 1 - step
    return (
        (step == row % T)
        & ((column // (kinds * N)) % nseq == row // length)
        & ((column // N) % kinds == kind)
    )


def state_end(proj, rate_weight, rate_bias, x, a2, bb, nseq, length):
    tiles, rows, _ = x.shape
    ch = tiles * 128
    o = jax.ShapeDtypeStruct
    return kernel_call(
        state_end_kernel, "state_end", ch,
        (proj, rate_weight, rate_bias, x, a2, bb),
        [whole(proj), block_of(rate_weight.shape[0]), block_of(1), tiles_of(rows), block_of(N), whole(bb)],
        [states_of(nseq), block_of(nseq), tiles_of(rows), tiles_of(rows)],
        (o((nseq, N, ch), f32), o((nseq, ch), f32), o(x.shape, f32), o(x.shape, f32)),
        2 * 10**10, nseq=nseq, length=length,
    )


def adjoint_end(dl, g, a2, cb, nseq, length):
    tiles, rows, _ = dl.shape
    ch = tiles * 128
    return kernel_call(
        adjoint_end_kernel, "adjoint_end", ch,
        (dl, g, a2, cb),
        [tiles_of(rows), tiles_of(rows), block_of(N), whole(cb)],
        [states_of(nseq)],
        (jax.ShapeDtypeStruct((nseq, N, ch), f32),),
        2 * 10**10, nseq=nseq, length=length,
    )[0]


def forward(dl, u, g, ga, gs, x, skip, bb, lc, a2, hin, nseq, length, unroll=1):
    tiles, rows, _ = dl.shape
    ch = tiles * 128
    o = jax.ShapeDtypeStruct
    t = tiles_of(rows)
    return kernel_call(
        forward_kernel, "forward", ch,
        (dl, u, g, ga, gs, x, skip, bb, lc, a2, hin),
        [t, t, t, t, t, t, block_of(1), whole(bb), whole(lc), block_of(N), states_of(nseq)],
        [block_of(rows * N), block_of(rows), block_of(rows), pl.BlockSpec((rows // T, T * N), lambda j: (0, 0)), block_of(8)],
        (o((rows * N, ch), bf16), o((rows, ch), bf16), o((rows, ch), bf16), o((rows // T, T * N), f32), o((8, ch), f32)),
        3 * 10**10, nseq=nseq, length=length, unroll=unroll,
    )


def backward(dl, u, g, x, skip, cb, lb, ls, a, a2, lin, hin, hb, nseq, length, unroll=1):
    tiles, rows, _ = dl.shape
    ch = tiles * 128
    o = jax.ShapeDtypeStruct
    t = tiles_of(rows)
    st = states_of(nseq)
    return kernel_call(
        backward_kernel, "backward", ch,
        (dl, u, g, x, skip, cb, lb, ls, a, a2, lin, hin, hb),
        [t, t, t, t, block_of(1), whole(cb), whole(lb), whole(ls), block_of(N), block_of(N), st, st, block_of(rows * N)],
        [block_of(rows), block_of(rows), pl.BlockSpec((rows // T, T * N), lambda j: (0, 0)), block_of(N), block_of(8)],
        (o((rows, ch), bf16), o((rows, ch), f32), o((rows // T, T * N), f32), o((N, ch), f32), o((8, ch), f32)),
        5 * 10**10, nseq=nseq, length=length, unroll=unroll,
    )


epsilon = 1e-05
ROWS = 64
PAD = 8


def normalized(tokens, gain):
    wide = tokens.astype(f32)
    return (wide * lax.rsqrt(jnp.mean(wide * wide, axis=1, keepdims=True) + epsilon) * gain).astype(bf16)


def gate_kernel(tok_ref, gain_ref, cot_ref, wg_ref, ow_ref, normed_ref, turned_ref, g_ref, ga_ref, gs_ref, gh_ref, gg_ref):
    rows = tok_ref.shape[0]

    @pl.when(pl.program_id(0) == 0)
    def _():
        def norm(i, _):
            at = pl.ds(pl.multiple_of(i * ROWS, ROWS), ROWS)
            normed_ref[at, :] = normalized(tok_ref[at, :], gain_ref[...])
            return 0

        lax.fori_loop(0, rows // ROWS, norm, 0)
        turned_ref[...] = normed_ref[...].T

    gh_ref[...] = jnp.dot(normed_ref[...], wg_ref[...], preferred_element_type=f32)
    gg_ref[...] = rows_dot(cot_ref[...], ow_ref[...])

    def mix(i, _):
        at = pl.ds(pl.multiple_of(i * ROWS, ROWS), ROWS)
        gh = gh_ref[at, :]
        gg = gg_ref[at, :]
        sg = sigmoid(gh)
        ga = gh * sg
        gs = gg * (sg * (1.0 + gh * (1.0 - sg)))
        g = gg * ga
        for l in range(NL):
            g_ref[l, at, :] = g[:, lane(l)]
            ga_ref[l, at, :] = ga[:, lane(l)]
            gs_ref[l, at, :] = gs[:, lane(l)]
        return 0

    lax.fori_loop(0, rows // ROWS, mix, 0)


def gate_side(tokens, gain, cotangent, in_weight, out_weight):
    rows, model = tokens.shape
    inner = out_weight.shape[0]
    first = inner // WIDTH
    tiles = jax.ShapeDtypeStruct((inner // 128, rows, 128), f32)
    return kernel_call(
        gate_kernel, "gate_side", inner,
        (tokens, gain, cotangent, in_weight, out_weight),
        [
            whole(tokens), whole(gain), whole(cotangent),
            pl.BlockSpec((model, WIDTH), lambda j: (0, j + first)),
            pl.BlockSpec((WIDTH, model), lambda j: (j, 0)),
        ],
        [pl.BlockSpec((rows, model), lambda j: (0, 0)), pl.BlockSpec((model, rows), lambda j: (0, 0))]
        + [tiles_of(rows)] * 3,
        (jax.ShapeDtypeStruct((rows, model), bf16), jax.ShapeDtypeStruct((model, rows), bf16), tiles, tiles, tiles),
        4 * rows * model * inner, scratch=[pltpu.VMEM((rows, WIDTH), f32)] * 2,
    )


def taps_of(ext, weight, first, rows):
    taps = weight.shape[0]
    return sum(weight[k : k + 1] * ext[first + k : first + k + rows] for k in range(taps))


def inner_kernel(
    normed_ref, halo_ref, gain_ref, wi_ref, cw_ref, cb_ref, sw_ref, inner_ref, before_ref, x_ref, proj_ref, ext_ref, flat_ref,
    *, nseq, length,
):
    part = jnp.dot(normed_ref[...], wi_ref[...], preferred_element_type=f32).astype(bf16)
    inner_ref[...] = part
    for s in range(nseq):
        ext_ref[s, PAD:, :] = part[s * length : (s + 1) * length].astype(f32)
    before = jnp.dot(
        normalized(halo_ref[...], gain_ref[...]), wi_ref[...], preferred_element_type=f32
    ).astype(bf16)
    before_ref[...] = before
    for s in range(nseq):
        ext_ref[s, :PAD, :] = before[s * PAD : (s + 1) * PAD].astype(f32)

    @pl.when(pl.program_id(0) == 0)
    def _():
        proj_ref[...] = jnp.zeros_like(proj_ref)

    taps = cw_ref.shape[0]
    for s in range(nseq):

        def mix(i, _):
            r = pl.multiple_of(i * ROWS, ROWS)
            at = pl.ds(pl.multiple_of(s * length + r, ROWS), ROWS)
            ext = ext_ref[s, pl.ds(r, ROWS + PAD), :]
            pre = taps_of(ext, cw_ref[...], PAD - taps + 1, ROWS) + cb_ref[...]
            x = (pre * sigmoid(pre)).astype(bf16)
            for l in range(NL):
                x_ref[l, at, :] = x[:, lane(l)]
            flat_ref[at, :] = x
            return 0

        lax.fori_loop(0, length // ROWS, mix, 0)
    proj_ref[...] += jnp.dot(flat_ref[...], sw_ref[...], preferred_element_type=f32)


def inner_side(normed, halo, gain, in_weight, conv_weight, conv_bias, select_weight, nseq, length):
    rows, model = normed.shape
    inner, picks = select_weight.shape
    o = jax.ShapeDtypeStruct
    operands = (normed, halo, gain, in_weight, conv_weight, conv_bias, select_weight)
    specs = [
        whole(normed), whole(halo), whole(gain), block_of(model), block_of(conv_weight.shape[0]), block_of(1),
        pl.BlockSpec((WIDTH, picks), lambda j: (j, 0)),
    ]
    return pl.pallas_call(
        functools.partial(inner_kernel, nseq=nseq, length=length),
        grid=(inner // WIDTH,),
        in_specs=specs,
        out_specs=[block_of(rows), block_of(halo.shape[0]), tiles_of(rows), pl.BlockSpec((rows, picks), lambda j: (0, 0))],
        out_shape=(
            o((rows, inner), bf16), o((halo.shape[0], inner), bf16), o((inner // 128, rows, 128), bf16), o((rows, picks), f32),
        ),
        scratch_shapes=[pltpu.VMEM((nseq, PAD + length, WIDTH), f32), pltpu.VMEM((rows, WIDTH), bf16)],
        compiler_params=pltpu.CompilerParams(vmem_limit_bytes=VMEM, dimension_semantics=("arbitrary",)),
        cost_estimate=pl.CostEstimate(flops=2 * rows * model * inner, bytes_accessed=14 * 2**20, transcendentals=0),
        name="inner_side",
    )(*operands)


def input_grad_kernel(
    place_ref, cp_ref, inner_ref, before_ref, x_ref, pg_ref, sw_ref, cw_ref, cb_ref, turned_ref, halo_ref, gain_ref,
    rl_ref, rank_ref, dlog_ref, rb_ref, sk_ref,
    packed_ref, igr_ref, tail_ref, head_ref, ext_ref, pre_ref, back_ref, vec_ref, *, nseq, length, part,
):
    taps = cw_ref.shape[0]
    j = pl.program_id(0)
    back_ref[...] = cp_ref[...] + rows_dot(pg_ref[...], sw_ref[...])
    vec_ref[...] = jnp.zeros_like(vec_ref)
    for s in range(nseq):
        ext_ref[s, :PAD, :] = before_ref[s * PAD : (s + 1) * PAD, :].astype(f32)
        pre_ref[s, :PAD, :] = jnp.zeros((PAD, WIDTH), f32)
        pre_ref[s, PAD + length :, :] = jnp.zeros((PAD, WIDTH), f32)

        def first(i, _):
            r = pl.multiple_of(i * ROWS, ROWS)
            at = pl.ds(pl.multiple_of(s * length + r, ROWS), ROWS)
            after = pl.ds(pl.multiple_of(r + PAD, PAD), ROWS)
            ext_ref[s, after, :] = inner_ref[at, :].astype(f32)
            ext = ext_ref[s, pl.ds(r, ROWS + PAD), :]
            pre = taps_of(ext, cw_ref[...], PAD - taps + 1, ROWS) + cb_ref[...]
            sg = sigmoid(pre)
            back = back_ref[at, :] * (sg * (1.0 + pre * (1.0 - sg)))
            pre_ref[s, after, :] = back
            for k in range(taps):
                at_k = PAD - taps + 1 + k
                vec_ref[k : k + 1, :] += jnp.sum(back * ext[at_k : at_k + ROWS], axis=0, keepdims=True)
            vec_ref[taps : taps + 1, :] += jnp.sum(back, axis=0, keepdims=True)
            return 0

        lax.fori_loop(0, length // ROWS, first, 0)

        def back_rows(ext, rows):
            return sum(cw_ref[k : k + 1, :] * ext[taps - 1 - k : taps - 1 - k + rows] for k in range(taps))

        def second(i, _):
            r = pl.multiple_of(i * ROWS, ROWS)
            at = pl.ds(pl.multiple_of(s * length + r, ROWS), ROWS)
            ext = pre_ref[s, pl.ds(pl.multiple_of(r + PAD, PAD), ROWS + PAD), :]
            igr_ref[at, :] = back_rows(ext, ROWS).astype(bf16)
            return 0

        lax.fori_loop(0, length // ROWS, second, 0)
        tail_ref[s * PAD : (s + 1) * PAD, :] = back_rows(pre_ref[s, length :, :], PAD)
        lead = pre_ref[s, : 2 * PAD, :]
        kept = lax.broadcasted_iota(jnp.int32, (PAD, WIDTH), 0) < taps - 1
        head = sum(cw_ref[k : k + 1, :] * lead[PAD - k : 2 * PAD - k] for k in range(taps))
        head_ref[s * PAD : (s + 1) * PAD, :] = jnp.where(kept, head, 0.0)

    vec_ref[taps + 1 : taps + 2, :] = rb_ref[0:1, :]
    vec_ref[taps + 2 : taps + 3, :] = sk_ref[0:1, :]
    vec_ref[8:, :] = dlog_ref[...]
    count = place_ref.shape[0]
    wide = packed_ref.shape[2]
    rows_each = turned_ref.shape[0] // count
    rows_pad = padded(rows_each)
    before_normed = normalized(halo_ref[...], gain_ref[...])
    for b in range(WIDTH // wide):
        cols = slice(b * wide, (b + 1) * wide)
        shifted = jnp.concatenate(
            [
                jnp.concatenate(
                    [jnp.zeros((PAD - taps + 1, wide), f32), head_ref[s * PAD : s * PAD + taps - 1, cols]], axis=0
                )
                for s in range(nseq)
            ],
            axis=0,
        )
        product = jnp.dot(turned_ref[...], igr_ref[:, cols], preferred_element_type=f32) + contract_rows(
            before_normed, shifted.astype(bf16)
        )
        at = pl.ds(pl.multiple_of((j * (WIDTH // wide) + b) * rows_pad, rows_pad), rows_pad)
        for q in range(count):
            packed_ref[place_ref[q], at, :] = share_rows(product, q, rows_each)
    eye = (
        lax.broadcasted_iota(jnp.int32, (vec_ref.shape[0], wide), 0) + 160
        == lax.broadcasted_iota(jnp.int32, (vec_ref.shape[0], wide), 1)
    ).astype(bf16)
    small = (
        contract_rows(joined(x_ref, slice(None)), pg_ref[...])
        + contract_rows(rl_ref[...], rank_ref[...])
        + contract_rows(vec_ref[...].astype(bf16), eye)
    )
    base = packed_ref.shape[1] - padded(part)
    for q in range(WIDTH // part):
        packed_ref[place_ref[j * (WIDTH // part) + q], base : base + padded(part), :] = share_rows(small, q, part)


def padded(rows):
    return max(rows, 16)


def share_rows(values, share, rows):
    taken = values[share * rows : (share + 1) * rows]
    if rows < padded(rows):
        taken = jnp.concatenate([taken, jnp.zeros((padded(rows) - rows, values.shape[1]), values.dtype)], axis=0)
    return taken.astype(bf16)


def weight_grad_kernel(place_ref, gated_ref, gate_ref, cot_ref, turned_ref, packed_ref, *, part):
    j = pl.program_id(0)
    count = place_ref.shape[0]
    model = cot_ref.shape[1]
    rows_each = model // count
    rows_pad = padded(rows_each)
    product = contract_rows(gated_ref[...], cot_ref[...])
    for q in range(WIDTH // part):
        packed_ref[place_ref[j * (WIDTH // part) + q], : padded(part), :] = share_rows(product, q, part)
    product = jnp.dot(turned_ref[...], gate_ref[...], preferred_element_type=f32)
    each = model // WIDTH
    at = pl.ds(pl.multiple_of(padded(part) + (j // each) * rows_pad, 16), rows_pad)
    cols = pl.ds(pl.multiple_of((j % each) * WIDTH, WIDTH), WIDTH)
    for q in range(count):
        packed_ref[place_ref[q], at, cols] = share_rows(product, q, rows_each)


def weight_grads(place, gated, gate_grad, cot, turned, part):
    rows, width = gated.shape
    model = cot.shape[1]
    count = place.shape[0]
    packed_rows = padded(part) + (width // model) * padded(model // count)
    col = pl.BlockSpec((rows, WIDTH), lambda j, _: (0, j))
    fixed = lambda a: pl.BlockSpec(a.shape, lambda j, _: (0,) * a.ndim, pipeline_mode=pl.Buffered(1))
    return pl.pallas_call(
        functools.partial(weight_grad_kernel, part=part),
        grid_spec=pltpu.PrefetchScalarGridSpec(
            num_scalar_prefetch=1,
            grid=(width // WIDTH,),
            in_specs=[col, col, fixed(cot), fixed(turned)],
            out_specs=pl.BlockSpec((count, packed_rows, model), lambda j, _: (0, 0, 0)),
        ),
        out_shape=jax.ShapeDtypeStruct((count, packed_rows, model), bf16),
        compiler_params=pltpu.CompilerParams(vmem_limit_bytes=VMEM, dimension_semantics=("arbitrary",)),
        cost_estimate=pl.CostEstimate(flops=4 * rows * width * model, bytes_accessed=14 * 2**20, transcendentals=0),
        name="weight_grads",
    )(place, gated, gate_grad, cot, turned)


def input_grads(
    place, cp, inner, before, x, pg, select_weight, conv_weight, conv_bias, turned, halo, gain, rate_low, rank_part,
    decay_grad, rate_bias_grad, skip_grad, nseq, length, part,
):
    rows, width = cp.shape
    wide = pg.shape[1]
    count = place.shape[0]
    model = turned.shape[0]
    packed_rows = (width // wide) * padded(model // count) + padded(part)
    o = jax.ShapeDtypeStruct

    def drop(spec):
        return pl.BlockSpec(spec.block_shape, lambda j, _, f=spec.index_map: f(j), pipeline_mode=spec.pipeline_mode)

    specs = [
        block_of(rows), block_of(rows), block_of(before.shape[0]), tiles_of(rows), whole(pg),
        pl.BlockSpec((WIDTH, wide), lambda j: (j, 0)), block_of(conv_weight.shape[0]), block_of(1), whole(turned),
        whole(halo), whole(gain), block_of(rows), whole(rank_part), block_of(N), block_of(8), block_of(8),
    ]
    out_specs = [
        pl.BlockSpec((count, packed_rows, wide), lambda j: (0, 0, 0)), block_of(rows), block_of(nseq * PAD),
        block_of(nseq * PAD),
    ]
    return pl.pallas_call(
        functools.partial(input_grad_kernel, nseq=nseq, length=length, part=part),
        grid_spec=pltpu.PrefetchScalarGridSpec(
            num_scalar_prefetch=1,
            grid=(width // WIDTH,),
            in_specs=[drop(s) for s in specs],
            out_specs=[drop(s) for s in out_specs],
            scratch_shapes=[
                pltpu.VMEM((nseq, PAD + length, WIDTH), f32), pltpu.VMEM((nseq, PAD + length + PAD, WIDTH), f32),
                pltpu.VMEM((rows, WIDTH), f32), pltpu.VMEM((8 + N, WIDTH), f32),
            ],
        ),
        out_shape=(
            o((count, packed_rows, wide), bf16), o((rows, width), bf16), o((nseq * PAD, width), f32),
            o((nseq * PAD, width), f32),
        ),
        compiler_params=pltpu.CompilerParams(vmem_limit_bytes=VMEM, dimension_semantics=("arbitrary",)),
        cost_estimate=pl.CostEstimate(flops=4 * rows * width * model, bytes_accessed=24 * 2**20, transcendentals=0),
        name="input_grads",
    )(
        place, cp, inner, before, x, pg, select_weight, conv_weight, conv_bias, turned, halo, gain, rate_low,
        rank_part, decay_grad, rate_bias_grad, skip_grad,
    )


def flip_bit(axis, bit):
    return [(i, i ^ bit) for i in range(lax.axis_size(axis))]


def bits_of(axis):
    size = lax.axis_size(axis)
    return [(axis, 1 << k) for k in range(size.bit_length() - 1)]


def places(order):
    grp = lax.axis_size("grp")
    other = jnp.arange(lax.axis_size("seq") * grp) ^ (lax.axis_index("seq") * grp + lax.axis_index("grp"))
    position = jnp.zeros_like(other)
    for axis, bit in order:
        position = 2 * position + (other // (bit * grp if axis == "seq" else bit)) % 2
    return position.astype(jnp.int32)


def pairs_of(bits):
    return [bits[i : i + 2] for i in range(0, len(bits), 2)]


def sum_packed(packed, order, rounds):
    held = packed
    for bits in rounds:
        count = 1 << len(bits)
        held = held.reshape((count, held.shape[0] // count) + held.shape[1:])
        total = held[0].astype(f32)
        for other in range(1, count):
            flip = sum(bit for i, (axis, bit) in enumerate(bits) if (other >> (len(bits) - 1 - i)) & 1)
            axis = bits[0][0]
            total = total + lax.ppermute(held[other].astype(bf16), axis, flip_bit(axis, flip)).astype(f32)
        held = total
    return held[0]


def ring_place(chips):
    ring = [i ^ (i >> 1) for i in range(chips)]
    return [ring.index(i) for i in range(chips)], ring


def half_places():
    grp, chips = lax.axis_size("grp"), lax.axis_size("seq") // 2
    place = jnp.array(ring_place(chips)[0], jnp.int32)
    share = jnp.arange(2 * chips * grp)
    seq = share // grp
    other = (seq % 2) ^ (lax.axis_index("seq") % 2)
    return ((other * chips + place[seq // 2]) * grp + share % grp).astype(jnp.int32)


def sum_offloaded(packed):
    half = packed.shape[0] // 2
    got = lax.ppermute(packed[half:], "seq", flip_bit("seq", 1))
    held = (packed[:half].astype(f32) + got.astype(f32)).astype(bf16)
    ring = ring_place(lax.axis_size("seq") // 2)[1]
    groups = [[2 * chip + core for chip in ring] for core in range(2)]
    held = lax.psum_scatter(held, "seq", scatter_dimension=0, axis_index_groups=groups, tiled=True)
    return lax.psum_scatter(held, "grp", scatter_dimension=0, tiled=True)[0].astype(f32)


def summary_block(span, summary):
    width = span.shape[-1]
    high = span.astype(bf16)
    low = (span - high.astype(f32)).astype(bf16)
    return jnp.concatenate([summary.astype(bf16).reshape(-1, width), high, low], axis=0)


def carried(block, shape, rates, backward, after=None):
    count, mine = lax.axis_size("seq"), lax.axis_index("seq")
    blocks = lax.all_gather(block, "seq")
    if after is not None:
        blocks, after = lax.optimization_barrier((blocks, after))
    rows = shape[0] * shape[1]
    entering = jnp.zeros(shape, f32)
    for turn in range(count - 1):
        j = count - 1 - turn if backward else turn
        theirs = blocks[j].astype(f32)
        span = theirs[rows : rows + shape[0]] + theirs[rows + shape[0] :]
        longer = jnp.exp(span[:, None, :] * rates) * entering + theirs[:rows].reshape(shape)
        entering = jnp.where(mine < j if backward else j < mine, longer, entering)
    return entering, after


def contract_rows(left, right, kind=f32):
    return lax.dot_general(left, right, (((0,), (0,)), ((), ())), preferred_element_type=f32).astype(kind)


def shards(
    tokens,
    cotangent,
    norm_gain,
    in_weight,
    conv_weight,
    conv_bias,
    select_weight,
    rate_weight,
    rate_bias,
    decay_log,
    skip_gain,
    out_weight,
):
    nseq, length, model = tokens.shape
    inner_width = out_weight.shape[0]
    rank = rate_weight.shape[0]
    taps = conv_weight.shape[0]
    rows = nseq * length
    share_count = lax.axis_size("seq") * lax.axis_size("grp")
    tok = tokens.reshape(rows, model)
    cot = cotangent.reshape(rows, model)
    gain, skip, bias = norm_gain[None], skip_gain[None], conv_bias[None]
    pieces, grp = lax.axis_size("seq"), lax.axis_size("grp")
    halo = lax.ppermute(tokens[:, length - PAD :], "seq", [(i, i + 1) for i in range(pieces - 1)])
    halo = halo.reshape(nseq * PAD, model)
    normed, turned, g, ga, gs = gate_side(tok, gain, cot, in_weight, out_weight)
    inner, before, x, proj = inner_side(
        normed, halo, gain, in_weight, conv_weight, bias, select_weight, nseq, length
    )
    in_gate, out_gate = proj[:, rank : rank + N], proj[:, rank + N :]
    rates = -jnp.exp(decay_log).T
    a2 = rates * LOG2E
    bb = jnp.broadcast_to(in_gate[:, :, None], (rows, N, 128))
    local_end, span, dl, u = state_end(proj, rate_weight, rate_bias[None], x, a2, bb, nseq, length)
    ahead = summary_block(span, local_end)
    ahead, g = lax.optimization_barrier((ahead, g))
    entering, _ = carried(ahead, local_end.shape, rates, False)
    cb = jnp.broadcast_to(out_gate[:, :, None], (rows, N, 128))
    sent_back = adjoint_end(dl, g, a2, cb, nseq, length)
    lc = spread(out_gate, nseq, length, 1, False)
    lb = spread(in_gate, nseq, length, 2, True)
    ls = own_column(nseq * T, T, T * nseq * 2 * N, nseq, 2, 1, True).astype(bf16)
    behind = summary_block(span, sent_back)
    behind, u = lax.optimization_barrier((behind, u))
    states, gated, gate_grad, out_grad, skip_grad = forward(
        dl, u, g, ga, gs, x, skip, bb, lc, a2, entering, nseq, length, 2
    )
    part, part_rows = inner_width // share_count, model // share_count
    weight_packed = weight_grads(half_places(), gated, gate_grad, cot, turned, part)
    leaving, weight_packed = carried(behind, sent_back.shape, rates, True, weight_packed)
    leaving, weight_packed = lax.optimization_barrier((leaving, weight_packed))
    weight_share = sum_offloaded(weight_packed)
    out_share = weight_share[:part]
    gate_share = weight_share[padded(part) :].reshape(-1, padded(part_rows), model)[:, :part_rows]
    gate_share = gate_share.transpose(1, 0, 2).reshape(part_rows, inner_width)
    rate_low, conv_part, in_grad, decay_grad, rate_bias_grad = backward(
        dl, u, g, x, skip, cb, lb, ls, rates, a2, leaving, entering, states, nseq, length, 2
    )
    rank_grad = rows_dot(rate_low, rate_weight)
    wide = 256
    picks = rank + 2 * N
    pg = jnp.concatenate(
        [
            rank_grad.astype(bf16),
            in_grad.reshape(rows, N).astype(bf16),
            out_grad.reshape(rows, N).astype(bf16),
            jnp.zeros((rows, wide - picks), bf16),
        ],
        axis=1,
    )
    rank_part = jnp.pad(proj[:, :rank].astype(bf16), ((0, 0), (picks, wide - picks - rank)))
    seq_bits, grp_bits = bits_of("seq"), bits_of("grp")
    order = seq_bits + grp_bits
    packed, inner_grad, tail, head = input_grads(
        places(order), conv_part, inner, before, x, pg, jnp.pad(select_weight, ((0, 0), (0, wide - picks))),
        conv_weight, bias, turned, halo, gain, rate_low, rank_part, decay_grad, rate_bias_grad, skip_grad,
        nseq, length, part,
    )
    rounds = [seq_bits[:1]] + pairs_of(seq_bits[1:]) + pairs_of(grp_bits)
    held = sum_packed(packed, order, rounds)
    blocks = inner_width // wide
    inner_share = held[: blocks * padded(part_rows)].reshape(blocks, padded(part_rows), wide)[:, :part_rows]
    inner_share = inner_share.transpose(1, 0, 2).reshape(part_rows, inner_width)
    small = held[blocks * padded(part_rows) :][:part]
    sent = head.reshape(nseq, PAD, inner_width)[:, : taps - 1].astype(bf16)
    returned = lax.ppermute(sent, "seq", [(i + 1, i) for i in range(pieces - 1)]).astype(f32)
    fixed = (tail.reshape(nseq, PAD, inner_width)[:, PAD - taps + 1 :] + returned).astype(bf16)
    inner_grad = (
        inner_grad.reshape(nseq, length, inner_width).at[:, length - taps + 1 :].set(fixed).reshape(rows, inner_width)
    )
    wide_tok = tok.astype(f32)
    scale = lax.rsqrt(jnp.mean(wide_tok * wide_tok, axis=1, keepdims=True) + epsilon)
    normed_grad = rows_dot(gate_grad, in_weight[:, inner_width:]) + rows_dot(inner_grad, in_weight[:, :inner_width])
    lifted = normed_grad * norm_gain
    dots = jnp.mean(lifted * wide_tok, axis=1, keepdims=True)
    tokens_grad = cot.astype(f32) + scale * lifted - wide_tok * (scale * scale * scale) * dots
    block_out = wide_tok + jnp.dot(gated, out_weight, preferred_element_type=f32)
    in_share = jnp.concatenate([inner_share, gate_share], axis=1)
    first = (lax.axis_index("seq") * grp + lax.axis_index("grp")) * part_rows
    own_weight = lax.dynamic_slice_in_dim(in_weight, first, part_rows, 0).astype(f32)
    own_gain = lax.dynamic_slice_in_dim(norm_gain, first, part_rows, 0)
    gain_share = jnp.sum(own_weight * in_share, axis=1) / own_gain
    vectors = small[:, picks + rank :].T
    return (
        block_out.astype(bf16).reshape(tokens.shape),
        tokens_grad.astype(bf16).reshape(tokens.shape),
        gain_share,
        in_share,
        vectors[:taps],
        vectors[taps],
        small[:, :picks],
        small[:, picks : picks + rank].T,
        vectors[taps + 1],
        small[:, picks + rank + 8 : picks + rank + 8 + N],
        vectors[taps + 2],
        out_share,
    )


def solution(mesh):
    sharded = P("grp", "seq", None)
    shares = ("seq", "grp")
    return jax.shard_map(
        shards,
        mesh=mesh,
        in_specs=(sharded, sharded) + (P(),) * 10,
        out_specs=(
            sharded,
            sharded,
            P(shares),
            P(shares, None),
            P(None, shares),
            P(shares),
            P(shares, None),
            P(None, shares),
            P(shares),
            P(shares, None),
            P(shares),
            P(shares, None),
        ),
        check_vma=False,
    )
```

```python
import functools
import math

import jax
import jax.numpy as jnp
import ml_dtypes
import numpy as np
from jax import lax
from jax.experimental import pallas as pl
from jax.experimental.pallas import tpu as pltpu
from jax.sharding import PartitionSpec as P

f32 = jnp.float32
bf16 = jnp.bfloat16
LOG2E = 1.4426950408889634
N = 16
T = 16
WIDTH = 512
NL = WIDTH // 128
VMEM = 60 * 2**20


def lane(l):
    return slice(l * 128, (l + 1) * 128)


def sigmoid(v):
    return pltpu.reciprocal(1.0 + jnp.exp2(v * -LOG2E), approx=True)


def joined(ref, rows):
    return jnp.concatenate([ref[l, rows, :] for l in range(NL)], axis=1)


def steps_of(rows):
    return pl.ds(pl.multiple_of(rows, T), T)


def state_of(t):
    return pl.ds(pl.multiple_of(t * N, N), N)


def rows_dot(left, right):
    return lax.dot_general(left, right, (((1,), (1,)), ((), ())), preferred_element_type=f32)


def rates_of(log_ref):
    return -jnp.exp(log_ref[...])


def state_end_kernel(
    proj_ref, rw_ref, rb_ref, x_ref, log_ref, bb_ref, block_ref, dl_ref, u_ref, a2_ref, pre_ref, *, nseq, length,
):
    rows = nseq * length
    a2_ref[...] = rates_of(log_ref) * LOG2E
    low = proj_ref[:, : rw_ref.shape[0]].astype(bf16)
    pre_ref[...] = jnp.dot(low, rw_ref[...], preferred_element_type=f32) + rb_ref[...]

    def steps(i, _):
        r = pl.multiple_of(i * 64, 64)
        at = pl.ds(r, 64)
        pre = pre_ref[at, :]
        d = jnp.maximum(pre, 0.0) + jnp.log(1.0 + jnp.exp(-jnp.abs(pre)))
        for l in range(NL):
            dl_ref[l, at, :] = d[:, lane(l)]
            u_ref[l, at, :] = d[:, lane(l)] * x_ref[l, at, :].astype(f32)
        return 0

    lax.fori_loop(0, rows // 64, steps, 0)
    for s in range(nseq):
        for l in range(NL):
            span = jnp.sum(dl_ref[l, s * length : (s + 1) * length, :], axis=0, keepdims=True)
            high = span.astype(bf16).astype(f32)
            for i, v in enumerate((high, span - high)):
                at = nseq * (N + i) + s
                block_ref[at : at + 1, lane(l)] = v
    block_ref[nseq * (N + 2) :, :] = jnp.zeros((block_ref.shape[0] - nseq * (N + 2), WIDTH), f32)

    def step(c, h):
        h = [list(v) for v in h]
        for k in range(T):
            for s in range(nseq):
                t = s * length + c * T + k
                bt = bb_ref[t]
                for l in range(NL):
                    f = jnp.exp2(dl_ref[l, pl.ds(t, 1), :] * a2_ref[:, lane(l)])
                    h[s][l] = f * h[s][l] + u_ref[l, pl.ds(t, 1), :] * bt
        return tuple(tuple(v) for v in h)

    z = jnp.zeros((N, 128), f32)
    h = lax.fori_loop(0, length // T, step, ((z,) * NL,) * nseq)
    for s in range(nseq):
        for l in range(NL):
            block_ref[s * N : (s + 1) * N, lane(l)] = h[s][l]


def adjoint_end_kernel(dl_ref, g_ref, log_ref, cb_ref, sb_ref, a2_ref, *, nseq, length):
    a2_ref[...] = rates_of(log_ref) * LOG2E
    nch = length // T

    def step(m, lam):
        lam = [list(v) for v in lam]
        c = nch - 1 - m
        for k in reversed(range(T)):
            for s in range(nseq):
                t = s * length + c * T + k
                ct = cb_ref[t]
                for l in range(NL):
                    f = jnp.exp2(dl_ref[l, pl.ds(t, 1), :] * a2_ref[:, lane(l)])
                    lam[s][l] = f * (lam[s][l] + g_ref[l, pl.ds(t, 1), :] * ct)
        return tuple(tuple(v) for v in lam)

    z = jnp.zeros((N, 128), f32)
    lam = lax.fori_loop(0, nch, step, ((z,) * NL,) * nseq)
    for s in range(nseq):
        for l in range(NL):
            sb_ref[s * N : (s + 1) * N, lane(l)] = lam[s][l].astype(bf16)


def forward_kernel(
    dl_ref, u_ref, g_ref, ga_ref, gs_ref, x_ref, skip_ref, bb_ref, bc_ref, lc_ref, log_ref, hin_ref,
    hb_ref, gated_ref, ggr_ref, outg_ref, gu_ref, sk_ref, a2_ref, *, nseq, length, unroll,
):
    a2_ref[...] = rates_of(log_ref) * LOG2E
    nch = length // T
    skip = skip_ref[...]
    ones = jnp.ones((8, 128), bf16)

    @pl.when(pl.program_id(0) == 0)
    def _():
        outg_ref[...] = jnp.zeros_like(outg_ref)
        gu_ref[...] = jnp.zeros_like(gu_ref)

    def chunk(c, h, acc):
        hbv, pov = {}, [[None] * T for _ in range(nseq)]
        for k in range(T):
            for s in range(nseq):
                t = s * length + c * T + k
                bt = bb_ref[t]
                po = None
                for l in range(NL):
                    g = jnp.broadcast_to(g_ref[l, pl.ds(t, 1), :], (N, 128)).astype(bf16)
                    f = jnp.exp2(dl_ref[l, pl.ds(t, 1), :] * a2_ref[:, lane(l)])
                    held = f * h[s][l]
                    h[s][l] = held + u_ref[l, pl.ds(t, 1), :] * bt
                    hb = held.astype(bf16)
                    hb_ref[state_of(t), lane(l)] = hb
                    hbv[k, s, l] = hb
                    po = hb * g if po is None else po + hb * g
                pov[s][k] = po
        lhs = jnp.concatenate([lc_ref[steps_of(s * length + c * T), :] for s in range(nseq)], axis=0)
        parts = []
        for l in range(0, NL, 2):
            rhs = jnp.concatenate(
                [
                    jnp.concatenate([hbv[k, s, l], hbv[k, s, l + 1]], axis=1)
                    for k in range(T) for s in range(nseq)
                ],
                axis=0,
            )
            parts.append(jnp.dot(lhs, rhs, preferred_element_type=f32))
        sc_all = jnp.concatenate(parts, axis=1)
        for s in range(nseq):
            og = rows_dot(ones, jnp.concatenate(pov[s], axis=0))
            outg_ref[pl.ds(s * nch + c, 1), :] += og[:1]
            at = steps_of(s * length + c * T)
            x = joined(x_ref, at).astype(f32)
            gx = joined(g_ref, at) * x
            d = joined(dl_ref, at)
            bc = jnp.concatenate([bc_ref[at, :]] * NL, axis=1)
            mo = sc_all[s * T : (s + 1) * T] + (d * bc + skip) * x
            gu = gx * d
            gu_ref[at, :] += sum(gu[:, lane(l)] for l in range(NL))
            gated_ref[at, :] = (mo * joined(ga_ref, at)).astype(bf16)
            ggr_ref[at, :] = (mo * joined(gs_ref, at)).astype(bf16)
            acc = acc + gx
        return acc

    def step(i, carry):
        h, acc = carry
        h = [list(v) for v in h]
        for p in range(unroll):
            acc = chunk(i * unroll + p, h, acc)
        return tuple(tuple(v) for v in h), acc

    h0 = tuple(tuple(hin_ref[s, :, lane(l)] for l in range(NL)) for s in range(nseq))
    _, acc = lax.fori_loop(0, nch // unroll, step, (h0, jnp.zeros((T, WIDTH), f32)))
    sk_ref[...] = jnp.broadcast_to(jnp.sum(acc, axis=0, keepdims=True), sk_ref.shape)


def backward_kernel(
    dl_ref, u_ref, g_ref, x_ref, skip_ref, cb_ref, lb_ref, ls_ref, log_ref, lin_ref, hb_ref,
    rl_ref, cp_ref, ing_ref, dlog_ref, rb_ref, a2_ref, *, nseq, length, unroll,
):
    a2_ref[...] = rates_of(log_ref) * LOG2E
    nch = length // T
    abf = rates_of(log_ref).astype(bf16)
    skip = skip_ref[...]
    ones = jnp.ones((8, 128), bf16)

    @pl.when(pl.program_id(0) == 0)
    def _():
        ing_ref[...] = jnp.zeros_like(ing_ref)

    def chunk(c, lam, dlog, rb):
        pov = [[None] * T for _ in range(nseq)]
        dacc = [None] * NL
        vals = {}
        for k in reversed(range(T)):
            for s in range(nseq):
                t = s * length + c * T + k
                ct = cb_ref[t]
                po = None
                for l in range(NL):
                    d = jnp.broadcast_to(dl_ref[l, pl.ds(t, 1), :], (N, 128))
                    u = jnp.broadcast_to(u_ref[l, pl.ds(t, 1), :], (N, 128)).astype(bf16)
                    a = g_ref[l, pl.ds(t, 1), :] * ct + lam[s][l]
                    lam[s][l] = jnp.exp2(d * a2_ref[:, lane(l)]) * a
                    ab = a.astype(bf16)
                    q = ab * hb_ref[state_of(t), lane(l)] * abf[:, lane(l)]
                    qd = q * d.astype(bf16)
                    vals[k, s, l] = (ab, q)
                    dacc[l] = qd if dacc[l] is None else dacc[l] + qd
                    po = ab * u if po is None else po + ab * u
                pov[s][k] = po
            if k % 8 == 0:
                for l in range(NL):
                    dlog[l] = dlog[l] + dacc[l].astype(f32)
                    dacc[l] = None
        lhs = jnp.concatenate(
            [lb_ref[steps_of(s * length + c * T), :] for s in range(nseq)] + [ls_ref[...]], axis=0
        )
        parts = []
        for l in range(0, NL, 2):
            rhs = jnp.concatenate(
                [
                    jnp.concatenate([vals[k, s, l][y], vals[k, s, l + 1][y]], axis=1)
                    for k in reversed(range(T)) for s in range(nseq) for y in range(2)
                ],
                axis=0,
            )
            parts.append(jnp.dot(lhs, rhs, preferred_element_type=f32))
        both = jnp.concatenate(parts, axis=1)
        for s in range(nseq):
            w = both[s * T : (s + 1) * T]
            qs = both[(nseq + s) * T : (nseq + s + 1) * T]
            ig = rows_dot(ones, jnp.concatenate(pov[s], axis=0))
            ing_ref[pl.ds(s * nch + c, 1), :] += ig[:1]
            at = steps_of(s * length + c * T)
            d = joined(dl_ref, at)
            rg = (qs + w * joined(x_ref, at).astype(f32)) * (1.0 - jnp.exp(-d))
            rb = rb + rg
            rl_ref[at, :] = rg.astype(bf16)
            cp_ref[at, :] = w * d + skip * joined(g_ref, at)
        return rb

    def step(m, carry):
        lam, dlog, rb = carry
        lam = [list(v) for v in lam]
        dlog = list(dlog)
        for p in range(unroll):
            rb = chunk(nch - 1 - (m * unroll + p), lam, dlog, rb)
        return tuple(tuple(v) for v in lam), tuple(dlog), rb

    l0 = tuple(tuple(lin_ref[s, :, lane(l)] for l in range(NL)) for s in range(nseq))
    z = jnp.zeros((N, 128), f32)
    _, dlog, rb = lax.fori_loop(0, nch // unroll, step, (l0, (z,) * NL, jnp.zeros((T, WIDTH), f32)))
    for l in range(NL):
        dlog_ref[:, lane(l)] = dlog[l]
    rb_ref[...] = jnp.broadcast_to(jnp.sum(rb, axis=0, keepdims=True), rb_ref.shape)


def block_of(rows):
    return pl.BlockSpec((rows, WIDTH), lambda j: (0, j))


def tiles_of(rows):
    return pl.BlockSpec((NL, rows, 128), lambda j: (j, 0, 0))


def states_of(nseq):
    return pl.BlockSpec((nseq, N, WIDTH), lambda j: (0, 0, j))


def whole(a):
    return pl.BlockSpec(a.shape, lambda j: (0,) * a.ndim, pipeline_mode=pl.Buffered(1))


def kernel_call(body, name, channels, operands, specs, out_specs, outs, flops, scratch=(), **options):
    moved = sum(a.size * a.dtype.itemsize for a in operands) + sum(
        math.prod(o.shape) * o.dtype.itemsize for o in outs
    )
    return pl.pallas_call(
        functools.partial(body, **options),
        grid=(channels // WIDTH,),
        in_specs=specs,
        out_specs=out_specs,
        out_shape=outs,
        scratch_shapes=scratch,
        compiler_params=pltpu.CompilerParams(vmem_limit_bytes=VMEM, dimension_semantics=("arbitrary",)),
        cost_estimate=pl.CostEstimate(flops=flops, bytes_accessed=moved, transcendentals=0),
        name=name,
    )(*operands)


def spread(values, nseq, length, kinds, reverse):
    mask = own_column(nseq * length, length, nseq, kinds, 0, reverse)
    width = mask.shape[1]
    pick = (np.arange(width)[None, :] % N == np.arange(N)[:, None]).astype(ml_dtypes.bfloat16)
    wide = jnp.dot(values.astype(bf16), pick, preferred_element_type=f32)
    return wide.astype(bf16) * mask


def own_column(rows, length, nseq, kinds, kind, reverse):
    column = np.arange(T * nseq * kinds * N)[None, :]
    row = np.arange(rows)[:, None]
    step = column // (nseq * kinds * N)
    if reverse:
        step = T - 1 - step
    own = (step == row % T) & ((column // (kinds * N)) % nseq == row // length) & ((column // N) % kinds == kind)
    return own.astype(ml_dtypes.bfloat16)


def block_rows(nseq):
    return -(-nseq * (N + 2) // 16) * 16


def state_end(proj, rate_weight, rate_bias, x, log, bb, nseq, length):
    tiles, rows, _ = x.shape
    ch = tiles * 128
    o = jax.ShapeDtypeStruct
    return kernel_call(
        state_end_kernel, "state_end", ch,
        (proj, rate_weight, rate_bias, x, log, bb),
        [whole(proj), block_of(rate_weight.shape[0]), block_of(1), tiles_of(rows), block_of(N), whole(bb)],
        [block_of(block_rows(nseq)), tiles_of(rows), tiles_of(rows)],
        (o((block_rows(nseq), ch), f32), o(x.shape, f32), o(x.shape, f32)),
        2 * 10**10, nseq=nseq, length=length,
        scratch=[pltpu.VMEM((N, WIDTH), f32), pltpu.VMEM((rows, WIDTH), f32)],
    )


def adjoint_end(dl, g, log, cb, nseq, length):
    tiles, rows, _ = dl.shape
    ch = tiles * 128
    return kernel_call(
        adjoint_end_kernel, "adjoint_end", ch,
        (dl, g, log, cb),
        [tiles_of(rows), tiles_of(rows), block_of(N), whole(cb)],
        [block_of(nseq * N)],
        (jax.ShapeDtypeStruct((nseq * N, ch), bf16),),
        2 * 10**10, nseq=nseq, length=length, scratch=[pltpu.VMEM((N, WIDTH), f32)],
    )[0]


def forward(dl, u, g, ga, gs, x, skip, bb, bc, lc, log, hin, nseq, length, unroll=1):
    tiles, rows, _ = dl.shape
    ch = tiles * 128
    o = jax.ShapeDtypeStruct
    t = tiles_of(rows)
    return kernel_call(
        forward_kernel, "forward", ch,
        (dl, u, g, ga, gs, x, skip, bb, bc, lc, log, hin),
        [t, t, t, t, t, t, block_of(1), whole(bb), whole(bc), whole(lc), block_of(N), states_of(nseq)],
        [
            block_of(rows * N), block_of(rows), block_of(rows), pl.BlockSpec((rows // T, T * N), lambda j: (0, 0)),
            pl.BlockSpec((rows, 128), lambda j: (0, 0)), block_of(8),
        ],
        (
            o((rows * N, ch), bf16), o((rows, ch), bf16), o((rows, ch), bf16), o((rows // T, T * N), f32),
            o((rows, 128), f32), o((8, ch), f32),
        ),
        3 * 10**10, nseq=nseq, length=length, unroll=unroll, scratch=[pltpu.VMEM((N, WIDTH), f32)],
    )


def backward(dl, u, g, x, skip, cb, lb, ls, log, lin, hb, nseq, length, unroll=1):
    tiles, rows, _ = dl.shape
    ch = tiles * 128
    o = jax.ShapeDtypeStruct
    t = tiles_of(rows)
    st = states_of(nseq)
    return kernel_call(
        backward_kernel, "backward", ch,
        (dl, u, g, x, skip, cb, lb, ls, log, lin, hb),
        [t, t, t, t, block_of(1), whole(cb), whole(lb), whole(ls), block_of(N), st, block_of(rows * N)],
        [block_of(rows), block_of(rows), pl.BlockSpec((rows // T, T * N), lambda j: (0, 0)), block_of(N), block_of(8)],
        (o((rows, ch), bf16), o((rows, ch), f32), o((rows // T, T * N), f32), o((N, ch), f32), o((8, ch), f32)),
        5 * 10**10, nseq=nseq, length=length, unroll=unroll, scratch=[pltpu.VMEM((N, WIDTH), f32)],
    )


epsilon = 1e-05
ROWS = 64
PAD = 8


def normalized(tokens, gain):
    wide = tokens.astype(f32)
    return (wide * lax.rsqrt(jnp.mean(wide * wide, axis=1, keepdims=True) + epsilon) * gain).astype(bf16)


def gate_kernel(tok_ref, gain_ref, cot_ref, wg_ref, ow_ref, normed_ref, turned_ref, scale_ref, g_ref, ga_ref, gs_ref, gh_ref, gg_ref):
    rows = tok_ref.shape[0]

    @pl.when(pl.program_id(0) == 0)
    def _():
        def norm(i, _):
            at = pl.ds(pl.multiple_of(i * ROWS, ROWS), ROWS)
            wide = tok_ref[at, :].astype(f32)
            scale = lax.rsqrt(jnp.mean(wide * wide, axis=1, keepdims=True) + epsilon)
            scale_ref[at, :] = jnp.broadcast_to(scale, (ROWS, 128))
            normed_ref[at, :] = (wide * scale * gain_ref[...]).astype(bf16)
            return 0

        lax.fori_loop(0, rows // ROWS, norm, 0)
        turned_ref[...] = normed_ref[...].T

    gh_ref[...] = jnp.dot(normed_ref[...], wg_ref[...], preferred_element_type=f32)
    gg_ref[...] = rows_dot(cot_ref[...], ow_ref[...])

    def mix(i, _):
        at = pl.ds(pl.multiple_of(i * ROWS, ROWS), ROWS)
        gh = gh_ref[at, :]
        gg = gg_ref[at, :]
        sg = sigmoid(gh)
        ga = gh * sg
        gs = gg * (sg * (1.0 + gh * (1.0 - sg)))
        g = gg * ga
        for l in range(NL):
            g_ref[l, at, :] = g[:, lane(l)]
            ga_ref[l, at, :] = ga[:, lane(l)]
            gs_ref[l, at, :] = gs[:, lane(l)]
        return 0

    lax.fori_loop(0, rows // ROWS, mix, 0)


def gate_side(tokens, gain, cotangent, in_weight, out_weight):
    rows, model = tokens.shape
    inner = out_weight.shape[0]
    first = inner // WIDTH
    tiles = jax.ShapeDtypeStruct((inner // 128, rows, 128), f32)
    return kernel_call(
        gate_kernel, "gate_side", inner,
        (tokens, gain, cotangent, in_weight, out_weight),
        [
            whole(tokens), whole(gain), whole(cotangent),
            pl.BlockSpec((model, WIDTH), lambda j: (0, j + first)),
            pl.BlockSpec((WIDTH, model), lambda j: (j, 0)),
        ],
        [pl.BlockSpec((rows, model), lambda j: (0, 0)), pl.BlockSpec((model, rows), lambda j: (0, 0)), pl.BlockSpec((rows, 128), lambda j: (0, 0))]
        + [tiles_of(rows)] * 3,
        (jax.ShapeDtypeStruct((rows, model), bf16), jax.ShapeDtypeStruct((model, rows), bf16), jax.ShapeDtypeStruct((rows, 128), f32), tiles, tiles, tiles),
        4 * rows * model * inner, scratch=[pltpu.VMEM((rows, WIDTH), f32)] * 2,
    )


def inner_kernel(
    normed_ref, halo_ref, gain_ref, wi_ref, cw_ref, cb_ref, sw_ref, inner_ref, before_ref, x_ref, slope_ref, proj_ref, ext_ref, flat_ref,
    *, nseq, length,
):
    part = jnp.dot(normed_ref[...], wi_ref[...], preferred_element_type=f32).astype(bf16)
    inner_ref[...] = part
    for s in range(nseq):
        for l in range(NL):
            ext_ref[s, l, PAD:, :] = part[s * length : (s + 1) * length, lane(l)].astype(f32)
    before = jnp.dot(
        normalized(halo_ref[...], gain_ref[...]), wi_ref[...], preferred_element_type=f32
    ).astype(bf16)
    before_ref[...] = before
    for s in range(nseq):
        for l in range(NL):
            ext_ref[s, l, :PAD, :] = before[s * PAD : (s + 1) * PAD, lane(l)].astype(f32)

    @pl.when(pl.program_id(0) == 0)
    def _():
        proj_ref[...] = jnp.zeros_like(proj_ref)

    taps = cw_ref.shape[0]
    for s in range(nseq):

        def mix(i, _):
            r = pl.multiple_of(i * ROWS, ROWS)
            at = pl.ds(pl.multiple_of(s * length + r, ROWS), ROWS)
            for l in range(NL):
                pre = cb_ref[:, lane(l)]
                for k in range(taps):
                    pre = pre + cw_ref[k : k + 1, lane(l)] * ext_ref[s, l, pl.ds(r + PAD - taps + 1 + k, ROWS), :]
                sg = sigmoid(pre)
                x = (pre * sg).astype(bf16)
                slope_ref[at, lane(l)] = sg * (1.0 + pre * (1.0 - sg))
                x_ref[l, at, :] = x
                flat_ref[at, lane(l)] = x
            return 0

        lax.fori_loop(0, length // ROWS, mix, 0)
    proj_ref[...] += jnp.dot(flat_ref[...], sw_ref[...], preferred_element_type=f32)


def inner_side(normed, halo, gain, in_weight, conv_weight, conv_bias, select_weight, nseq, length):
    rows, model = normed.shape
    inner, picks = select_weight.shape
    o = jax.ShapeDtypeStruct
    operands = (normed, halo, gain, in_weight, conv_weight, conv_bias, select_weight)
    specs = [
        whole(normed), whole(halo), whole(gain), block_of(model), block_of(conv_weight.shape[0]), block_of(1),
        pl.BlockSpec((WIDTH, picks), lambda j: (j, 0)),
    ]
    return pl.pallas_call(
        functools.partial(inner_kernel, nseq=nseq, length=length),
        grid=(inner // WIDTH,),
        in_specs=specs,
        out_specs=[
            block_of(rows), block_of(halo.shape[0]), tiles_of(rows), block_of(rows),
            pl.BlockSpec((rows, picks), lambda j: (0, 0)),
        ],
        out_shape=(
            o((rows, inner), bf16), o((halo.shape[0], inner), bf16), o((inner // 128, rows, 128), bf16),
            o((rows, inner), f32), o((rows, picks), f32),
        ),
        scratch_shapes=[pltpu.VMEM((nseq, NL, PAD + length, 128), f32), pltpu.VMEM((rows, WIDTH), bf16)],
        compiler_params=pltpu.CompilerParams(vmem_limit_bytes=VMEM, dimension_semantics=("arbitrary",)),
        cost_estimate=pl.CostEstimate(flops=2 * rows * model * inner, bytes_accessed=14 * 2**20, transcendentals=0),
        name="inner_side",
    )(*operands)


def input_grad_kernel(
    place_ref, cp_ref, inner_ref, before_ref, x_ref, slope_ref, pg_ref, sw_ref, cw_ref, turned_ref, halo_ref, gain_ref,
    rl_ref, proj_ref, dlog_ref, rb_ref, sk_ref, *refs, nseq, length, part, rank, grp, last,
):
    if last:
        early_ref, kept_ref, sent_ref, igr_ref, tail_ref, head_ref, pre_ref, back_ref, vec_ref = refs
    else:
        early_ref, (kept_ref, sent_ref, igr_ref, tail_ref, head_ref, small_ref, pre_ref, back_ref, vec_ref) = None, refs
    taps = cw_ref.shape[0]
    j = pl.program_id(0)
    wide = pg_ref.shape[1]
    back_ref[...] = cp_ref[...] + rows_dot(pg_ref[:, wide // 2 :], sw_ref[...])
    vec_ref[...] = jnp.zeros_like(vec_ref)
    small_step = 32
    for s in range(nseq):
        pre_ref[s, :, :PAD, :] = jnp.zeros((NL, PAD, 128), f32)
        pre_ref[s, :, PAD + length :, :] = jnp.zeros((NL, PAD, 128), f32)

        def first(i, total):
            r = pl.multiple_of(i * small_step, small_step)
            at = pl.ds(pl.multiple_of(s * length + r, small_step), small_step)
            back = back_ref[at, :] * slope_ref[at, :]
            for l in range(NL):
                pre_ref[s, l, pl.ds(pl.multiple_of(r + PAD, PAD), small_step), :] = back[:, lane(l)]
            return total + sum(back[q * 8 : (q + 1) * 8] for q in range(small_step // 8))

        total = lax.fori_loop(0, length // small_step, first, jnp.zeros((8, WIDTH), f32))
        vec_ref[taps : taps + 1, :] += jnp.sum(total, axis=0, keepdims=True)

        def second(i, totals):
            r = pl.multiple_of(i * small_step, small_step)
            at = pl.ds(pl.multiple_of(s * length + r, small_step), small_step)
            sums = []
            for l in range(NL):
                inner = inner_ref[at, lane(l)].astype(f32)
                result = jnp.zeros((small_step, 128), f32)
                for k in range(taps):
                    later = pre_ref[s, l, pl.ds(r + PAD + taps - 1 - k, small_step), :]
                    result = result + cw_ref[k : k + 1, lane(l)] * later
                    product = inner * later
                    sums.append(
                        totals[l * taps + k] + sum(product[q * 8 : (q + 1) * 8] for q in range(small_step // 8))
                    )
                igr_ref[at, lane(l)] = result.astype(bf16)
            return tuple(sums)

        totals = lax.fori_loop(0, length // small_step, second, (jnp.zeros((8, 128), f32),) * (taps * NL))
        head_rows = lax.broadcasted_iota(jnp.int32, (PAD, 128), 0) < taps - 1
        for l in range(NL):
            late = pre_ref[s, l, length:, :]
            tail_ref[s * PAD : (s + 1) * PAD, lane(l)] = sum(
                cw_ref[k : k + 1, lane(l)] * late[taps - 1 - k : taps - 1 - k + PAD] for k in range(taps)
            )
            lead = pre_ref[s, l, : 2 * PAD, :]
            before = before_ref[s * PAD : (s + 1) * PAD, lane(l)].astype(f32)
            before = jnp.concatenate([before[PAD - taps + 1 :], jnp.zeros((PAD - taps + 1, 128), f32)], axis=0)
            head = jnp.zeros((PAD, 128), f32)
            for k in range(taps):
                early = jnp.where(head_rows, lead[PAD - k : 2 * PAD - k], 0.0)
                head = head + cw_ref[k : k + 1, lane(l)] * early
                vec_ref[k : k + 1, lane(l)] += jnp.sum(totals[l * taps + k] + before * early, axis=0, keepdims=True)
            head_ref[s * PAD : (s + 1) * PAD, lane(l)] = head

    vec_ref[taps + 1 : taps + 2, :] = rb_ref[0:1, :]
    vec_ref[taps + 2 : taps + 3, :] = sk_ref[0:1, :]
    vec_ref[8:, :] = dlog_ref[...]
    count = place_ref.shape[0] - 1
    rows_each = turned_ref.shape[0] // count
    rows_pad = padded(rows_each)
    before_normed = normalized(halo_ref[...], gain_ref[...])
    products = []
    for b in range(WIDTH // wide):
        cols = slice(b * wide, (b + 1) * wide)
        shifted = jnp.concatenate(
            [
                jnp.concatenate(
                    [jnp.zeros((PAD - taps + 1, wide), f32), head_ref[s * PAD : s * PAD + taps - 1, cols]], axis=0
                )
                for s in range(nseq)
            ],
            axis=0,
        )
        product = jnp.dot(turned_ref[...], igr_ref[:, cols], preferred_element_type=f32) + contract_rows(
            before_normed, shifted.astype(bf16)
        )
        products.append(product.astype(bf16) if rows_each == rows_pad else product)
    eye = (
        lax.broadcasted_iota(jnp.int32, (vec_ref.shape[0], wide), 0) + rank
        == lax.broadcasted_iota(jnp.int32, (vec_ref.shape[0], wide), 1)
    ).astype(bf16)
    low = jnp.concatenate([proj_ref[...], jnp.zeros((proj_ref.shape[0], wide - proj_ref.shape[1]), f32)], axis=1)
    low = jnp.where(lax.broadcasted_iota(jnp.int32, low.shape, 1) < rank, low, 0.0).astype(bf16)
    small = (
        contract_rows(joined(x_ref, slice(None)), pg_ref[...])
        + contract_rows(rl_ref[...], low)
        + contract_rows(vec_ref[...].astype(bf16), eye)
    )
    def store(flag):
        half = count // 2
        for q in range(count):
            ref = kept_ref if (q // grp) % 2 == flag else sent_ref
            spot = lax.rem(place_ref[q], half)
            for b, product in enumerate(products):
                at = pl.ds(pl.multiple_of((j * len(products) + b) * rows_pad, rows_pad), rows_pad)
                ref[spot, at, :] = share_rows(product, q, rows_each)

    core = place_ref[count]
    for flag in range(2):
        pl.when(core == flag)(functools.partial(store, flag))
    if not last:
        small_ref[...] = small.astype(small_ref.dtype)
        return
    base = kept_ref.shape[1] - padded(part)

    def place_small(values, first):
        for q in range(WIDTH // part):
            share = place_ref[first + q]
            rows = share_rows(values, q, part)

            @pl.when(share < count // 2)
            def _():
                kept_ref[share, base : base + padded(part), :] = rows

            @pl.when(share >= count // 2)
            def _():
                sent_ref[share - count // 2, base : base + padded(part), :] = rows

    steps = pl.num_programs(0)
    place_small(early_ref[...], j * (WIDTH // part))
    place_small(small, (steps + j) * (WIDTH // part))


def input_grads(
    place, cp, inner, before, x, slope, pg, select_weight, conv_weight, turned, halo, gain, rate_low, proj,
    decay_grad, rate_bias_grad, skip_grad, early, nseq, length, part, rank, grp,
):
    rows, width = cp.shape
    width = width // 2
    last = early is not None
    first = width // WIDTH if last else 0
    wide = pg.shape[1]
    count = place.shape[0] - 1
    model = turned.shape[0]
    packed_rows = (width // wide) * padded(model // count) + (padded(part) if last else 0)
    o = jax.ShapeDtypeStruct

    def drop(spec, first=0):
        return pl.BlockSpec(
            spec.block_shape, lambda j, _, f=spec.index_map: f(j + first), pipeline_mode=spec.pipeline_mode
        )

    specs = [
        block_of(rows), block_of(rows), block_of(before.shape[0]), tiles_of(rows), block_of(rows), whole(pg),
        pl.BlockSpec((WIDTH, wide // 2), lambda j: (j, 0)), block_of(conv_weight.shape[0]), whole(turned),
        whole(halo), whole(gain), block_of(rows), whole(proj), block_of(N), block_of(8), block_of(8),
    ]
    packed = pl.BlockSpec((count // 2, packed_rows, wide), lambda j: (0, 0, 0))
    out_specs = [packed, packed, block_of(rows), block_of(nseq * PAD), block_of(nseq * PAD)]
    outs = [
        o((count // 2, packed_rows, wide), bf16), o((count // 2, packed_rows, wide), bf16), o((rows, width), bf16),
        o((nseq * PAD, width), f32), o((nseq * PAD, width), f32),
    ]
    operands = [
        place, cp, inner, before, x, slope, pg, select_weight, conv_weight, turned, halo, gain, rate_low, proj,
        decay_grad, rate_bias_grad, skip_grad,
    ]
    in_specs = [drop(s, first) for s in specs]
    block = pl.BlockSpec((WIDTH, wide), lambda j: (j, 0))
    if last:
        operands.append(early)
        in_specs.append(drop(block))
    else:
        out_specs.append(block)
        outs.append(o((width, wide), f32 if part < 16 else bf16))
    return pl.pallas_call(
        functools.partial(input_grad_kernel, nseq=nseq, length=length, part=part, rank=rank, grp=grp, last=last),
        grid_spec=pltpu.PrefetchScalarGridSpec(
            num_scalar_prefetch=1,
            grid=(width // WIDTH,),
            in_specs=in_specs,
            out_specs=[drop(s) for s in out_specs],
            scratch_shapes=[
                pltpu.VMEM((nseq, NL, PAD + length + PAD, 128), f32), pltpu.VMEM((rows, WIDTH), f32),
                pltpu.VMEM((8 + N, WIDTH), f32),
            ],
        ),
        out_shape=outs,
        compiler_params=pltpu.CompilerParams(vmem_limit_bytes=VMEM, dimension_semantics=("arbitrary",)),
        cost_estimate=pl.CostEstimate(flops=24 * rows * width * model, bytes_accessed=16 * 2**20, transcendentals=0),
        name="input_grads",
    )(*operands)


def padded(rows):
    return max(rows, 16)


def share_rows(values, share, rows):
    taken = values[share * rows : (share + 1) * rows]
    if rows < padded(rows):
        taken = jnp.concatenate([taken, jnp.zeros((padded(rows) - rows, values.shape[1]), values.dtype)], axis=0)
    return taken.astype(bf16)


def weight_grad_kernel(gated_ref, gate_ref, cot_ref, turned_ref, packed_ref, *, part):
    j = pl.program_id(0)
    count = packed_ref.shape[0]
    model = cot_ref.shape[1]
    rows_each = model // count
    rows_pad = padded(rows_each)
    product = contract_rows(gated_ref[...], cot_ref[...])
    for q in range(WIDTH // part):
        packed_ref[j * (WIDTH // part) + q, : padded(part), :] = share_rows(product, q, part)
    product = jnp.dot(turned_ref[...], gate_ref[...], preferred_element_type=f32)
    each = model // WIDTH
    at = pl.ds(pl.multiple_of(padded(part) + (j // each) * rows_pad, 16), rows_pad)
    cols = pl.ds(pl.multiple_of((j % each) * WIDTH, WIDTH), WIDTH)
    for q in range(count):
        packed_ref[q, at, cols] = share_rows(product, q, rows_each)


def weight_grads(gated, gate_grad, cot, turned, part):
    rows, width = gated.shape
    model = cot.shape[1]
    count = width // part
    packed_rows = padded(part) + (width // model) * padded(model // count)
    return pl.pallas_call(
        functools.partial(weight_grad_kernel, part=part),
        grid=(width // WIDTH,),
        in_specs=[block_of(rows), block_of(rows), whole(cot), whole(turned)],
        out_specs=pl.BlockSpec((count, packed_rows, model), lambda j: (0, 0, 0)),
        out_shape=jax.ShapeDtypeStruct((count, packed_rows, model), bf16),
        compiler_params=pltpu.CompilerParams(vmem_limit_bytes=VMEM, dimension_semantics=("arbitrary",)),
        cost_estimate=pl.CostEstimate(flops=4 * rows * width * model, bytes_accessed=14 * 2**20, transcendentals=0),
        name="weight_grads",
    )(gated, gate_grad, cot, turned)


def flip_bit(axis, bit):
    return [(i, i ^ bit) for i in range(lax.axis_size(axis))]


def bits_of(axis):
    size = lax.axis_size(axis)
    return [(axis, 1 << k) for k in range(size.bit_length() - 1)]


def places(order):
    grp = lax.axis_size("grp")
    other = jnp.arange(lax.axis_size("seq") * grp) ^ (lax.axis_index("seq") * grp + lax.axis_index("grp"))
    position = jnp.zeros_like(other)
    for axis, bit in order:
        position = 2 * position + (other // (bit * grp if axis == "seq" else bit)) % 2
    return position.astype(jnp.int32)


def pairs_of(bits):
    return [bits[i : i + 2] for i in range(0, len(bits), 2)]


def round_parts(held, bits):
    count = 1 << len(bits)
    size = held[0].shape[0] // count
    parts = [sum(h[i * size : (i + 1) * size].astype(f32) for h in held) for i in range(count)]
    return parts[:1] + [part.astype(bf16) for part in parts[1:]]


def round_trade(parts, bits):
    held = parts[:1]
    for i in range(1, len(parts)):
        flip = sum(bit for at, (axis, bit) in enumerate(bits) if (i >> (len(bits) - 1 - at)) & 1)
        held.append(lax.ppermute(parts[i], bits[0][0], flip_bit(bits[0][0], flip)))
    return held


def sum_packed(kept, sent, rounds, later):
    axis, bit = rounds[0][0]
    held = [kept, lax.ppermute(sent, axis, flip_bit(axis, bit))]
    for bits in rounds[1:]:
        parts = round_parts(held, bits)
        if later is not None:
            *parts, later = lax.optimization_barrier((*parts, later))
        held = round_trade(parts, bits)
    return held, later


def sum_rounds(held, rounds):
    for bits in rounds:
        held = round_trade(round_parts(held, bits), bits)
    return sum(h[0].astype(f32) for h in held)


def carried(block, shape, rates, backward, after=None, spans=None):
    count, mine = lax.axis_size("seq"), lax.axis_index("seq")
    blocks = lax.all_gather(block.astype(bf16), "seq")
    if after is not None:
        blocks, after = lax.optimization_barrier((blocks, after))
    rows = shape[0] * shape[1]
    entering = jnp.zeros(shape, f32)
    for turn in range(count - 1):
        j = count - 1 - turn if backward else turn
        theirs = blocks[j].astype(f32)
        span = (theirs if spans is None else spans[j].astype(f32))[rows : rows + 2 * shape[0]]
        span = span[: shape[0]] + span[shape[0] :]
        longer = jnp.exp(span[:, None, :] * rates) * entering + theirs[:rows].reshape(shape)
        entering = jnp.where(mine < j if backward else j < mine, longer, entering)
    return entering, after, blocks


def contract_rows(left, right, kind=f32):
    return lax.dot_general(left, right, (((0,), (0,)), ((), ())), preferred_element_type=f32).astype(kind)


def shards(
    tokens,
    cotangent,
    norm_gain,
    in_weight,
    conv_weight,
    conv_bias,
    select_weight,
    rate_weight,
    rate_bias,
    decay_log,
    skip_gain,
    out_weight,
):
    nseq, length, model = tokens.shape
    inner_width = out_weight.shape[0]
    rank = rate_weight.shape[0]
    taps = conv_weight.shape[0]
    rows = nseq * length
    share_count = lax.axis_size("seq") * lax.axis_size("grp")
    tok = tokens.reshape(rows, model)
    cot = cotangent.reshape(rows, model)
    gain, skip, bias = norm_gain[None], skip_gain[None], conv_bias[None]
    pieces, grp = lax.axis_size("seq"), lax.axis_size("grp")
    halo = lax.ppermute(tokens[:, length - PAD :], "seq", [(i, i + 1) for i in range(pieces - 1)])
    halo = halo.reshape(nseq * PAD, model)
    normed, turned, scale, g, ga, gs = gate_side(tok, gain, cot, in_weight, out_weight)
    picks, wide = rank + 2 * N, 256
    select_weight = jnp.pad(select_weight, ((0, 0), (0, wide // 2 - picks)))
    inner, before, x, slope, proj = inner_side(
        normed, halo, gain, in_weight, conv_weight, bias, select_weight, nseq, length
    )
    in_gate, out_gate = proj[:, rank : rank + N], proj[:, rank + N : picks]
    log = decay_log.T
    rates = -jnp.exp(log)
    bb = jnp.broadcast_to(in_gate[:, :, None], (rows, N, 128))
    ahead, dl, u = state_end(proj, rate_weight, rate_bias[None], x, log, bb, nseq, length)
    ahead, g = lax.optimization_barrier((ahead.astype(bf16), g))
    state_shape = (nseq, N, inner_width)
    entering, _, spans = carried(ahead, state_shape, rates, False)
    cb = jnp.broadcast_to(out_gate[:, :, None], (rows, N, 128))
    sent_back = adjoint_end(dl, g, log, cb, nseq, length)
    lc = spread(out_gate, nseq, length, 1, False)
    lb = spread(in_gate, nseq, length, 2, True)
    ls = jnp.asarray(own_column(nseq * T, T, nseq, 2, 1, True))
    meet = jnp.sum(in_gate * out_gate, axis=1, keepdims=True)
    bc = jnp.broadcast_to(meet, (rows, 128))
    behind, lb, ls, u = lax.optimization_barrier((sent_back, lb, ls, u))
    states, gated, gate_grad, out_grad, shift, skip_grad = forward(
        dl, u, g, ga, gs, x, skip, bb, bc, lc, log, entering, nseq, length, 4
    )
    part, part_rows = inner_width // share_count, model // share_count
    weight_packed = weight_grads(gated, gate_grad, cot, turned, part)
    leaving, weight_packed, _ = carried(behind, state_shape, rates, True, weight_packed, spans)
    weight_sum = lax.psum_scatter(weight_packed, "seq", scatter_dimension=0, tiled=True)
    rate_low, conv_part, in_grad, decay_grad, rate_bias_grad = backward(
        dl, u, g, x, skip, cb, lb, ls, log, leaving, states, nseq, length, 4
    )
    out_grad = out_grad.reshape(rows, N) + in_gate * jnp.sum(shift, axis=1, keepdims=True)
    rank_grad = rows_dot(rate_low, rate_weight)
    pg = jnp.concatenate(
        [
            jnp.zeros((rows, wide // 2), bf16),
            rank_grad.astype(bf16),
            in_grad.reshape(rows, N).astype(bf16),
            out_grad.astype(bf16),
            jnp.zeros((rows, wide // 2 - picks), bf16),
        ],
        axis=1,
    )
    seq_bits, grp_bits = bits_of("seq"), bits_of("grp")
    order = seq_bits + grp_bits
    place = jnp.concatenate([places(order), (lax.axis_index("seq") % 2)[None].astype(jnp.int32)])
    rounds = [seq_bits[:1]] + pairs_of(seq_bits[1:]) + pairs_of(grp_bits)
    half_width = inner_width // 2

    def half(conv_part, early):
        return input_grads(
            place, conv_part, inner, before, x, slope, pg, select_weight, conv_weight, turned, halo, gain, rate_low,
            proj, decay_grad, rate_bias_grad, skip_grad, early, nseq, length, part, rank, grp,
        )

    wide_tok = tok.astype(f32)
    kept, sent, first_grad, first_tail, first_head, early = half(conv_part, None)
    sent, gated = lax.optimization_barrier((sent, gated))
    block_out = wide_tok + jnp.dot(gated, out_weight, preferred_element_type=f32)
    first_held, (conv_part, block_out) = sum_packed(kept, sent, rounds[:2], (conv_part, block_out))
    kept, sent, second_grad, second_tail, second_head = half(conv_part, early)
    head = jnp.concatenate([first_head, second_head], axis=1)
    *first_held, sent, head = lax.optimization_barrier((*first_held, sent, head))
    head = head.reshape(nseq, PAD, inner_width)[:, : taps - 1].astype(bf16)
    returned = lax.ppermute(head, "seq", [(i + 1, i) for i in range(pieces - 1)]).astype(f32)
    held, (returned, gate_grad, first_grad, weight_sum) = sum_packed(
        kept, sent, rounds[:2], (returned, gate_grad, first_grad, weight_sum)
    )
    first_held = sum_rounds(first_held, rounds[2:])
    held = sum_rounds(held, rounds[2:])
    weight_share = lax.psum_scatter(weight_sum, "grp", scatter_dimension=0, tiled=True)[0].astype(f32)
    out_share = weight_share[:part]
    gate_share = weight_share[padded(part) :].reshape(-1, padded(part_rows), model)[:, :part_rows]
    gate_share = gate_share.transpose(1, 0, 2).reshape(part_rows, inner_width)
    blocks = half_width // wide

    def in_rows(held):
        share = held[: blocks * padded(part_rows)].reshape(blocks, padded(part_rows), wide)[:, :part_rows]
        return share.transpose(1, 0, 2).reshape(part_rows, half_width)

    inner_share = jnp.concatenate([in_rows(first_held), in_rows(held)], axis=1)
    small = held[blocks * padded(part_rows) :][:part]
    inner_grad = jnp.concatenate([first_grad, second_grad], axis=1)
    tail = jnp.concatenate([first_tail, second_tail], axis=1)
    fixed = (tail.reshape(nseq, PAD, inner_width)[:, PAD - taps + 1 :] + returned).astype(bf16)
    inner_grad = (
        inner_grad.reshape(nseq, length, inner_width).at[:, length - taps + 1 :].set(fixed).reshape(rows, inner_width)
    )
    scale = scale[:, :1]
    normed_grad = rows_dot(gate_grad, in_weight[:, inner_width:]) + rows_dot(inner_grad, in_weight[:, :inner_width])
    lifted = normed_grad * norm_gain
    dots = jnp.mean(lifted * wide_tok, axis=1, keepdims=True)
    tokens_grad = cot.astype(f32) + scale * lifted - wide_tok * (scale * scale * scale) * dots
    in_share = jnp.concatenate([inner_share, gate_share], axis=1)
    first = (lax.axis_index("seq") * grp + lax.axis_index("grp")) * part_rows
    own_weight = lax.dynamic_slice_in_dim(in_weight, first, part_rows, 0).astype(f32)
    own_gain = lax.dynamic_slice_in_dim(norm_gain, first, part_rows, 0)
    gain_share = jnp.sum(own_weight * in_share, axis=1) / own_gain
    vectors = small[:, rank : rank + 8].T
    return (
        block_out.astype(bf16).reshape(tokens.shape),
        tokens_grad.astype(bf16).reshape(tokens.shape),
        gain_share,
        in_share,
        vectors[:taps],
        vectors[taps],
        small[:, wide // 2 : wide // 2 + picks],
        small[:, :rank].T,
        vectors[taps + 1],
        small[:, rank + 8 : rank + 8 + N],
        vectors[taps + 2],
        out_share,
    )


def solution(mesh):
    sharded = P("grp", "seq", None)
    shares = ("seq", "grp")
    return jax.shard_map(
        shards,
        mesh=mesh,
        in_specs=(sharded, sharded) + (P(),) * 10,
        out_specs=(
            sharded,
            sharded,
            P(shares),
            P(shares, None),
            P(None, shares),
            P(shares),
            P(shares, None),
            P(None, shares),
            P(shares),
            P(shares, None),
            P(shares),
            P(shares, None),
        ),
        check_vma=False,
    )
```

```python
import functools
import math

import jax
import jax.numpy as jnp
import ml_dtypes
import numpy as np
from jax import lax
from jax.experimental import pallas as pl
from jax.experimental.pallas import tpu as pltpu
from jax.sharding import PartitionSpec as P

f32 = jnp.float32
bf16 = jnp.bfloat16
LOG2E = 1.4426950408889634
N = 16
T = 16
WIDTH = 512
NL = WIDTH // 128
VMEM = 60 * 2**20


def lane(l):
    return slice(l * 128, (l + 1) * 128)


def sigmoid(v):
    return pltpu.reciprocal(1.0 + jnp.exp2(v * -LOG2E), approx=True)


def joined(ref, rows):
    return jnp.concatenate([ref[l, rows, :] for l in range(NL)], axis=1)


def steps_of(rows):
    return pl.ds(pl.multiple_of(rows, T), T)


def state_of(t):
    return pl.ds(pl.multiple_of(t * N, N), N)


def rows_dot(left, right):
    return lax.dot_general(left, right, (((1,), (1,)), ((), ())), preferred_element_type=f32)


def rates_of(log_ref):
    return -jnp.exp(log_ref[...])


def state_end_kernel(
    proj_ref, rw_ref, rb_ref, x_ref, log_ref, bb_ref, block_ref, dl_ref, u_ref, a2_ref, pre_ref, *, nseq, length,
):
    rows = nseq * length
    a2_ref[...] = rates_of(log_ref) * LOG2E
    low = proj_ref[:, : rw_ref.shape[0]].astype(bf16)
    pre_ref[...] = jnp.dot(low, rw_ref[...], preferred_element_type=f32) + rb_ref[...]

    def steps(i, _):
        r = pl.multiple_of(i * 64, 64)
        at = pl.ds(r, 64)
        pre = pre_ref[at, :]
        d = jnp.maximum(pre, 0.0) + jnp.log(1.0 + jnp.exp(-jnp.abs(pre)))
        for l in range(NL):
            dl_ref[l, at, :] = d[:, lane(l)]
            u_ref[l, at, :] = d[:, lane(l)] * x_ref[l, at, :].astype(f32)
        return 0

    lax.fori_loop(0, rows // 64, steps, 0)
    for s in range(nseq):
        for l in range(NL):
            span = jnp.sum(dl_ref[l, s * length : (s + 1) * length, :], axis=0, keepdims=True)
            high = span.astype(bf16).astype(f32)
            for i, v in enumerate((high, span - high)):
                at = nseq * (N + i) + s
                block_ref[at : at + 1, lane(l)] = v
    block_ref[nseq * (N + 2) :, :] = jnp.zeros((block_ref.shape[0] - nseq * (N + 2), WIDTH), f32)

    def step(c, h):
        h = [list(v) for v in h]
        for k in range(T):
            for s in range(nseq):
                t = s * length + c * T + k
                bt = bb_ref[t]
                for l in range(NL):
                    f = jnp.exp2(dl_ref[l, pl.ds(t, 1), :] * a2_ref[:, lane(l)])
                    h[s][l] = f * h[s][l] + u_ref[l, pl.ds(t, 1), :] * bt
        return tuple(tuple(v) for v in h)

    z = jnp.zeros((N, 128), f32)
    h = lax.fori_loop(0, length // T, step, ((z,) * NL,) * nseq)
    for s in range(nseq):
        for l in range(NL):
            block_ref[s * N : (s + 1) * N, lane(l)] = h[s][l]


def adjoint_end_kernel(dl_ref, g_ref, log_ref, cb_ref, sb_ref, a2_ref, *, nseq, length):
    a2_ref[...] = rates_of(log_ref) * LOG2E
    nch = length // T

    def step(m, lam):
        lam = [list(v) for v in lam]
        c = nch - 1 - m
        for k in reversed(range(T)):
            for s in range(nseq):
                t = s * length + c * T + k
                ct = cb_ref[t]
                for l in range(NL):
                    f = jnp.exp2(dl_ref[l, pl.ds(t, 1), :] * a2_ref[:, lane(l)])
                    lam[s][l] = f * (lam[s][l] + g_ref[l, pl.ds(t, 1), :] * ct)
        return tuple(tuple(v) for v in lam)

    z = jnp.zeros((N, 128), f32)
    lam = lax.fori_loop(0, nch, step, ((z,) * NL,) * nseq)
    for s in range(nseq):
        for l in range(NL):
            sb_ref[s * N : (s + 1) * N, lane(l)] = lam[s][l].astype(bf16)


def forward_kernel(
    dl_ref, u_ref, g_ref, ga_ref, gs_ref, x_ref, skip_ref, bb_ref, bc_ref, lc_ref, log_ref, hin_ref,
    hb_ref, gated_ref, ggr_ref, outg_ref, gu_ref, sk_ref, a2_ref, *, nseq, length, unroll,
):
    a2_ref[...] = rates_of(log_ref) * LOG2E
    nch = length // T
    skip = skip_ref[...]
    ones = jnp.ones((8, 128), bf16)

    @pl.when(pl.program_id(0) == 0)
    def _():
        outg_ref[...] = jnp.zeros_like(outg_ref)
        gu_ref[...] = jnp.zeros_like(gu_ref)

    def chunk(c, h, acc):
        hbv, pov = {}, [[None] * T for _ in range(nseq)]
        for k in range(T):
            for s in range(nseq):
                t = s * length + c * T + k
                bt = bb_ref[t]
                po = None
                for l in range(NL):
                    g = jnp.broadcast_to(g_ref[l, pl.ds(t, 1), :], (N, 128)).astype(bf16)
                    f = jnp.exp2(dl_ref[l, pl.ds(t, 1), :] * a2_ref[:, lane(l)])
                    held = f * h[s][l]
                    h[s][l] = held + u_ref[l, pl.ds(t, 1), :] * bt
                    hb = held.astype(bf16)
                    hb_ref[state_of(t), lane(l)] = hb
                    hbv[k, s, l] = hb
                    po = hb * g if po is None else po + hb * g
                pov[s][k] = po
        lhs = jnp.concatenate([lc_ref[steps_of(s * length + c * T), :] for s in range(nseq)], axis=0)
        parts = []
        for l in range(0, NL, 2):
            rhs = jnp.concatenate(
                [
                    jnp.concatenate([hbv[k, s, l], hbv[k, s, l + 1]], axis=1)
                    for k in range(T) for s in range(nseq)
                ],
                axis=0,
            )
            parts.append(jnp.dot(lhs, rhs, preferred_element_type=f32))
        sc_all = jnp.concatenate(parts, axis=1)
        for s in range(nseq):
            og = rows_dot(ones, jnp.concatenate(pov[s], axis=0))
            outg_ref[pl.ds(s * nch + c, 1), :] += og[:1]
            at = steps_of(s * length + c * T)
            x = joined(x_ref, at).astype(f32)
            gx = joined(g_ref, at) * x
            d = joined(dl_ref, at)
            bc = jnp.concatenate([bc_ref[at, :]] * NL, axis=1)
            mo = sc_all[s * T : (s + 1) * T] + (d * bc + skip) * x
            gu = gx * d
            gu_ref[at, :] += sum(gu[:, lane(l)] for l in range(NL))
            gated_ref[at, :] = (mo * joined(ga_ref, at)).astype(bf16)
            ggr_ref[at, :] = (mo * joined(gs_ref, at)).astype(bf16)
            acc = acc + gx
        return acc

    def step(i, carry):
        h, acc = carry
        h = [list(v) for v in h]
        for p in range(unroll):
            acc = chunk(i * unroll + p, h, acc)
        return tuple(tuple(v) for v in h), acc

    h0 = tuple(tuple(hin_ref[s, :, lane(l)] for l in range(NL)) for s in range(nseq))
    _, acc = lax.fori_loop(0, nch // unroll, step, (h0, jnp.zeros((T, WIDTH), f32)))
    sk_ref[...] = jnp.broadcast_to(jnp.sum(acc, axis=0, keepdims=True), sk_ref.shape)


def backward_kernel(
    dl_ref, u_ref, g_ref, x_ref, skip_ref, cb_ref, lb_ref, ls_ref, log_ref, lin_ref, hb_ref,
    rl_ref, cp_ref, ing_ref, dlog_ref, rb_ref, a2_ref, *, nseq, length, unroll,
):
    a2_ref[...] = rates_of(log_ref) * LOG2E
    nch = length // T
    abf = rates_of(log_ref).astype(bf16)
    skip = skip_ref[...]
    ones = jnp.ones((8, 128), bf16)

    @pl.when(pl.program_id(0) == 0)
    def _():
        ing_ref[...] = jnp.zeros_like(ing_ref)

    def chunk(c, lam, dlog, rb):
        pov = [[None] * T for _ in range(nseq)]
        dacc = [None] * NL
        vals = {}
        for k in reversed(range(T)):
            for s in range(nseq):
                t = s * length + c * T + k
                ct = cb_ref[t]
                po = None
                for l in range(NL):
                    d = jnp.broadcast_to(dl_ref[l, pl.ds(t, 1), :], (N, 128))
                    u = jnp.broadcast_to(u_ref[l, pl.ds(t, 1), :], (N, 128)).astype(bf16)
                    a = g_ref[l, pl.ds(t, 1), :] * ct + lam[s][l]
                    lam[s][l] = jnp.exp2(d * a2_ref[:, lane(l)]) * a
                    ab = a.astype(bf16)
                    q = ab * hb_ref[state_of(t), lane(l)] * abf[:, lane(l)]
                    qd = q * d.astype(bf16)
                    vals[k, s, l] = (ab, q)
                    dacc[l] = qd if dacc[l] is None else dacc[l] + qd
                    po = ab * u if po is None else po + ab * u
                pov[s][k] = po
            if k % 8 == 0:
                for l in range(NL):
                    dlog[l] = dlog[l] + dacc[l].astype(f32)
                    dacc[l] = None
        lhs = jnp.concatenate(
            [lb_ref[steps_of(s * length + c * T), :] for s in range(nseq)] + [ls_ref[...]], axis=0
        )
        parts = []
        for l in range(0, NL, 2):
            rhs = jnp.concatenate(
                [
                    jnp.concatenate([vals[k, s, l][y], vals[k, s, l + 1][y]], axis=1)
                    for k in reversed(range(T)) for s in range(nseq) for y in range(2)
                ],
                axis=0,
            )
            parts.append(jnp.dot(lhs, rhs, preferred_element_type=f32))
        both = jnp.concatenate(parts, axis=1)
        for s in range(nseq):
            w = both[s * T : (s + 1) * T]
            qs = both[(nseq + s) * T : (nseq + s + 1) * T]
            ig = rows_dot(ones, jnp.concatenate(pov[s], axis=0))
            ing_ref[pl.ds(s * nch + c, 1), :] += ig[:1]
            at = steps_of(s * length + c * T)
            d = joined(dl_ref, at)
            rg = (qs + w * joined(x_ref, at).astype(f32)) * (1.0 - jnp.exp(-d))
            rb = rb + rg
            rl_ref[at, :] = rg.astype(bf16)
            cp_ref[at, :] = w * d + skip * joined(g_ref, at)
        return rb

    def step(m, carry):
        lam, dlog, rb = carry
        lam = [list(v) for v in lam]
        dlog = list(dlog)
        for p in range(unroll):
            rb = chunk(nch - 1 - (m * unroll + p), lam, dlog, rb)
        return tuple(tuple(v) for v in lam), tuple(dlog), rb

    l0 = tuple(tuple(lin_ref[s, :, lane(l)] for l in range(NL)) for s in range(nseq))
    z = jnp.zeros((N, 128), f32)
    _, dlog, rb = lax.fori_loop(0, nch // unroll, step, (l0, (z,) * NL, jnp.zeros((T, WIDTH), f32)))
    for l in range(NL):
        dlog_ref[:, lane(l)] = dlog[l]
    rb_ref[...] = jnp.broadcast_to(jnp.sum(rb, axis=0, keepdims=True), rb_ref.shape)


def block_of(rows):
    return pl.BlockSpec((rows, WIDTH), lambda j: (0, j))


def tiles_of(rows):
    return pl.BlockSpec((NL, rows, 128), lambda j: (j, 0, 0))


def states_of(nseq):
    return pl.BlockSpec((nseq, N, WIDTH), lambda j: (0, 0, j))


def whole(a):
    return pl.BlockSpec(a.shape, lambda j: (0,) * a.ndim, pipeline_mode=pl.Buffered(1))


def kernel_call(body, name, channels, operands, specs, out_specs, outs, flops, scratch=(), **options):
    moved = sum(a.size * a.dtype.itemsize for a in operands) + sum(
        math.prod(o.shape) * o.dtype.itemsize for o in outs
    )
    return pl.pallas_call(
        functools.partial(body, **options),
        grid=(channels // WIDTH,),
        in_specs=specs,
        out_specs=out_specs,
        out_shape=outs,
        scratch_shapes=scratch,
        compiler_params=pltpu.CompilerParams(vmem_limit_bytes=VMEM, dimension_semantics=("arbitrary",)),
        cost_estimate=pl.CostEstimate(flops=flops, bytes_accessed=moved, transcendentals=0),
        name=name,
    )(*operands)


def spread(values, nseq, length, kinds, reverse):
    mask = own_column(nseq * length, length, nseq, kinds, 0, reverse)
    width = mask.shape[1]
    pick = (np.arange(width)[None, :] % N == np.arange(N)[:, None]).astype(ml_dtypes.bfloat16)
    wide = jnp.dot(values.astype(bf16), pick, preferred_element_type=f32)
    return wide.astype(bf16) * mask


def own_column(rows, length, nseq, kinds, kind, reverse):
    column = np.arange(T * nseq * kinds * N)[None, :]
    row = np.arange(rows)[:, None]
    step = column // (nseq * kinds * N)
    if reverse:
        step = T - 1 - step
    own = (step == row % T) & ((column // (kinds * N)) % nseq == row // length) & ((column // N) % kinds == kind)
    return own.astype(ml_dtypes.bfloat16)


def block_rows(nseq):
    return -(-nseq * (N + 2) // 16) * 16


def state_end(proj, rate_weight, rate_bias, x, log, bb, nseq, length):
    tiles, rows, _ = x.shape
    ch = tiles * 128
    o = jax.ShapeDtypeStruct
    return kernel_call(
        state_end_kernel, "state_end", ch,
        (proj, rate_weight, rate_bias, x, log, bb),
        [whole(proj), block_of(rate_weight.shape[0]), block_of(1), tiles_of(rows), block_of(N), whole(bb)],
        [block_of(block_rows(nseq)), tiles_of(rows), tiles_of(rows)],
        (o((block_rows(nseq), ch), f32), o(x.shape, f32), o(x.shape, f32)),
        2 * 10**10, nseq=nseq, length=length,
        scratch=[pltpu.VMEM((N, WIDTH), f32), pltpu.VMEM((rows, WIDTH), f32)],
    )


def adjoint_end(dl, g, log, cb, nseq, length):
    tiles, rows, _ = dl.shape
    ch = tiles * 128
    return kernel_call(
        adjoint_end_kernel, "adjoint_end", ch,
        (dl, g, log, cb),
        [tiles_of(rows), tiles_of(rows), block_of(N), whole(cb)],
        [block_of(nseq * N)],
        (jax.ShapeDtypeStruct((nseq * N, ch), bf16),),
        2 * 10**10, nseq=nseq, length=length, scratch=[pltpu.VMEM((N, WIDTH), f32)],
    )[0]


def forward(dl, u, g, ga, gs, x, skip, bb, bc, lc, log, hin, nseq, length, unroll=1):
    tiles, rows, _ = dl.shape
    ch = tiles * 128
    o = jax.ShapeDtypeStruct
    t = tiles_of(rows)
    return kernel_call(
        forward_kernel, "forward", ch,
        (dl, u, g, ga, gs, x, skip, bb, bc, lc, log, hin),
        [t, t, t, t, t, t, block_of(1), whole(bb), whole(bc), whole(lc), block_of(N), states_of(nseq)],
        [
            block_of(rows * N), block_of(rows), block_of(rows), pl.BlockSpec((rows // T, T * N), lambda j: (0, 0)),
            pl.BlockSpec((rows, 128), lambda j: (0, 0)), block_of(8),
        ],
        (
            o((rows * N, ch), bf16), o((rows, ch), bf16), o((rows, ch), bf16), o((rows // T, T * N), f32),
            o((rows, 128), f32), o((8, ch), f32),
        ),
        3 * 10**10, nseq=nseq, length=length, unroll=unroll, scratch=[pltpu.VMEM((N, WIDTH), f32)],
    )


def backward(dl, u, g, x, skip, cb, lb, ls, log, lin, hb, nseq, length, unroll=1):
    tiles, rows, _ = dl.shape
    ch = tiles * 128
    o = jax.ShapeDtypeStruct
    t = tiles_of(rows)
    st = states_of(nseq)
    return kernel_call(
        backward_kernel, "backward", ch,
        (dl, u, g, x, skip, cb, lb, ls, log, lin, hb),
        [t, t, t, t, block_of(1), whole(cb), whole(lb), whole(ls), block_of(N), st, block_of(rows * N)],
        [block_of(rows), block_of(rows), pl.BlockSpec((rows // T, T * N), lambda j: (0, 0)), block_of(N), block_of(8)],
        (o((rows, ch), bf16), o((rows, ch), f32), o((rows // T, T * N), f32), o((N, ch), f32), o((8, ch), f32)),
        5 * 10**10, nseq=nseq, length=length, unroll=unroll, scratch=[pltpu.VMEM((N, WIDTH), f32)],
    )


epsilon = 1e-05
ROWS = 64
PAD = 8


def normalized(tokens, gain):
    wide = tokens.astype(f32)
    return (wide * lax.rsqrt(jnp.mean(wide * wide, axis=1, keepdims=True) + epsilon) * gain).astype(bf16)


def gate_kernel(normed_ref, cot_ref, wg_ref, ow_ref, turned_ref, g_ref, ga_ref, gs_ref, gh_ref, gg_ref):
    rows = normed_ref.shape[0]

    @pl.when(pl.program_id(0) == 0)
    def _():
        turned_ref[...] = normed_ref[...].T

    gh_ref[...] = jnp.dot(normed_ref[...], wg_ref[...], preferred_element_type=f32)
    gg_ref[...] = rows_dot(cot_ref[...], ow_ref[...])

    def mix(i, _):
        at = pl.ds(pl.multiple_of(i * ROWS, ROWS), ROWS)
        gh = gh_ref[at, :]
        gg = gg_ref[at, :]
        sg = sigmoid(gh)
        ga = gh * sg
        gs = gg * (sg * (1.0 + gh * (1.0 - sg)))
        g = gg * ga
        for l in range(NL):
            g_ref[l, at, :] = g[:, lane(l)]
            ga_ref[l, at, :] = ga[:, lane(l)]
            gs_ref[l, at, :] = gs[:, lane(l)]
        return 0

    lax.fori_loop(0, rows // ROWS, mix, 0)


def gate_side(normed, cotangent, in_weight, out_weight):
    rows, model = normed.shape
    inner = out_weight.shape[0]
    first = inner // WIDTH
    tiles = jax.ShapeDtypeStruct((inner // 128, rows, 128), f32)
    return kernel_call(
        gate_kernel, "gate_side", inner,
        (normed, cotangent, in_weight, out_weight),
        [
            whole(normed), whole(cotangent), pl.BlockSpec((model, WIDTH), lambda j: (0, j + first)),
            pl.BlockSpec((WIDTH, model), lambda j: (j, 0)),
        ],
        [pl.BlockSpec((model, rows), lambda j: (0, 0))] + [tiles_of(rows)] * 3,
        (jax.ShapeDtypeStruct((model, rows), bf16), tiles, tiles, tiles),
        4 * rows * model * inner, scratch=[pltpu.VMEM((rows, WIDTH), f32)] * 2,
    )


def inner_kernel(
    tok_ref, halo_ref, gain_ref, wi_ref, cw_ref, cb_ref, sw_ref,
    normed_ref, inner_ref, before_ref, x_ref, slope_ref, proj_ref, ext_ref, flat_ref, *, nseq, length,
):
    @pl.when(pl.program_id(0) == 0)
    def _():
        def norm(i, _):
            at = pl.ds(pl.multiple_of(i * ROWS, ROWS), ROWS)
            normed_ref[at, :] = normalized(tok_ref[at, :], gain_ref[...])
            return 0

        lax.fori_loop(0, nseq * length // ROWS, norm, 0)

    part = jnp.dot(normed_ref[...], wi_ref[...], preferred_element_type=f32).astype(bf16)
    inner_ref[...] = part
    for s in range(nseq):
        for l in range(NL):
            ext_ref[s, l, PAD:, :] = part[s * length : (s + 1) * length, lane(l)].astype(f32)
    before = jnp.dot(
        normalized(halo_ref[...], gain_ref[...]), wi_ref[...], preferred_element_type=f32
    ).astype(bf16)
    before_ref[...] = before
    for s in range(nseq):
        for l in range(NL):
            ext_ref[s, l, :PAD, :] = before[s * PAD : (s + 1) * PAD, lane(l)].astype(f32)

    @pl.when(pl.program_id(0) == 0)
    def _():
        proj_ref[...] = jnp.zeros_like(proj_ref)

    taps = cw_ref.shape[0]
    for s in range(nseq):

        def mix(i, _):
            r = pl.multiple_of(i * ROWS, ROWS)
            at = pl.ds(pl.multiple_of(s * length + r, ROWS), ROWS)
            for l in range(NL):
                pre = cb_ref[:, lane(l)]
                for k in range(taps):
                    pre = pre + cw_ref[k : k + 1, lane(l)] * ext_ref[s, l, pl.ds(r + PAD - taps + 1 + k, ROWS), :]
                sg = sigmoid(pre)
                x = (pre * sg).astype(bf16)
                slope_ref[at, lane(l)] = sg * (1.0 + pre * (1.0 - sg))
                x_ref[l, at, :] = x
                flat_ref[at, lane(l)] = x
            return 0

        lax.fori_loop(0, length // ROWS, mix, 0)
    proj_ref[...] += jnp.dot(flat_ref[...], sw_ref[...], preferred_element_type=f32)


def inner_side(tokens, halo, gain, in_weight, conv_weight, conv_bias, select_weight, nseq, length):
    rows, model = tokens.shape
    inner, picks = select_weight.shape
    o = jax.ShapeDtypeStruct
    operands = (tokens, halo, gain, in_weight, conv_weight, conv_bias, select_weight)
    specs = [
        whole(tokens), whole(halo), whole(gain), block_of(model), block_of(conv_weight.shape[0]), block_of(1),
        pl.BlockSpec((WIDTH, picks), lambda j: (j, 0)),
    ]
    return pl.pallas_call(
        functools.partial(inner_kernel, nseq=nseq, length=length),
        grid=(inner // WIDTH,),
        in_specs=specs,
        out_specs=[
            pl.BlockSpec((rows, model), lambda j: (0, 0)), block_of(rows), block_of(halo.shape[0]), tiles_of(rows), block_of(rows),
            pl.BlockSpec((rows, picks), lambda j: (0, 0)),
        ],
        out_shape=(
            o((rows, model), bf16), o((rows, inner), bf16), o((halo.shape[0], inner), bf16), o((inner // 128, rows, 128), bf16),
            o((rows, inner), f32), o((rows, picks), f32),
        ),
        scratch_shapes=[pltpu.VMEM((nseq, NL, PAD + length, 128), f32), pltpu.VMEM((rows, WIDTH), bf16)],
        compiler_params=pltpu.CompilerParams(vmem_limit_bytes=VMEM, dimension_semantics=("arbitrary",)),
        cost_estimate=pl.CostEstimate(flops=2 * rows * model * inner, bytes_accessed=14 * 2**20, transcendentals=0),
        name="inner_side",
    )(*operands)


def input_grad_kernel(
    place_ref, cp_ref, inner_ref, before_ref, x_ref, slope_ref, pg_ref, sw_ref, cw_ref, turned_ref, halo_ref, gain_ref,
    rl_ref, proj_ref, dlog_ref, rb_ref, sk_ref, *refs, nseq, length, part, rank, grp, last,
):
    if last:
        early_ref, kept_ref, sent_ref, igr_ref, tail_ref, head_ref, pre_ref, back_ref, vec_ref = refs
    else:
        early_ref, (kept_ref, sent_ref, igr_ref, tail_ref, head_ref, small_ref, pre_ref, back_ref, vec_ref) = None, refs
    taps = cw_ref.shape[0]
    j = pl.program_id(0)
    wide = pg_ref.shape[1]
    back_ref[...] = cp_ref[...] + rows_dot(pg_ref[:, wide // 2 :], sw_ref[...])
    vec_ref[...] = jnp.zeros_like(vec_ref)
    small_step = 32
    for s in range(nseq):
        pre_ref[s, :, :PAD, :] = jnp.zeros((NL, PAD, 128), f32)
        pre_ref[s, :, PAD + length :, :] = jnp.zeros((NL, PAD, 128), f32)

        def first(i, total):
            r = pl.multiple_of(i * small_step, small_step)
            at = pl.ds(pl.multiple_of(s * length + r, small_step), small_step)
            back = back_ref[at, :] * slope_ref[at, :]
            for l in range(NL):
                pre_ref[s, l, pl.ds(pl.multiple_of(r + PAD, PAD), small_step), :] = back[:, lane(l)]
            return total + sum(back[q * 8 : (q + 1) * 8] for q in range(small_step // 8))

        total = lax.fori_loop(0, length // small_step, first, jnp.zeros((8, WIDTH), f32))
        vec_ref[taps : taps + 1, :] += jnp.sum(total, axis=0, keepdims=True)

        def second(i, totals):
            r = pl.multiple_of(i * small_step, small_step)
            at = pl.ds(pl.multiple_of(s * length + r, small_step), small_step)
            sums = []
            for l in range(NL):
                inner = inner_ref[at, lane(l)].astype(f32)
                result = jnp.zeros((small_step, 128), f32)
                for k in range(taps):
                    later = pre_ref[s, l, pl.ds(r + PAD + taps - 1 - k, small_step), :]
                    result = result + cw_ref[k : k + 1, lane(l)] * later
                    product = inner * later
                    sums.append(
                        totals[l * taps + k] + sum(product[q * 8 : (q + 1) * 8] for q in range(small_step // 8))
                    )
                igr_ref[at, lane(l)] = result.astype(bf16)
            return tuple(sums)

        totals = lax.fori_loop(0, length // small_step, second, (jnp.zeros((8, 128), f32),) * (taps * NL))
        head_rows = lax.broadcasted_iota(jnp.int32, (PAD, 128), 0) < taps - 1
        for l in range(NL):
            late = pre_ref[s, l, length:, :]
            tail_ref[s * PAD : (s + 1) * PAD, lane(l)] = sum(
                cw_ref[k : k + 1, lane(l)] * late[taps - 1 - k : taps - 1 - k + PAD] for k in range(taps)
            )
            lead = pre_ref[s, l, : 2 * PAD, :]
            before = before_ref[s * PAD : (s + 1) * PAD, lane(l)].astype(f32)
            before = jnp.concatenate([before[PAD - taps + 1 :], jnp.zeros((PAD - taps + 1, 128), f32)], axis=0)
            head = jnp.zeros((PAD, 128), f32)
            for k in range(taps):
                early = jnp.where(head_rows, lead[PAD - k : 2 * PAD - k], 0.0)
                head = head + cw_ref[k : k + 1, lane(l)] * early
                vec_ref[k : k + 1, lane(l)] += jnp.sum(totals[l * taps + k] + before * early, axis=0, keepdims=True)
            head_ref[s * PAD : (s + 1) * PAD, lane(l)] = head

    vec_ref[taps + 1 : taps + 2, :] = rb_ref[0:1, :]
    vec_ref[taps + 2 : taps + 3, :] = sk_ref[0:1, :]
    vec_ref[8:, :] = dlog_ref[...]
    count = place_ref.shape[0] - 1
    rows_each = turned_ref.shape[0] // count
    rows_pad = padded(rows_each)
    before_normed = normalized(halo_ref[...], gain_ref[...])
    products = []
    for b in range(WIDTH // wide):
        cols = slice(b * wide, (b + 1) * wide)
        shifted = jnp.concatenate(
            [
                jnp.concatenate(
                    [jnp.zeros((PAD - taps + 1, wide), f32), head_ref[s * PAD : s * PAD + taps - 1, cols]], axis=0
                )
                for s in range(nseq)
            ],
            axis=0,
        )
        product = jnp.dot(turned_ref[...], igr_ref[:, cols], preferred_element_type=f32) + contract_rows(
            before_normed, shifted.astype(bf16)
        )
        products.append(product.astype(bf16) if rows_each == rows_pad else product)
    eye = (
        lax.broadcasted_iota(jnp.int32, (vec_ref.shape[0], wide), 0) + rank
        == lax.broadcasted_iota(jnp.int32, (vec_ref.shape[0], wide), 1)
    ).astype(bf16)
    low = jnp.concatenate([proj_ref[...], jnp.zeros((proj_ref.shape[0], wide - proj_ref.shape[1]), f32)], axis=1)
    low = jnp.where(lax.broadcasted_iota(jnp.int32, low.shape, 1) < rank, low, 0.0).astype(bf16)
    small = (
        contract_rows(joined(x_ref, slice(None)), pg_ref[...])
        + contract_rows(rl_ref[...], low)
        + contract_rows(vec_ref[...].astype(bf16), eye)
    )
    def store(flag):
        half = count // 2
        for q in range(count):
            ref = kept_ref if (q // grp) % 2 == flag else sent_ref
            spot = lax.rem(place_ref[q], half)
            for b, product in enumerate(products):
                at = pl.ds(pl.multiple_of((j * len(products) + b) * rows_pad, rows_pad), rows_pad)
                ref[spot, at, :] = share_rows(product, q, rows_each)

    core = place_ref[count]
    for flag in range(2):
        pl.when(core == flag)(functools.partial(store, flag))
    if not last:
        small_ref[...] = small.astype(small_ref.dtype)
        return
    base = kept_ref.shape[1] - padded(part)

    def place_small(values, first):
        for q in range(WIDTH // part):
            share = place_ref[first + q]
            rows = share_rows(values, q, part)

            @pl.when(share < count // 2)
            def _():
                kept_ref[share, base : base + padded(part), :] = rows

            @pl.when(share >= count // 2)
            def _():
                sent_ref[share - count // 2, base : base + padded(part), :] = rows

    steps = pl.num_programs(0)
    place_small(early_ref[...], j * (WIDTH // part))
    place_small(small, (steps + j) * (WIDTH // part))


def input_grads(
    place, cp, inner, before, x, slope, pg, select_weight, conv_weight, turned, halo, gain, rate_low, proj,
    decay_grad, rate_bias_grad, skip_grad, early, nseq, length, part, rank, grp,
):
    rows, width = cp.shape
    width = width // 2
    last = early is not None
    first = width // WIDTH if last else 0
    wide = pg.shape[1]
    count = place.shape[0] - 1
    model = turned.shape[0]
    packed_rows = (width // wide) * padded(model // count) + (padded(part) if last else 0)
    o = jax.ShapeDtypeStruct

    def drop(spec, first=0):
        return pl.BlockSpec(
            spec.block_shape, lambda j, _, f=spec.index_map: f(j + first), pipeline_mode=spec.pipeline_mode
        )

    specs = [
        block_of(rows), block_of(rows), block_of(before.shape[0]), tiles_of(rows), block_of(rows), whole(pg),
        pl.BlockSpec((WIDTH, wide // 2), lambda j: (j, 0)), block_of(conv_weight.shape[0]), whole(turned),
        whole(halo), whole(gain), block_of(rows), whole(proj), block_of(N), block_of(8), block_of(8),
    ]
    packed = pl.BlockSpec((count // 2, packed_rows, wide), lambda j: (0, 0, 0))
    out_specs = [packed, packed, block_of(rows), block_of(nseq * PAD), block_of(nseq * PAD)]
    outs = [
        o((count // 2, packed_rows, wide), bf16), o((count // 2, packed_rows, wide), bf16), o((rows, width), bf16),
        o((nseq * PAD, width), f32), o((nseq * PAD, width), f32),
    ]
    operands = [
        place, cp, inner, before, x, slope, pg, select_weight, conv_weight, turned, halo, gain, rate_low, proj,
        decay_grad, rate_bias_grad, skip_grad,
    ]
    in_specs = [drop(s, first) for s in specs]
    block = pl.BlockSpec((WIDTH, wide), lambda j: (j, 0))
    if last:
        operands.append(early)
        in_specs.append(drop(block))
    else:
        out_specs.append(block)
        outs.append(o((width, wide), f32 if part < 16 else bf16))
    return pl.pallas_call(
        functools.partial(input_grad_kernel, nseq=nseq, length=length, part=part, rank=rank, grp=grp, last=last),
        grid_spec=pltpu.PrefetchScalarGridSpec(
            num_scalar_prefetch=1,
            grid=(width // WIDTH,),
            in_specs=in_specs,
            out_specs=[drop(s) for s in out_specs],
            scratch_shapes=[
                pltpu.VMEM((nseq, NL, PAD + length + PAD, 128), f32), pltpu.VMEM((rows, WIDTH), f32),
                pltpu.VMEM((8 + N, WIDTH), f32),
            ],
        ),
        out_shape=outs,
        compiler_params=pltpu.CompilerParams(vmem_limit_bytes=VMEM, dimension_semantics=("arbitrary",)),
        cost_estimate=pl.CostEstimate(flops=24 * rows * width * model, bytes_accessed=16 * 2**20, transcendentals=0),
        name="input_grads",
    )(*operands)


def padded(rows):
    return max(rows, 16)


def share_rows(values, share, rows):
    taken = values[share * rows : (share + 1) * rows]
    if rows < padded(rows):
        taken = jnp.concatenate([taken, jnp.zeros((padded(rows) - rows, values.shape[1]), values.dtype)], axis=0)
    return taken.astype(bf16)


def weight_grad_kernel(gated_ref, gate_ref, cot_ref, turned_ref, packed_ref, *, part):
    j = pl.program_id(0)
    count = packed_ref.shape[0]
    model = cot_ref.shape[1]
    rows_each = model // count
    rows_pad = padded(rows_each)
    product = contract_rows(gated_ref[...], cot_ref[...])
    for q in range(WIDTH // part):
        packed_ref[j * (WIDTH // part) + q, : padded(part), :] = share_rows(product, q, part)
    product = jnp.dot(turned_ref[...], gate_ref[...], preferred_element_type=f32)
    each = model // WIDTH
    at = pl.ds(pl.multiple_of(padded(part) + (j // each) * rows_pad, 16), rows_pad)
    cols = pl.ds(pl.multiple_of((j % each) * WIDTH, WIDTH), WIDTH)
    for q in range(count):
        packed_ref[q, at, cols] = share_rows(product, q, rows_each)


def weight_grads(gated, gate_grad, cot, turned, part):
    rows, width = gated.shape
    model = cot.shape[1]
    count = width // part
    packed_rows = padded(part) + (width // model) * padded(model // count)
    return pl.pallas_call(
        functools.partial(weight_grad_kernel, part=part),
        grid=(width // WIDTH,),
        in_specs=[block_of(rows), block_of(rows), whole(cot), whole(turned)],
        out_specs=pl.BlockSpec((count, packed_rows, model), lambda j: (0, 0, 0)),
        out_shape=jax.ShapeDtypeStruct((count, packed_rows, model), bf16),
        compiler_params=pltpu.CompilerParams(vmem_limit_bytes=VMEM, dimension_semantics=("arbitrary",)),
        cost_estimate=pl.CostEstimate(flops=4 * rows * width * model, bytes_accessed=14 * 2**20, transcendentals=0),
        name="weight_grads",
    )(gated, gate_grad, cot, turned)


def share_kernel(*refs, count, rank, taps, part, part_rows, picks):
    first, second = refs[:count], refs[count : 2 * count]
    summed_ref, weight_ref, gain_ref = refs[2 * count : 2 * count + 3]
    in_ref, out_ref, conv_ref, bias_ref, select_ref, rate_ref, rate_bias_ref, decay_ref, skip_ref, norm_ref = refs[
        2 * count + 3 :
    ]
    pad = padded(part_rows)
    wide = first[0].shape[2]
    model = summed_ref.shape[1]
    each = first[0].shape[1] // pad

    def total(held, at, rows):
        return sum(h[0, at : at + rows, :].astype(f32) for h in held)

    for half, held in enumerate((first, second)):
        for b in range(each):
            at = (half * each + b) * wide
            in_ref[:, at : at + wide] = total(held, b * pad, pad)[:part_rows]
    gate_at = 2 * each * wide
    for b in range((in_ref.shape[1] - gate_at) // model):
        at = padded(part) + b * pad
        in_ref[:, gate_at + b * model : gate_at + (b + 1) * model] = summed_ref[at : at + pad, :][:part_rows].astype(f32)
    out_ref[...] = summed_ref[: padded(part), :][:part].astype(f32)
    gain = jnp.sum(weight_ref[...].astype(f32) * in_ref[...], axis=1, keepdims=True)
    gain = jnp.broadcast_to(gain, (part_rows, 128))
    if part_rows < 8:
        gain = jnp.concatenate([gain, jnp.zeros((8 - part_rows, 128), f32)], axis=0)
    norm_ref[...] = gain.T[:1, :part_rows] / gain_ref[...]
    small = total(second, each * pad, padded(part))[:part]
    turned = small[:, : wide // 2].T
    rate_ref[...] = turned[:rank]
    conv_ref[...] = turned[rank : rank + taps]
    bias_ref[...] = turned[rank + taps : rank + taps + 1]
    rate_bias_ref[...] = turned[rank + taps + 1 : rank + taps + 2]
    skip_ref[...] = turned[rank + taps + 2 : rank + taps + 3]
    decay_ref[...] = turned[rank + 8 : rank + 8 + N].T
    select_ref[...] = small[:, wide // 2 : wide // 2 + picks]


def shares_of(first, second, summed, own_weight, own_gain, rank, taps, part, picks):
    part_rows, width = own_weight.shape
    model = summed.shape[1]
    o = lambda *shape: jax.ShapeDtypeStruct(shape, f32)
    return pl.pallas_call(
        functools.partial(
            share_kernel, count=len(first), rank=rank, taps=taps, part=part, part_rows=part_rows, picks=picks
        ),
        out_shape=(
            o(part_rows, width), o(part, model), o(taps, part), o(1, part), o(part, picks), o(rank, part), o(1, part),
            o(part, N), o(1, part), o(1, part_rows),
        ),
        compiler_params=pltpu.CompilerParams(vmem_limit_bytes=VMEM),
        name="shares",
    )(*first, *second, summed, own_weight, own_gain)


def flip_bit(axis, bit):
    return [(i, i ^ bit) for i in range(lax.axis_size(axis))]


def bits_of(axis):
    size = lax.axis_size(axis)
    return [(axis, 1 << k) for k in range(size.bit_length() - 1)]


def places(order):
    grp = lax.axis_size("grp")
    other = jnp.arange(lax.axis_size("seq") * grp) ^ (lax.axis_index("seq") * grp + lax.axis_index("grp"))
    position = jnp.zeros_like(other)
    for axis, bit in order:
        position = 2 * position + (other // (bit * grp if axis == "seq" else bit)) % 2
    return position.astype(jnp.int32)


def pairs_of(bits):
    return [bits[i : i + 2] for i in range(0, len(bits), 2)]


def round_parts(held, bits):
    count = 1 << len(bits)
    size = held[0].shape[0] // count
    parts = [sum(h[i * size : (i + 1) * size].astype(f32) for h in held) for i in range(count)]
    return parts[:1] + [part.astype(bf16) for part in parts[1:]]


def round_trade(parts, bits):
    held = parts[:1]
    for i in range(1, len(parts)):
        flip = sum(bit for at, (axis, bit) in enumerate(bits) if (i >> (len(bits) - 1 - at)) & 1)
        held.append(lax.ppermute(parts[i], bits[0][0], flip_bit(bits[0][0], flip)))
    return held


def sum_packed(kept, sent, rounds, later):
    axis, bit = rounds[0][0]
    held = [kept, lax.ppermute(sent, axis, flip_bit(axis, bit))]
    for bits in rounds[1:]:
        parts = round_parts(held, bits)
        if later is not None:
            *parts, later = lax.optimization_barrier((*parts, later))
        held = round_trade(parts, bits)
    return held, later


def remaining_rounds(held, rounds, later):
    for bits in rounds:
        parts = round_parts(held, bits)
        if later is not None and bits is rounds[-1]:
            *parts, later = lax.optimization_barrier((*parts, later))
        held = round_trade(parts, bits)
    return held, later


def carried(block, shape, rates, backward, after=None, spans=None):
    count, mine = lax.axis_size("seq"), lax.axis_index("seq")
    blocks = lax.all_gather(block.astype(bf16), "seq")
    if after is not None:
        blocks, after = lax.optimization_barrier((blocks, after))
    rows = shape[0] * shape[1]
    entering = jnp.zeros(shape, f32)
    for turn in range(count - 1):
        j = count - 1 - turn if backward else turn
        theirs = blocks[j].astype(f32)
        span = (theirs if spans is None else spans[j].astype(f32))[rows : rows + 2 * shape[0]]
        span = span[: shape[0]] + span[shape[0] :]
        longer = jnp.exp(span[:, None, :] * rates) * entering + theirs[:rows].reshape(shape)
        entering = jnp.where(mine < j if backward else j < mine, longer, entering)
    return entering, after, blocks


def contract_rows(left, right, kind=f32):
    return lax.dot_general(left, right, (((0,), (0,)), ((), ())), preferred_element_type=f32).astype(kind)


def shards(
    tokens,
    cotangent,
    norm_gain,
    in_weight,
    conv_weight,
    conv_bias,
    select_weight,
    rate_weight,
    rate_bias,
    decay_log,
    skip_gain,
    out_weight,
):
    nseq, length, model = tokens.shape
    inner_width = out_weight.shape[0]
    rank = rate_weight.shape[0]
    taps = conv_weight.shape[0]
    rows = nseq * length
    share_count = lax.axis_size("seq") * lax.axis_size("grp")
    tok = tokens.reshape(rows, model)
    cot = cotangent.reshape(rows, model)
    gain, skip, bias = norm_gain[None], skip_gain[None], conv_bias[None]
    pieces, grp = lax.axis_size("seq"), lax.axis_size("grp")
    halo = lax.ppermute(tokens[:, length - PAD :], "seq", [(i, i + 1) for i in range(pieces - 1)])
    halo = halo.reshape(nseq * PAD, model)
    picks, wide = rank + 2 * N, 256
    select_weight = jnp.pad(select_weight, ((0, 0), (0, wide // 2 - picks)))
    normed, inner, before, x, slope, proj = inner_side(
        tok, halo, gain, in_weight, conv_weight, bias, select_weight, nseq, length
    )
    in_gate, out_gate = proj[:, rank : rank + N], proj[:, rank + N : picks]
    log = decay_log.T
    rates = -jnp.exp(log)
    bb = jnp.broadcast_to(in_gate[:, :, None], (rows, N, 128))
    ahead, dl, u = state_end(proj, rate_weight, rate_bias[None], x, log, bb, nseq, length)
    ahead, cot = lax.optimization_barrier((ahead.astype(bf16), cot))
    turned, g, ga, gs = gate_side(normed, cot, in_weight, out_weight)
    state_shape = (nseq, N, inner_width)
    entering, _, spans = carried(ahead, state_shape, rates, False)
    cb = jnp.broadcast_to(out_gate[:, :, None], (rows, N, 128))
    sent_back = adjoint_end(dl, g, log, cb, nseq, length)
    lc = spread(out_gate, nseq, length, 1, False)
    lb = spread(in_gate, nseq, length, 2, True)
    ls = jnp.asarray(own_column(nseq * T, T, nseq, 2, 1, True))
    meet = jnp.sum(in_gate * out_gate, axis=1, keepdims=True)
    bc = jnp.broadcast_to(meet, (rows, 128))
    behind, lb, ls, u = lax.optimization_barrier((sent_back, lb, ls, u))
    states, gated, gate_grad, out_grad, shift, skip_grad = forward(
        dl, u, g, ga, gs, x, skip, bb, bc, lc, log, entering, nseq, length, 4
    )
    part, part_rows = inner_width // share_count, model // share_count
    weight_packed = weight_grads(gated, gate_grad, cot, turned, part)
    leaving, weight_packed, _ = carried(behind, state_shape, rates, True, weight_packed, spans)
    weight_sum = lax.psum_scatter(weight_packed, "seq", scatter_dimension=0, tiled=True)
    rate_low, conv_part, in_grad, decay_grad, rate_bias_grad = backward(
        dl, u, g, x, skip, cb, lb, ls, log, leaving, states, nseq, length, 4
    )
    out_grad = out_grad.reshape(rows, N) + in_gate * jnp.sum(shift, axis=1, keepdims=True)
    rank_grad = rows_dot(rate_low, rate_weight)
    pg = jnp.concatenate(
        [
            jnp.zeros((rows, wide // 2), bf16),
            rank_grad.astype(bf16),
            in_grad.reshape(rows, N).astype(bf16),
            out_grad.astype(bf16),
            jnp.zeros((rows, wide // 2 - picks), bf16),
        ],
        axis=1,
    )
    seq_bits, grp_bits = bits_of("seq"), bits_of("grp")
    order = seq_bits + grp_bits
    place = jnp.concatenate([places(order), (lax.axis_index("seq") % 2)[None].astype(jnp.int32)])
    rounds = [seq_bits[:1]] + pairs_of(seq_bits[1:]) + pairs_of(grp_bits)
    half_width = inner_width // 2

    def half(conv_part, early):
        return input_grads(
            place, conv_part, inner, before, x, slope, pg, select_weight, conv_weight, turned, halo, gain, rate_low,
            proj, decay_grad, rate_bias_grad, skip_grad, early, nseq, length, part, rank, grp,
        )

    kept, sent, first_grad, first_tail, first_head, early = half(conv_part, None)
    sent, gated = lax.optimization_barrier((sent, gated))
    wide_tok = tok.astype(f32)
    block_out = wide_tok + jnp.dot(gated, out_weight, preferred_element_type=f32)
    first_held, (conv_part, block_out) = sum_packed(kept, sent, rounds[:2], (conv_part, block_out))
    kept, sent, second_grad, second_tail, second_head = half(conv_part, early)
    head = jnp.concatenate([first_head, second_head], axis=1)
    *first_held, sent, head, weight_sum = lax.optimization_barrier((*first_held, sent, head, weight_sum))
    head = head.reshape(nseq, PAD, inner_width)[:, : taps - 1].astype(bf16)
    returned = lax.ppermute(head, "seq", [(i + 1, i) for i in range(pieces - 1)]).astype(f32)
    held, (gate_grad, *first_held) = sum_packed(kept, sent, rounds[:2], (gate_grad, *first_held))
    normed_grad = rows_dot(gate_grad, in_weight[:, inner_width:])
    *first_held, normed_grad = lax.optimization_barrier((*first_held, normed_grad))
    first_held, _ = remaining_rounds(first_held, rounds[2:], None)
    held, (returned, second_grad, normed_grad) = remaining_rounds(
        held, rounds[2:], (returned, second_grad, normed_grad)
    )
    weight_share = lax.psum_scatter(weight_sum, "grp", scatter_dimension=0, tiled=True)[0]
    first = (lax.axis_index("seq") * grp + lax.axis_index("grp")) * part_rows
    own_weight = lax.dynamic_slice_in_dim(in_weight, first, part_rows, 0)
    own_gain = lax.dynamic_slice_in_dim(norm_gain, first, part_rows, 0)[None]
    in_share, out_share, conv_share, bias_share, select_share, rate_share, rate_bias_share, decay_share, skip_share, (
        gain_share
    ) = shares_of(first_held, held, weight_share, own_weight, own_gain, rank, taps, part, picks)
    tail = jnp.concatenate([first_tail, second_tail], axis=1)
    fixed = (tail.reshape(nseq, PAD, inner_width)[:, PAD - taps + 1 :] + returned).astype(bf16)

    def patched(grad, at):
        rows_of = grad.reshape(nseq, length, half_width)
        rows_of = rows_of.at[:, length - taps + 1 :].set(fixed[:, :, at : at + half_width])
        return rows_of.reshape(rows, half_width)

    normed_grad = (
        normed_grad
        + rows_dot(patched(first_grad, 0), in_weight[:, :half_width])
        + rows_dot(patched(second_grad, half_width), in_weight[:, half_width:inner_width])
    )
    scale = lax.rsqrt(jnp.mean(wide_tok * wide_tok, axis=1, keepdims=True) + epsilon)
    lifted = normed_grad * norm_gain
    dots = jnp.mean(lifted * wide_tok, axis=1, keepdims=True)
    tokens_grad = cot.astype(f32) + scale * lifted - wide_tok * (scale * scale * scale) * dots
    return (
        block_out.astype(bf16).reshape(tokens.shape),
        tokens_grad.astype(bf16).reshape(tokens.shape),
        gain_share[0],
        in_share,
        conv_share,
        bias_share[0],
        select_share,
        rate_share,
        rate_bias_share[0],
        decay_share,
        skip_share[0],
        out_share,
    )


def solution(mesh):
    sharded = P("grp", "seq", None)
    shares = ("seq", "grp")
    return jax.shard_map(
        shards,
        mesh=mesh,
        in_specs=(sharded, sharded) + (P(),) * 10,
        out_specs=(
            sharded,
            sharded,
            P(shares),
            P(shares, None),
            P(None, shares),
            P(shares),
            P(shares, None),
            P(None, shares),
            P(shares),
            P(shares, None),
            P(shares),
            P(shares, None),
        ),
        check_vma=False,
    )
```

```python
import functools
import math

import jax
import jax.numpy as jnp
import ml_dtypes
import numpy as np
from jax import lax
from jax.experimental import pallas as pl
from jax.experimental.pallas import tpu as pltpu
from jax.sharding import PartitionSpec as P

f32 = jnp.float32
bf16 = jnp.bfloat16
LOG2E = 1.4426950408889634
N = 16
T = 16
WIDTH = 512
NL = WIDTH // 128
VMEM = 60 * 2**20


def lane(l):
    return slice(l * 128, (l + 1) * 128)


def sigmoid(v):
    return pltpu.reciprocal(1.0 + jnp.exp2(v * -LOG2E), approx=True)


def joined(ref, rows):
    return jnp.concatenate([ref[l, rows, :] for l in range(NL)], axis=1)


def steps_of(rows):
    return pl.ds(pl.multiple_of(rows, T), T)


def state_of(t):
    return pl.ds(pl.multiple_of(t * N, N), N)


def rows_dot(left, right):
    return lax.dot_general(left, right, (((1,), (1,)), ((), ())), preferred_element_type=f32)


def rates_of(log_ref):
    return -jnp.exp(log_ref[...])


def state_end_kernel(
    proj_ref, rw_ref, rb_ref, x_ref, log_ref, bb_ref, block_ref, dl_ref, u_ref, a2_ref, pre_ref, *, nseq, length,
):
    rows = nseq * length
    a2_ref[...] = rates_of(log_ref) * LOG2E
    low = proj_ref[:, : rw_ref.shape[0]].astype(bf16)
    pre_ref[...] = jnp.dot(low, rw_ref[...], preferred_element_type=f32) + rb_ref[...]

    def steps(i, _):
        r = pl.multiple_of(i * 64, 64)
        at = pl.ds(r, 64)
        pre = pre_ref[at, :]
        d = jnp.maximum(pre, 0.0) + jnp.log(1.0 + jnp.exp(-jnp.abs(pre)))
        for l in range(NL):
            dl_ref[l, at, :] = d[:, lane(l)]
            u_ref[l, at, :] = d[:, lane(l)] * x_ref[l, at, :].astype(f32)
        return 0

    lax.fori_loop(0, rows // 64, steps, 0)
    fill = block_ref.shape[0] - nseq * (N + 2)
    for l in range(NL):
        spans = [
            jnp.sum(dl_ref[l, s * length : (s + 1) * length, :], axis=0, keepdims=True) for s in range(nseq)
        ]
        highs = [span.astype(bf16).astype(f32) for span in spans]
        lows = [span - high for span, high in zip(spans, highs)]
        rows_of = jnp.concatenate(highs + lows + [jnp.zeros((fill, 128), f32)], axis=0)
        block_ref[nseq * N :, lane(l)] = rows_of.astype(bf16)

    def step(c, h):
        h = [list(v) for v in h]
        for k in range(T):
            for s in range(nseq):
                t = s * length + c * T + k
                bt = bb_ref[t]
                for l in range(NL):
                    f = jnp.exp2(dl_ref[l, pl.ds(t, 1), :] * a2_ref[:, lane(l)])
                    h[s][l] = f * h[s][l] + u_ref[l, pl.ds(t, 1), :] * bt
        return tuple(tuple(v) for v in h)

    z = jnp.zeros((N, 128), f32)
    h = lax.fori_loop(0, length // T, step, ((z,) * NL,) * nseq)
    for s in range(nseq):
        for l in range(NL):
            block_ref[s * N : (s + 1) * N, lane(l)] = h[s][l].astype(bf16)


def adjoint_end_kernel(dl_ref, g_ref, log_ref, cb_ref, sb_ref, a2_ref, *, nseq, length):
    a2_ref[...] = rates_of(log_ref) * LOG2E
    nch = length // T

    def step(m, lam):
        lam = [list(v) for v in lam]
        c = nch - 1 - m
        for k in reversed(range(T)):
            for s in range(nseq):
                t = s * length + c * T + k
                ct = cb_ref[t]
                for l in range(NL):
                    f = jnp.exp2(dl_ref[l, pl.ds(t, 1), :] * a2_ref[:, lane(l)])
                    lam[s][l] = f * (lam[s][l] + g_ref[l, pl.ds(t, 1), :] * ct)
        return tuple(tuple(v) for v in lam)

    z = jnp.zeros((N, 128), f32)
    lam = lax.fori_loop(0, nch, step, ((z,) * NL,) * nseq)
    for s in range(nseq):
        for l in range(NL):
            sb_ref[s * N : (s + 1) * N, lane(l)] = lam[s][l].astype(bf16)


def forward_kernel(
    dl_ref, u_ref, g_ref, ga_ref, gs_ref, x_ref, skip_ref, bb_ref, bc_ref, lc_ref, log_ref, hin_ref,
    hb_ref, gated_ref, ggr_ref, outg_ref, gu_ref, sk_ref, a2_ref, *, nseq, length, unroll,
):
    a2_ref[...] = rates_of(log_ref) * LOG2E
    nch = length // T
    skip = skip_ref[...]
    ones = jnp.ones((8, 128), bf16)

    @pl.when(pl.program_id(0) == 0)
    def _():
        outg_ref[...] = jnp.zeros_like(outg_ref)
        gu_ref[...] = jnp.zeros_like(gu_ref)

    def chunk(c, h, acc):
        hbv, pov = {}, [[None] * T for _ in range(nseq)]
        for k in range(T):
            for s in range(nseq):
                t = s * length + c * T + k
                bt = bb_ref[t]
                po = None
                for l in range(NL):
                    g = jnp.broadcast_to(g_ref[l, pl.ds(t, 1), :], (N, 128)).astype(bf16)
                    f = jnp.exp2(dl_ref[l, pl.ds(t, 1), :] * a2_ref[:, lane(l)])
                    held = f * h[s][l]
                    h[s][l] = held + u_ref[l, pl.ds(t, 1), :] * bt
                    hb = held.astype(bf16)
                    hb_ref[state_of(t), lane(l)] = hb
                    hbv[k, s, l] = hb
                    po = hb * g if po is None else po + hb * g
                pov[s][k] = po
        lhs = jnp.concatenate([lc_ref[steps_of(s * length + c * T), :] for s in range(nseq)], axis=0)
        parts = []
        for l in range(0, NL, 2):
            rhs = jnp.concatenate(
                [
                    jnp.concatenate([hbv[k, s, l], hbv[k, s, l + 1]], axis=1)
                    for k in range(T) for s in range(nseq)
                ],
                axis=0,
            )
            parts.append(jnp.dot(lhs, rhs, preferred_element_type=f32))
        sc_all = jnp.concatenate(parts, axis=1)
        for s in range(nseq):
            og = rows_dot(ones, jnp.concatenate(pov[s], axis=0))
            outg_ref[pl.ds(s * nch + c, 1), :] += og[:1]
            at = steps_of(s * length + c * T)
            x = joined(x_ref, at).astype(f32)
            gx = joined(g_ref, at) * x
            d = joined(dl_ref, at)
            bc = jnp.concatenate([bc_ref[at, :]] * NL, axis=1)
            mo = sc_all[s * T : (s + 1) * T] + (d * bc + skip) * x
            gu = gx * d
            gu_ref[at, :] += sum(gu[:, lane(l)] for l in range(NL))
            gated_ref[at, :] = (mo * joined(ga_ref, at)).astype(bf16)
            ggr_ref[at, :] = (mo * joined(gs_ref, at)).astype(bf16)
            acc = acc + gx
        return acc

    def step(i, carry):
        h, acc = carry
        h = [list(v) for v in h]
        for p in range(unroll):
            acc = chunk(i * unroll + p, h, acc)
        return tuple(tuple(v) for v in h), acc

    h0 = tuple(tuple(hin_ref[s, :, lane(l)] for l in range(NL)) for s in range(nseq))
    _, acc = lax.fori_loop(0, nch // unroll, step, (h0, jnp.zeros((T, WIDTH), f32)))
    sk_ref[...] = jnp.broadcast_to(jnp.sum(acc, axis=0, keepdims=True), sk_ref.shape)


def backward_kernel(
    dl_ref, u_ref, g_ref, x_ref, skip_ref, cb_ref, lb_ref, ls_ref, log_ref, lin_ref, hb_ref,
    rl_ref, cp_ref, ing_ref, dlog_ref, rb_ref, a2_ref, *, nseq, length, unroll,
):
    a2_ref[...] = rates_of(log_ref) * LOG2E
    nch = length // T
    abf = rates_of(log_ref).astype(bf16)
    skip = skip_ref[...]
    ones = jnp.ones((8, 128), bf16)

    @pl.when(pl.program_id(0) == 0)
    def _():
        ing_ref[...] = jnp.zeros_like(ing_ref)

    def chunk(c, lam, dlog, rb):
        pov = [[None] * T for _ in range(nseq)]
        dacc = [None] * NL
        vals = {}
        for k in reversed(range(T)):
            for s in range(nseq):
                t = s * length + c * T + k
                ct = cb_ref[t]
                po = None
                for l in range(NL):
                    d = jnp.broadcast_to(dl_ref[l, pl.ds(t, 1), :], (N, 128))
                    u = jnp.broadcast_to(u_ref[l, pl.ds(t, 1), :], (N, 128)).astype(bf16)
                    a = g_ref[l, pl.ds(t, 1), :] * ct + lam[s][l]
                    lam[s][l] = jnp.exp2(d * a2_ref[:, lane(l)]) * a
                    ab = a.astype(bf16)
                    q = ab * hb_ref[state_of(t), lane(l)] * abf[:, lane(l)]
                    qd = q * d.astype(bf16)
                    vals[k, s, l] = (ab, q)
                    dacc[l] = qd if dacc[l] is None else dacc[l] + qd
                    po = ab * u if po is None else po + ab * u
                pov[s][k] = po
            if k % 8 == 0:
                for l in range(NL):
                    dlog[l] = dlog[l] + dacc[l].astype(f32)
                    dacc[l] = None
        lhs = jnp.concatenate(
            [lb_ref[steps_of(s * length + c * T), :] for s in range(nseq)] + [ls_ref[...]], axis=0
        )
        parts = []
        for l in range(0, NL, 2):
            rhs = jnp.concatenate(
                [
                    jnp.concatenate([vals[k, s, l][y], vals[k, s, l + 1][y]], axis=1)
                    for k in reversed(range(T)) for s in range(nseq) for y in range(2)
                ],
                axis=0,
            )
            parts.append(jnp.dot(lhs, rhs, preferred_element_type=f32))
        both = jnp.concatenate(parts, axis=1)
        for s in range(nseq):
            w = both[s * T : (s + 1) * T]
            qs = both[(nseq + s) * T : (nseq + s + 1) * T]
            ig = rows_dot(ones, jnp.concatenate(pov[s], axis=0))
            ing_ref[pl.ds(s * nch + c, 1), :] += ig[:1]
            at = steps_of(s * length + c * T)
            d = joined(dl_ref, at)
            rg = (qs + w * joined(x_ref, at).astype(f32)) * (1.0 - jnp.exp(-d))
            rb = rb + rg
            rl_ref[at, :] = rg.astype(bf16)
            cp_ref[at, :] = w * d + skip * joined(g_ref, at)
        return rb

    def step(m, carry):
        lam, dlog, rb = carry
        lam = [list(v) for v in lam]
        dlog = list(dlog)
        for p in range(unroll):
            rb = chunk(nch - 1 - (m * unroll + p), lam, dlog, rb)
        return tuple(tuple(v) for v in lam), tuple(dlog), rb

    l0 = tuple(tuple(lin_ref[s, :, lane(l)] for l in range(NL)) for s in range(nseq))
    z = jnp.zeros((N, 128), f32)
    _, dlog, rb = lax.fori_loop(0, nch // unroll, step, (l0, (z,) * NL, jnp.zeros((T, WIDTH), f32)))
    for l in range(NL):
        dlog_ref[:, lane(l)] = dlog[l]
    rb_ref[...] = jnp.broadcast_to(jnp.sum(rb, axis=0, keepdims=True), rb_ref.shape)


def block_of(rows):
    return pl.BlockSpec((rows, WIDTH), lambda j: (0, j))


def tiles_of(rows):
    return pl.BlockSpec((NL, rows, 128), lambda j: (j, 0, 0))


def states_of(nseq):
    return pl.BlockSpec((nseq, N, WIDTH), lambda j: (0, 0, j))


def whole(a):
    return pl.BlockSpec(a.shape, lambda j: (0,) * a.ndim, pipeline_mode=pl.Buffered(1))


def kernel_call(body, name, channels, operands, specs, out_specs, outs, flops, scratch=(), **options):
    moved = sum(a.size * a.dtype.itemsize for a in operands) + sum(
        math.prod(o.shape) * o.dtype.itemsize for o in outs
    )
    return pl.pallas_call(
        functools.partial(body, **options),
        grid=(channels // WIDTH,),
        in_specs=specs,
        out_specs=out_specs,
        out_shape=outs,
        scratch_shapes=scratch,
        compiler_params=pltpu.CompilerParams(vmem_limit_bytes=VMEM, dimension_semantics=("arbitrary",)),
        cost_estimate=pl.CostEstimate(flops=flops, bytes_accessed=moved, transcendentals=0),
        name=name,
    )(*operands)


def spread(values, nseq, length, kinds, reverse):
    mask = own_column(nseq * length, length, nseq, kinds, 0, reverse)
    width = mask.shape[1]
    pick = (np.arange(width)[None, :] % N == np.arange(N)[:, None]).astype(ml_dtypes.bfloat16)
    wide = jnp.dot(values.astype(bf16), pick, preferred_element_type=f32)
    return wide.astype(bf16) * mask


def own_column(rows, length, nseq, kinds, kind, reverse):
    column = np.arange(T * nseq * kinds * N)[None, :]
    row = np.arange(rows)[:, None]
    step = column // (nseq * kinds * N)
    if reverse:
        step = T - 1 - step
    own = (step == row % T) & ((column // (kinds * N)) % nseq == row // length) & ((column // N) % kinds == kind)
    return own.astype(ml_dtypes.bfloat16)


def block_rows(nseq):
    return -(-nseq * (N + 2) // 16) * 16


def state_end(proj, rate_weight, rate_bias, x, log, bb, nseq, length):
    tiles, rows, _ = x.shape
    ch = tiles * 128
    o = jax.ShapeDtypeStruct
    return kernel_call(
        state_end_kernel, "state_end", ch,
        (proj, rate_weight, rate_bias, x, log, bb),
        [whole(proj), block_of(rate_weight.shape[0]), block_of(1), tiles_of(rows), block_of(N), whole(bb)],
        [block_of(block_rows(nseq)), tiles_of(rows), tiles_of(rows)],
        (o((block_rows(nseq), ch), bf16), o(x.shape, f32), o(x.shape, f32)),
        2 * 10**10, nseq=nseq, length=length,
        scratch=[pltpu.VMEM((N, WIDTH), f32), pltpu.VMEM((rows, WIDTH), f32)],
    )


def adjoint_end(dl, g, log, cb, nseq, length):
    tiles, rows, _ = dl.shape
    ch = tiles * 128
    return kernel_call(
        adjoint_end_kernel, "adjoint_end", ch,
        (dl, g, log, cb),
        [tiles_of(rows), tiles_of(rows), block_of(N), whole(cb)],
        [block_of(nseq * N)],
        (jax.ShapeDtypeStruct((nseq * N, ch), bf16),),
        2 * 10**10, nseq=nseq, length=length, scratch=[pltpu.VMEM((N, WIDTH), f32)],
    )[0]


def forward(dl, u, g, ga, gs, x, skip, bb, bc, lc, log, hin, nseq, length, unroll=1):
    tiles, rows, _ = dl.shape
    ch = tiles * 128
    o = jax.ShapeDtypeStruct
    t = tiles_of(rows)
    return kernel_call(
        forward_kernel, "forward", ch,
        (dl, u, g, ga, gs, x, skip, bb, bc, lc, log, hin),
        [t, t, t, t, t, t, block_of(1), whole(bb), whole(bc), whole(lc), block_of(N), states_of(nseq)],
        [
            block_of(rows * N), block_of(rows), block_of(rows), pl.BlockSpec((rows // T, T * N), lambda j: (0, 0)),
            pl.BlockSpec((rows, 128), lambda j: (0, 0)), block_of(8),
        ],
        (
            o((rows * N, ch), bf16), o((rows, ch), bf16), o((rows, ch), bf16), o((rows // T, T * N), f32),
            o((rows, 128), f32), o((8, ch), f32),
        ),
        3 * 10**10, nseq=nseq, length=length, unroll=unroll, scratch=[pltpu.VMEM((N, WIDTH), f32)],
    )


def backward(dl, u, g, x, skip, cb, lb, ls, log, lin, hb, nseq, length, unroll=1):
    tiles, rows, _ = dl.shape
    ch = tiles * 128
    o = jax.ShapeDtypeStruct
    t = tiles_of(rows)
    st = states_of(nseq)
    return kernel_call(
        backward_kernel, "backward", ch,
        (dl, u, g, x, skip, cb, lb, ls, log, lin, hb),
        [t, t, t, t, block_of(1), whole(cb), whole(lb), whole(ls), block_of(N), st, block_of(rows * N)],
        [block_of(rows), block_of(rows), pl.BlockSpec((rows // T, T * N), lambda j: (0, 0)), block_of(N), block_of(8)],
        (o((rows, ch), bf16), o((rows, ch), f32), o((rows // T, T * N), f32), o((N, ch), f32), o((8, ch), f32)),
        5 * 10**10, nseq=nseq, length=length, unroll=unroll, scratch=[pltpu.VMEM((N, WIDTH), f32)],
    )


epsilon = 1e-05
ROWS = 64
PAD = 8


def normalized(tokens, gain):
    wide = tokens.astype(f32)
    return (wide * lax.rsqrt(jnp.mean(wide * wide, axis=1, keepdims=True) + epsilon) * gain).astype(bf16)


def gate_kernel(normed_ref, cot_ref, wg_ref, ow_ref, turned_ref, g_ref, ga_ref, gs_ref, gh_ref, gg_ref):
    rows = normed_ref.shape[0]

    @pl.when(pl.program_id(0) == 0)
    def _():
        turned_ref[...] = normed_ref[...].T

    gh_ref[...] = jnp.dot(normed_ref[...], wg_ref[...], preferred_element_type=f32)
    gg_ref[...] = rows_dot(cot_ref[...], ow_ref[...])

    def mix(i, _):
        at = pl.ds(pl.multiple_of(i * ROWS, ROWS), ROWS)
        gh = gh_ref[at, :]
        gg = gg_ref[at, :]
        sg = sigmoid(gh)
        ga = gh * sg
        gs = gg * (sg * (1.0 + gh * (1.0 - sg)))
        g = gg * ga
        for l in range(NL):
            g_ref[l, at, :] = g[:, lane(l)]
            ga_ref[l, at, :] = ga[:, lane(l)]
            gs_ref[l, at, :] = gs[:, lane(l)]
        return 0

    lax.fori_loop(0, rows // ROWS, mix, 0)


def gate_side(normed, cotangent, in_weight, out_weight):
    rows, model = normed.shape
    inner = out_weight.shape[0]
    first = inner // WIDTH
    tiles = jax.ShapeDtypeStruct((inner // 128, rows, 128), f32)
    return kernel_call(
        gate_kernel, "gate_side", inner,
        (normed, cotangent, in_weight, out_weight),
        [
            whole(normed), whole(cotangent), pl.BlockSpec((model, WIDTH), lambda j: (0, j + first)),
            pl.BlockSpec((WIDTH, model), lambda j: (j, 0)),
        ],
        [pl.BlockSpec((model, rows), lambda j: (0, 0))] + [tiles_of(rows)] * 3,
        (jax.ShapeDtypeStruct((model, rows), bf16), tiles, tiles, tiles),
        4 * rows * model * inner, scratch=[pltpu.VMEM((rows, WIDTH), f32)] * 2,
    )


def filled(weight):
    return jnp.concatenate([weight, jnp.zeros((128 - weight.shape[0], weight.shape[1]), weight.dtype)], axis=0)


def inner_kernel(
    tok_ref, halo_ref, gain_ref, wi_ref, cw_ref, cb_ref, sw_ref,
    normed_ref, inner_ref, before_ref, x_ref, slope_ref, proj_ref, meet_ref, ext_ref, flat_ref, *, nseq, length, rank,
):
    @pl.when(pl.program_id(0) == 0)
    def _():
        def norm(i, _):
            at = pl.ds(pl.multiple_of(i * ROWS, ROWS), ROWS)
            normed_ref[at, :] = normalized(tok_ref[at, :], gain_ref[...])
            return 0

        lax.fori_loop(0, nseq * length // ROWS, norm, 0)

    part = jnp.dot(normed_ref[...], wi_ref[...], preferred_element_type=f32).astype(bf16)
    inner_ref[...] = part
    for s in range(nseq):
        for l in range(NL):
            ext_ref[s, l, PAD:, :] = part[s * length : (s + 1) * length, lane(l)].astype(f32)
    before = jnp.dot(
        normalized(halo_ref[...], gain_ref[...]), wi_ref[...], preferred_element_type=f32
    ).astype(bf16)
    before_ref[...] = before
    for s in range(nseq):
        for l in range(NL):
            ext_ref[s, l, :PAD, :] = before[s * PAD : (s + 1) * PAD, lane(l)].astype(f32)

    @pl.when(pl.program_id(0) == 0)
    def _():
        proj_ref[...] = jnp.zeros_like(proj_ref)

    taps = cw_ref.shape[0]
    for s in range(nseq):

        def mix(i, _):
            r = pl.multiple_of(i * ROWS, ROWS)
            at = pl.ds(pl.multiple_of(s * length + r, ROWS), ROWS)
            for l in range(NL):
                pre = cb_ref[:, lane(l)]
                for k in range(taps):
                    pre = pre + cw_ref[k : k + 1, lane(l)] * ext_ref[s, l, pl.ds(r + PAD - taps + 1 + k, ROWS), :]
                sg = sigmoid(pre)
                x = (pre * sg).astype(bf16)
                slope_ref[at, lane(l)] = sg * (1.0 + pre * (1.0 - sg))
                x_ref[l, at, :] = x
                flat_ref[at, lane(l)] = x
            return 0

        lax.fori_loop(0, length // ROWS, mix, 0)
    proj_ref[...] += rows_dot(flat_ref[...], filled(sw_ref[...]))

    @pl.when(pl.program_id(0) == pl.num_programs(0) - 1)
    def _():
        values = proj_ref[...]
        lanes = lax.broadcasted_iota(jnp.int32, values.shape, 1)
        products = values * pltpu.roll(values, 128 - N, 1)
        own = (lanes >= rank) & (lanes < rank + N)
        total = jnp.sum(jnp.where(own, products, 0.0), axis=1, keepdims=True)
        meet_ref[...] = jnp.broadcast_to(total, meet_ref.shape)


def inner_side(tokens, halo, gain, in_weight, conv_weight, conv_bias, select_weight, nseq, length, rank):
    rows, model = tokens.shape
    picks, inner = select_weight.shape
    o = jax.ShapeDtypeStruct
    operands = (tokens, halo, gain, in_weight, conv_weight, conv_bias, select_weight)
    specs = [
        whole(tokens), whole(halo), whole(gain), block_of(model), block_of(conv_weight.shape[0]), block_of(1),
        block_of(picks),
    ]
    square = pl.BlockSpec((rows, 128), lambda j: (0, 0))
    return pl.pallas_call(
        functools.partial(inner_kernel, nseq=nseq, length=length, rank=rank),
        grid=(inner // WIDTH,),
        in_specs=specs,
        out_specs=[
            pl.BlockSpec((rows, model), lambda j: (0, 0)), block_of(rows), block_of(halo.shape[0]), tiles_of(rows), block_of(rows),
            square, square,
        ],
        out_shape=(
            o((rows, model), bf16), o((rows, inner), bf16), o((halo.shape[0], inner), bf16), o((inner // 128, rows, 128), bf16),
            o((rows, inner), f32), o((rows, 128), f32), o((rows, 128), f32),
        ),
        scratch_shapes=[pltpu.VMEM((nseq, NL, PAD + length, 128), f32), pltpu.VMEM((rows, WIDTH), bf16)],
        compiler_params=pltpu.CompilerParams(vmem_limit_bytes=VMEM, dimension_semantics=("arbitrary",)),
        cost_estimate=pl.CostEstimate(flops=2 * rows * model * inner, bytes_accessed=14 * 2**20, transcendentals=0),
        name="inner_side",
    )(*operands)


def input_grad_kernel(
    place_ref, cp_ref, inner_ref, before_ref, x_ref, slope_ref, pg_ref, sw_ref, cw_ref, turned_ref, halo_ref, gain_ref,
    rl_ref, proj_ref, dlog_ref, rb_ref, sk_ref, *refs, nseq, length, part, rank, grp, last,
):
    if last:
        early_ref, kept_ref, sent_ref, igr_ref, tail_ref, head_ref, pre_ref, back_ref, vec_ref = refs
    else:
        early_ref, (kept_ref, sent_ref, igr_ref, tail_ref, head_ref, small_ref, pre_ref, back_ref, vec_ref) = None, refs
    taps = cw_ref.shape[0]
    j = pl.program_id(0)
    wide = pg_ref.shape[1]
    back_ref[...] = cp_ref[...] + jnp.dot(
        pg_ref[:, wide // 2 :], filled(sw_ref[...]), preferred_element_type=f32
    )
    vec_ref[...] = jnp.zeros_like(vec_ref)
    small_step = 32
    for s in range(nseq):
        pre_ref[s, :, :PAD, :] = jnp.zeros((NL, PAD, 128), f32)
        pre_ref[s, :, PAD + length :, :] = jnp.zeros((NL, PAD, 128), f32)

        def first(i, total):
            r = pl.multiple_of(i * small_step, small_step)
            at = pl.ds(pl.multiple_of(s * length + r, small_step), small_step)
            back = back_ref[at, :] * slope_ref[at, :]
            for l in range(NL):
                pre_ref[s, l, pl.ds(pl.multiple_of(r + PAD, PAD), small_step), :] = back[:, lane(l)]
            return total + sum(back[q * 8 : (q + 1) * 8] for q in range(small_step // 8))

        total = lax.fori_loop(0, length // small_step, first, jnp.zeros((8, WIDTH), f32))
        vec_ref[taps : taps + 1, :] += jnp.sum(total, axis=0, keepdims=True)

        def second(i, totals):
            r = pl.multiple_of(i * small_step, small_step)
            at = pl.ds(pl.multiple_of(s * length + r, small_step), small_step)
            sums = []
            for l in range(NL):
                inner = inner_ref[at, lane(l)].astype(f32)
                result = jnp.zeros((small_step, 128), f32)
                for k in range(taps):
                    later = pre_ref[s, l, pl.ds(r + PAD + taps - 1 - k, small_step), :]
                    result = result + cw_ref[k : k + 1, lane(l)] * later
                    product = inner * later
                    sums.append(
                        totals[l * taps + k] + sum(product[q * 8 : (q + 1) * 8] for q in range(small_step // 8))
                    )
                igr_ref[at, lane(l)] = result.astype(bf16)
            return tuple(sums)

        totals = lax.fori_loop(0, length // small_step, second, (jnp.zeros((8, 128), f32),) * (taps * NL))
        head_rows = lax.broadcasted_iota(jnp.int32, (PAD, 128), 0) < taps - 1
        for l in range(NL):
            late = pre_ref[s, l, length:, :]
            tail_ref[s * PAD : (s + 1) * PAD, lane(l)] = sum(
                cw_ref[k : k + 1, lane(l)] * late[taps - 1 - k : taps - 1 - k + PAD] for k in range(taps)
            )
            lead = pre_ref[s, l, : 2 * PAD, :]
            before = before_ref[s * PAD : (s + 1) * PAD, lane(l)].astype(f32)
            before = jnp.concatenate([before[PAD - taps + 1 :], jnp.zeros((PAD - taps + 1, 128), f32)], axis=0)
            head = jnp.zeros((PAD, 128), f32)
            for k in range(taps):
                early = jnp.where(head_rows, lead[PAD - k : 2 * PAD - k], 0.0)
                head = head + cw_ref[k : k + 1, lane(l)] * early
                vec_ref[k : k + 1, lane(l)] += jnp.sum(totals[l * taps + k] + before * early, axis=0, keepdims=True)
            head_ref[s * PAD : (s + 1) * PAD, lane(l)] = head

    vec_ref[taps + 1 : taps + 2, :] = rb_ref[0:1, :]
    vec_ref[taps + 2 : taps + 3, :] = sk_ref[0:1, :]
    vec_ref[8:, :] = dlog_ref[...]
    count = place_ref.shape[0] - 1
    rows_each = turned_ref.shape[0] // count
    rows_pad = padded(rows_each)
    before_normed = normalized(halo_ref[...], gain_ref[...])
    products = []
    for b in range(WIDTH // wide):
        cols = slice(b * wide, (b + 1) * wide)
        shifted = jnp.concatenate(
            [
                jnp.concatenate(
                    [jnp.zeros((PAD - taps + 1, wide), f32), head_ref[s * PAD : s * PAD + taps - 1, cols]], axis=0
                )
                for s in range(nseq)
            ],
            axis=0,
        )
        product = jnp.dot(turned_ref[...], igr_ref[:, cols], preferred_element_type=f32) + contract_rows(
            before_normed, shifted.astype(bf16)
        )
        products.append(product.astype(bf16) if rows_each == rows_pad else product)
    eye = (
        lax.broadcasted_iota(jnp.int32, (vec_ref.shape[0], wide), 0) + rank
        == lax.broadcasted_iota(jnp.int32, (vec_ref.shape[0], wide), 1)
    ).astype(bf16)
    low = jnp.concatenate([proj_ref[...], jnp.zeros((proj_ref.shape[0], wide - proj_ref.shape[1]), f32)], axis=1)
    low = jnp.where(lax.broadcasted_iota(jnp.int32, low.shape, 1) < rank, low, 0.0).astype(bf16)
    small = (
        contract_rows(joined(x_ref, slice(None)), pg_ref[...])
        + contract_rows(rl_ref[...], low)
        + contract_rows(vec_ref[...].astype(bf16), eye)
    )
    def store(flag):
        half = count // 2
        for q in range(count):
            ref = kept_ref if (q // grp) % 2 == flag else sent_ref
            spot = lax.rem(place_ref[q], half)
            for b, product in enumerate(products):
                at = pl.ds(pl.multiple_of((j * len(products) + b) * rows_pad, rows_pad), rows_pad)
                ref[spot, at, :] = share_rows(product, q, rows_each)

    core = place_ref[count]
    for flag in range(2):
        pl.when(core == flag)(functools.partial(store, flag))
    if not last:
        small_ref[...] = small.astype(small_ref.dtype)
        return
    base = kept_ref.shape[1] - padded(part)

    def place_small(values, first):
        for q in range(WIDTH // part):
            share = place_ref[first + q]
            rows = share_rows(values, q, part)

            @pl.when(share < count // 2)
            def _():
                kept_ref[share, base : base + padded(part), :] = rows

            @pl.when(share >= count // 2)
            def _():
                sent_ref[share - count // 2, base : base + padded(part), :] = rows

    steps = pl.num_programs(0)
    place_small(early_ref[...], j * (WIDTH // part))
    place_small(small, (steps + j) * (WIDTH // part))


def input_grads(
    place, cp, inner, before, x, slope, pg, select_weight, conv_weight, turned, halo, gain, rate_low, proj,
    decay_grad, rate_bias_grad, skip_grad, early, nseq, length, part, rank, grp,
):
    rows, width = cp.shape
    width = width // 2
    last = early is not None
    first = width // WIDTH if last else 0
    wide = pg.shape[1]
    count = place.shape[0] - 1
    model = turned.shape[0]
    packed_rows = (width // wide) * padded(model // count) + (padded(part) if last else 0)
    o = jax.ShapeDtypeStruct

    def drop(spec, first=0):
        return pl.BlockSpec(
            spec.block_shape, lambda j, _, f=spec.index_map: f(j + first), pipeline_mode=spec.pipeline_mode
        )

    specs = [
        block_of(rows), block_of(rows), block_of(before.shape[0]), tiles_of(rows), block_of(rows), whole(pg),
        block_of(select_weight.shape[0]), block_of(conv_weight.shape[0]), whole(turned),
        whole(halo), whole(gain), block_of(rows), whole(proj), block_of(N), block_of(8), block_of(8),
    ]
    packed = pl.BlockSpec((count // 2, packed_rows, wide), lambda j: (0, 0, 0))
    out_specs = [packed, packed, block_of(rows), block_of(nseq * PAD), block_of(nseq * PAD)]
    outs = [
        o((count // 2, packed_rows, wide), bf16), o((count // 2, packed_rows, wide), bf16), o((rows, width), bf16),
        o((nseq * PAD, width), f32), o((nseq * PAD, width), f32),
    ]
    operands = [
        place, cp, inner, before, x, slope, pg, select_weight, conv_weight, turned, halo, gain, rate_low, proj,
        decay_grad, rate_bias_grad, skip_grad,
    ]
    in_specs = [drop(s, first) for s in specs]
    block = pl.BlockSpec((WIDTH, wide), lambda j: (j, 0))
    if last:
        operands.append(early)
        in_specs.append(drop(block))
    else:
        out_specs.append(block)
        outs.append(o((width, wide), f32 if part < 16 else bf16))
    return pl.pallas_call(
        functools.partial(input_grad_kernel, nseq=nseq, length=length, part=part, rank=rank, grp=grp, last=last),
        grid_spec=pltpu.PrefetchScalarGridSpec(
            num_scalar_prefetch=1,
            grid=(width // WIDTH,),
            in_specs=in_specs,
            out_specs=[drop(s) for s in out_specs],
            scratch_shapes=[
                pltpu.VMEM((nseq, NL, PAD + length + PAD, 128), f32), pltpu.VMEM((rows, WIDTH), f32),
                pltpu.VMEM((8 + N, WIDTH), f32),
            ],
        ),
        out_shape=outs,
        compiler_params=pltpu.CompilerParams(vmem_limit_bytes=VMEM, dimension_semantics=("arbitrary",)),
        cost_estimate=pl.CostEstimate(flops=24 * rows * width * model, bytes_accessed=16 * 2**20, transcendentals=0),
        name="input_grads",
    )(*operands)


def padded(rows):
    return max(rows, 16)


def share_rows(values, share, rows):
    taken = values[share * rows : (share + 1) * rows]
    if rows < padded(rows):
        taken = jnp.concatenate([taken, jnp.zeros((padded(rows) - rows, values.shape[1]), values.dtype)], axis=0)
    return taken.astype(bf16)


def weight_grad_kernel(gated_ref, gate_ref, cot_ref, turned_ref, packed_ref, *, part):
    j = pl.program_id(0)
    count = packed_ref.shape[0]
    model = cot_ref.shape[1]
    rows_each = model // count
    rows_pad = padded(rows_each)
    product = contract_rows(gated_ref[...], cot_ref[...])
    for q in range(WIDTH // part):
        packed_ref[j * (WIDTH // part) + q, : padded(part), :] = share_rows(product, q, part)
    product = jnp.dot(turned_ref[...], gate_ref[...], preferred_element_type=f32)
    each = model // WIDTH
    at = pl.ds(pl.multiple_of(padded(part) + (j // each) * rows_pad, 16), rows_pad)
    cols = pl.ds(pl.multiple_of((j % each) * WIDTH, WIDTH), WIDTH)
    for q in range(count):
        packed_ref[q, at, cols] = share_rows(product, q, rows_each)


def weight_grads(gated, gate_grad, cot, turned, part):
    rows, width = gated.shape
    model = cot.shape[1]
    count = width // part
    packed_rows = padded(part) + (width // model) * padded(model // count)
    return pl.pallas_call(
        functools.partial(weight_grad_kernel, part=part),
        grid=(width // WIDTH,),
        in_specs=[block_of(rows), block_of(rows), whole(cot), whole(turned)],
        out_specs=pl.BlockSpec((count, packed_rows, model), lambda j: (0, 0, 0)),
        out_shape=jax.ShapeDtypeStruct((count, packed_rows, model), bf16),
        compiler_params=pltpu.CompilerParams(vmem_limit_bytes=VMEM, dimension_semantics=("arbitrary",)),
        cost_estimate=pl.CostEstimate(flops=4 * rows * width * model, bytes_accessed=14 * 2**20, transcendentals=0),
        name="weight_grads",
    )(gated, gate_grad, cot, turned)


def share_kernel(place_ref, *refs, count, rank, taps, part, part_rows, picks):
    first, second = refs[:count], refs[count : 2 * count]
    summed_ref, weight_ref, gain_ref = refs[2 * count : 2 * count + 3]
    in_ref, out_ref, conv_ref, bias_ref, select_ref, rate_ref, rate_bias_ref, decay_ref, skip_ref, norm_ref = refs[
        2 * count + 3 :
    ]
    pad = padded(part_rows)
    wide = first[0].shape[2]
    model = summed_ref.shape[1]
    each = first[0].shape[1] // pad

    def total(held, at, rows):
        return sum(h[0, at : at + rows, :].astype(f32) for h in held)

    for half, held in enumerate((first, second)):
        for b in range(each):
            at = (half * each + b) * wide
            in_ref[:, at : at + wide] = total(held, b * pad, pad)[:part_rows]
    gate_at = 2 * each * wide
    for b in range((in_ref.shape[1] - gate_at) // model):
        at = padded(part) + b * pad
        in_ref[:, gate_at + b * model : gate_at + (b + 1) * model] = summed_ref[at : at + pad, :][:part_rows].astype(f32)
    out_ref[...] = summed_ref[: padded(part), :][:part].astype(f32)
    gain = jnp.sum(weight_ref[...].astype(f32) * in_ref[...], axis=1, keepdims=True)
    gain = jnp.broadcast_to(gain, (part_rows, 128))
    if part_rows < 8:
        gain = jnp.concatenate([gain, jnp.zeros((8 - part_rows, 128), f32)], axis=0)
    gains = gain_ref[...]
    gains = pltpu.roll(gains, gains.shape[1] - place_ref[0] * part_rows, 1)
    norm_ref[...] = gain.T[:1, :part_rows] / gains[:, :part_rows]
    small = total(second, each * pad, padded(part))[:part]
    turned = small[:, : wide // 2].T
    rate_ref[...] = turned[:rank]
    conv_ref[...] = turned[rank : rank + taps]
    bias_ref[...] = turned[rank + taps : rank + taps + 1]
    rate_bias_ref[...] = turned[rank + taps + 1 : rank + taps + 2]
    skip_ref[...] = turned[rank + taps + 2 : rank + taps + 3]
    decay_ref[...] = turned[rank + 8 : rank + 8 + N]
    select_ref[...] = small[:, wide // 2 : wide // 2 + picks]


def shares_of(first, second, summed, in_weight, gain, place, rank, taps, part, part_rows, picks):
    width = in_weight.shape[1]
    model = summed.shape[1]
    o = lambda *shape: jax.ShapeDtypeStruct(shape, f32)
    own = pl.BlockSpec((part_rows, width), lambda i, s: (s[0], 0))
    if part_rows % 16:
        in_weight = lax.dynamic_slice_in_dim(in_weight, place * part_rows, part_rows, 0)
        own = pl.BlockSpec((part_rows, width), lambda i, s: (0, 0))
    fixed = lambda shape: pl.BlockSpec(shape, lambda i, s: (0,) * len(shape))
    arrays = (*first, *second, summed, in_weight, gain)
    specs = [fixed(a.shape) for a in arrays]
    specs[-2] = own
    outs = (
        o(part_rows, width), o(part, model), o(taps, part), o(1, part), o(part, picks), o(rank, part), o(1, part),
        o(N, part), o(1, part), o(1, part_rows),
    )
    return pl.pallas_call(
        functools.partial(
            share_kernel, count=len(first), rank=rank, taps=taps, part=part, part_rows=part_rows, picks=picks
        ),
        grid_spec=pltpu.PrefetchScalarGridSpec(
            num_scalar_prefetch=1, grid=(1,), in_specs=specs, out_specs=[fixed(out.shape) for out in outs],
        ),
        out_shape=outs,
        compiler_params=pltpu.CompilerParams(vmem_limit_bytes=VMEM, dimension_semantics=("arbitrary",)),
        name="shares",
    )(place[None].astype(jnp.int32), *arrays)


def flip_bit(axis, bit):
    return [(i, i ^ bit) for i in range(lax.axis_size(axis))]


def bits_of(axis):
    size = lax.axis_size(axis)
    return [(axis, 1 << k) for k in range(size.bit_length() - 1)]


def places(order):
    grp = lax.axis_size("grp")
    other = jnp.arange(lax.axis_size("seq") * grp) ^ (lax.axis_index("seq") * grp + lax.axis_index("grp"))
    position = jnp.zeros_like(other)
    for axis, bit in order:
        position = 2 * position + (other // (bit * grp if axis == "seq" else bit)) % 2
    return position.astype(jnp.int32)


def pairs_of(bits):
    return [bits[i : i + 2] for i in range(0, len(bits), 2)]


def round_parts(held, bits):
    count = 1 << len(bits)
    size = held[0].shape[0] // count
    parts = [sum(h[i * size : (i + 1) * size].astype(f32) for h in held) for i in range(count)]
    return parts[:1] + [part.astype(bf16) for part in parts[1:]]


def round_trade(parts, bits):
    held = parts[:1]
    for i in range(1, len(parts)):
        flip = sum(bit for at, (axis, bit) in enumerate(bits) if (i >> (len(bits) - 1 - at)) & 1)
        held.append(lax.ppermute(parts[i], bits[0][0], flip_bit(bits[0][0], flip)))
    return held


def sum_packed(kept, sent, rounds, later):
    axis, bit = rounds[0][0]
    held = [kept, lax.ppermute(sent, axis, flip_bit(axis, bit))]
    for bits in rounds[1:]:
        parts = round_parts(held, bits)
        if later is not None:
            *parts, later = lax.optimization_barrier((*parts, later))
        held = round_trade(parts, bits)
    return held, later


def remaining_rounds(held, rounds, later):
    for bits in rounds:
        parts = round_parts(held, bits)
        if later is not None and bits is rounds[-1]:
            *parts, later = lax.optimization_barrier((*parts, later))
        held = round_trade(parts, bits)
    return held, later


def carried(block, shape, rates, backward, after=None, spans=None):
    count, mine = lax.axis_size("seq"), lax.axis_index("seq")
    blocks = lax.all_gather(block, "seq")
    if after is not None:
        blocks, after = lax.optimization_barrier((blocks, after))
    rows = shape[0] * shape[1]
    entering = jnp.zeros(shape, f32)
    for turn in range(count - 1):
        j = count - 1 - turn if backward else turn
        theirs = blocks[j].astype(f32)
        span = (theirs if spans is None else spans[j].astype(f32))[rows : rows + 2 * shape[0]]
        span = span[: shape[0]] + span[shape[0] :]
        longer = jnp.exp(span[:, None, :] * rates) * entering + theirs[:rows].reshape(shape)
        entering = jnp.where(mine < j if backward else j < mine, longer, entering)
    return entering, after, blocks


def contract_rows(left, right, kind=f32):
    return lax.dot_general(left, right, (((0,), (0,)), ((), ())), preferred_element_type=f32).astype(kind)


def shards(
    tokens,
    cotangent,
    norm_gain,
    in_weight,
    conv_weight,
    conv_bias,
    select_weight,
    rate_weight,
    rate_bias,
    decay_log,
    skip_gain,
    out_weight,
):
    nseq, length, model = tokens.shape
    inner_width = out_weight.shape[0]
    rank = rate_weight.shape[0]
    taps = conv_weight.shape[0]
    rows = nseq * length
    share_count = lax.axis_size("seq") * lax.axis_size("grp")
    tok = tokens.reshape(rows, model)
    cot = cotangent.reshape(rows, model)
    gain, skip, bias = norm_gain[None], skip_gain[None], conv_bias[None]
    pieces, grp = lax.axis_size("seq"), lax.axis_size("grp")
    halo = lax.ppermute(tokens[:, length - PAD :], "seq", [(i, i + 1) for i in range(pieces - 1)])
    halo = halo.reshape(nseq * PAD, model)
    picks, wide = rank + 2 * N, 256
    select_weight = select_weight.T
    normed, inner, before, x, slope, proj, bc = inner_side(
        tok, halo, gain, in_weight, conv_weight, bias, select_weight, nseq, length, rank
    )
    in_gate, out_gate = proj[:, rank : rank + N], proj[:, rank + N : picks]
    log = decay_log.T
    rates = -jnp.exp(log)
    bb = jnp.broadcast_to(in_gate[:, :, None], (rows, N, 128))
    ahead, dl, u = state_end(proj, rate_weight, rate_bias[None], x, log, bb, nseq, length)
    ahead, cot = lax.optimization_barrier((ahead, cot))
    turned, g, ga, gs = gate_side(normed, cot, in_weight, out_weight)
    state_shape = (nseq, N, inner_width)
    entering, _, spans = carried(ahead, state_shape, rates, False)
    cb = jnp.broadcast_to(out_gate[:, :, None], (rows, N, 128))
    sent_back = adjoint_end(dl, g, log, cb, nseq, length)
    lc = spread(out_gate, nseq, length, 1, False)
    lb = spread(in_gate, nseq, length, 2, True)
    ls = jnp.asarray(own_column(nseq * T, T, nseq, 2, 1, True))
    behind, lb, ls, u = lax.optimization_barrier((sent_back, lb, ls, u))
    states, gated, gate_grad, out_grad, shift, skip_grad = forward(
        dl, u, g, ga, gs, x, skip, bb, bc, lc, log, entering, nseq, length, 4
    )
    part, part_rows = inner_width // share_count, model // share_count
    weight_packed = weight_grads(gated, gate_grad, cot, turned, part)
    leaving, weight_packed, _ = carried(behind, state_shape, rates, True, weight_packed, spans)
    weight_sum = lax.psum_scatter(weight_packed, "seq", scatter_dimension=0, tiled=True)
    rate_low, conv_part, in_grad, decay_grad, rate_bias_grad = backward(
        dl, u, g, x, skip, cb, lb, ls, log, leaving, states, nseq, length, 4
    )
    out_grad = out_grad.reshape(rows, N) + in_gate * jnp.sum(shift, axis=1, keepdims=True)
    rank_grad = rows_dot(rate_low, rate_weight)
    pg = jnp.concatenate(
        [
            jnp.zeros((rows, wide // 2), bf16),
            rank_grad.astype(bf16),
            in_grad.reshape(rows, N).astype(bf16),
            out_grad.astype(bf16),
            jnp.zeros((rows, wide // 2 - picks), bf16),
        ],
        axis=1,
    )
    seq_bits, grp_bits = bits_of("seq"), bits_of("grp")
    order = seq_bits + grp_bits
    place = jnp.concatenate([places(order), (lax.axis_index("seq") % 2)[None].astype(jnp.int32)])
    rounds = [seq_bits[:1]] + pairs_of(seq_bits[1:]) + pairs_of(grp_bits)
    half_width = inner_width // 2

    def half(conv_part, early):
        return input_grads(
            place, conv_part, inner, before, x, slope, pg, select_weight, conv_weight, turned, halo, gain, rate_low,
            proj, decay_grad, rate_bias_grad, skip_grad, early, nseq, length, part, rank, grp,
        )

    kept, sent, first_grad, first_tail, first_head, early = half(conv_part, None)
    sent, gated = lax.optimization_barrier((sent, gated))
    wide_tok = tok.astype(f32)
    block_out = wide_tok + jnp.dot(gated, out_weight, preferred_element_type=f32)
    first_held, (conv_part, block_out) = sum_packed(kept, sent, rounds[:2], (conv_part, block_out))
    kept, sent, second_grad, second_tail, second_head = half(conv_part, early)
    head = jnp.concatenate([first_head, second_head], axis=1)
    *first_held, sent, head, weight_sum = lax.optimization_barrier((*first_held, sent, head, weight_sum))
    head = head.reshape(nseq, PAD, inner_width)[:, : taps - 1].astype(bf16)
    returned = lax.ppermute(head, "seq", [(i + 1, i) for i in range(pieces - 1)]).astype(f32)
    held, (gate_grad, *first_held) = sum_packed(kept, sent, rounds[:2], (gate_grad, *first_held))
    normed_grad = rows_dot(gate_grad, in_weight[:, inner_width:])
    *first_held, normed_grad = lax.optimization_barrier((*first_held, normed_grad))
    first_held, _ = remaining_rounds(first_held, rounds[2:], None)
    held, (returned, second_grad, normed_grad, second_tail) = remaining_rounds(
        held, rounds[2:], (returned, second_grad, normed_grad, second_tail)
    )
    weight_share = lax.psum_scatter(weight_sum, "grp", scatter_dimension=0, tiled=True)[0]
    in_share, out_share, conv_share, bias_share, select_share, rate_share, rate_bias_share, decay_share, skip_share, (
        gain_share
    ) = shares_of(
        first_held, held, weight_share, in_weight, gain, lax.axis_index("seq") * grp + lax.axis_index("grp"), rank,
        taps, part, part_rows, picks,
    )
    tail = jnp.concatenate([first_tail, second_tail], axis=1)
    fixed = (tail.reshape(nseq, PAD, inner_width)[:, PAD - taps + 1 :] + returned).astype(bf16)

    def patched(grad, at):
        rows_of = grad.reshape(nseq, length, half_width)
        rows_of = rows_of.at[:, length - taps + 1 :].set(fixed[:, :, at : at + half_width])
        return rows_of.reshape(rows, half_width)

    normed_grad = (
        normed_grad
        + rows_dot(patched(first_grad, 0), in_weight[:, :half_width])
        + rows_dot(patched(second_grad, half_width), in_weight[:, half_width:inner_width])
    )
    scale = lax.rsqrt(jnp.mean(wide_tok * wide_tok, axis=1, keepdims=True) + epsilon)
    lifted = normed_grad * norm_gain
    dots = jnp.mean(lifted * wide_tok, axis=1, keepdims=True)
    tokens_grad = cot.astype(f32) + scale * lifted - wide_tok * (scale * scale * scale) * dots
    return (
        block_out.astype(bf16).reshape(tokens.shape),
        tokens_grad.astype(bf16).reshape(tokens.shape),
        gain_share[0],
        in_share,
        conv_share,
        bias_share[0],
        select_share,
        rate_share,
        rate_bias_share[0],
        decay_share.T,
        skip_share[0],
        out_share,
    )


def solution(mesh):
    sharded = P("grp", "seq", None)
    shares = ("seq", "grp")
    return jax.shard_map(
        shards,
        mesh=mesh,
        in_specs=(sharded, sharded) + (P(),) * 10,
        out_specs=(
            sharded,
            sharded,
            P(shares),
            P(shares, None),
            P(None, shares),
            P(shares),
            P(shares, None),
            P(None, shares),
            P(shares),
            P(shares, None),
            P(shares),
            P(shares, None),
        ),
        check_vma=False,
    )
```

```python
import functools
import math

import jax
import jax.numpy as jnp
import ml_dtypes
import numpy as np
from jax import lax
from jax.experimental import pallas as pl
from jax.experimental.pallas import tpu as pltpu
from jax.sharding import PartitionSpec as P

f32 = jnp.float32
bf16 = jnp.bfloat16
LOG2E = 1.4426950408889634
N = 16
T = 16
WIDTH = 512
NL = WIDTH // 128
VMEM = 60 * 2**20


def lane(l):
    return slice(l * 128, (l + 1) * 128)


def sigmoid(v):
    return pltpu.reciprocal(1.0 + jnp.exp2(v * -LOG2E), approx=True)


def joined(ref, rows):
    return jnp.concatenate([ref[l, rows, :] for l in range(NL)], axis=1)


def steps_of(rows):
    return pl.ds(pl.multiple_of(rows, T), T)


def rows_dot(left, right):
    return lax.dot_general(left, right, (((1,), (1,)), ((), ())), preferred_element_type=f32)


def rates_of(log_ref):
    return -jnp.exp(log_ref[...])


def state_end_kernel(
    proj_ref, rw_ref, rb_ref, x_ref, log_ref, bb_ref, block_ref, dl_ref, u_ref, a2_ref, pre_ref, *, nseq, length,
):
    rows = nseq * length
    a2_ref[...] = rates_of(log_ref) * LOG2E
    low = proj_ref[:, : rw_ref.shape[0]].astype(bf16)
    pre_ref[...] = jnp.dot(low, rw_ref[...], preferred_element_type=f32) + rb_ref[...]

    def steps(i, _):
        r = pl.multiple_of(i * 64, 64)
        at = pl.ds(r, 64)
        pre = pre_ref[at, :]
        d = jnp.maximum(pre, 0.0) + jnp.log(1.0 + jnp.exp(-jnp.abs(pre)))
        for l in range(NL):
            dl_ref[l, at, :] = d[:, lane(l)]
            u_ref[l, at, :] = d[:, lane(l)] * x_ref[l, at, :].astype(f32)
        return 0

    lax.fori_loop(0, rows // 64, steps, 0)
    fill = block_ref.shape[0] - nseq * (N + 2)
    for l in range(NL):
        spans = [
            jnp.sum(dl_ref[l, s * length : (s + 1) * length, :], axis=0, keepdims=True) for s in range(nseq)
        ]
        highs = [span.astype(bf16).astype(f32) for span in spans]
        lows = [span - high for span, high in zip(spans, highs)]
        rows_of = jnp.concatenate(highs + lows + [jnp.zeros((fill, 128), f32)], axis=0)
        block_ref[nseq * N :, lane(l)] = rows_of.astype(bf16)

    def step(c, h):
        h = [list(v) for v in h]
        for k in range(T):
            for s in range(nseq):
                t = s * length + c * T + k
                bt = bb_ref[t]
                for l in range(NL):
                    f = jnp.exp2(dl_ref[l, pl.ds(t, 1), :] * a2_ref[:, lane(l)])
                    h[s][l] = f * h[s][l] + u_ref[l, pl.ds(t, 1), :] * bt
        return tuple(tuple(v) for v in h)

    z = jnp.zeros((N, 128), f32)
    h = lax.fori_loop(0, length // T, step, ((z,) * NL,) * nseq)
    for s in range(nseq):
        for l in range(NL):
            block_ref[s * N : (s + 1) * N, lane(l)] = h[s][l].astype(bf16)


def adjoint_end_kernel(dl_ref, g_ref, log_ref, cb_ref, sb_ref, a2_ref, *, nseq, length):
    a2_ref[...] = rates_of(log_ref) * LOG2E
    nch = length // T

    def step(m, lam):
        lam = [list(v) for v in lam]
        c = nch - 1 - m
        for k in reversed(range(T)):
            for s in range(nseq):
                t = s * length + c * T + k
                ct = cb_ref[t]
                for l in range(NL):
                    f = jnp.exp2(dl_ref[l, pl.ds(t, 1), :] * a2_ref[:, lane(l)])
                    lam[s][l] = f * (lam[s][l] + g_ref[l, pl.ds(t, 1), :] * ct)
        return tuple(tuple(v) for v in lam)

    z = jnp.zeros((N, 128), f32)
    lam = lax.fori_loop(0, nch, step, ((z,) * NL,) * nseq)
    for s in range(nseq):
        for l in range(NL):
            sb_ref[s * N : (s + 1) * N, lane(l)] = lam[s][l].astype(bf16)


def state_copy(states_ref, held_ref, sems, at, q, s, length, unroll, out):
    size = unroll * T * N
    rows = pl.ds(pl.multiple_of(s * length * N + q * size, size), size)
    far = states_ref.at[rows, pl.ds(pl.multiple_of(at * WIDTH, WIDTH), WIDTH)]
    near = held_ref.at[s, q]
    return pltpu.make_async_copy(near, far, sems.at[s, q]) if out else pltpu.make_async_copy(far, near, sems.at[s, q])


def state_scratch(nseq, length, unroll):
    groups = length // (T * unroll)
    return [
        pltpu.VMEM((N, WIDTH), f32), pltpu.VMEM((nseq, groups, unroll * T * N, WIDTH), bf16),
        pltpu.SemaphoreType.DMA((nseq, groups)),
    ]


def forward_kernel(
    dl_ref, u_ref, g_ref, ga_ref, gs_ref, x_ref, skip_ref, bb_ref, bc_ref, lc_ref, log_ref, hin_ref,
    hb_ref, gated_ref, ggr_ref, outg_ref, gu_ref, sk_ref, a2_ref, held_ref, sems, *, nseq, length, unroll,
):
    a2_ref[...] = rates_of(log_ref) * LOG2E
    nch = length // T
    skip = skip_ref[...]
    ones = jnp.ones((8, 128), bf16)

    @pl.when(pl.program_id(0) == 0)
    def _():
        outg_ref[...] = jnp.zeros_like(outg_ref)
        gu_ref[...] = jnp.zeros_like(gu_ref)

    step_at, last_step = pl.program_id(0), pl.num_programs(0) - 1

    def leaving(at, q, s):
        return state_copy(hb_ref, held_ref, sems, at, q, s, length, unroll, True)

    def chunk(c, p, q, h, acc):
        hbv, pov = {}, [[None] * T for _ in range(nseq)]
        for k in range(T):
            for s in range(nseq):
                t = s * length + c * T + k
                bt = bb_ref[t]
                po = None
                for l in range(NL):
                    g = jnp.broadcast_to(g_ref[l, pl.ds(t, 1), :], (N, 128)).astype(bf16)
                    f = jnp.exp2(dl_ref[l, pl.ds(t, 1), :] * a2_ref[:, lane(l)])
                    held = f * h[s][l]
                    h[s][l] = held + u_ref[l, pl.ds(t, 1), :] * bt
                    hb = held.astype(bf16)
                    held_ref[s, q, (p * T + k) * N : (p * T + k + 1) * N, lane(l)] = hb
                    hbv[k, s, l] = hb
                    po = hb * g if po is None else po + hb * g
                pov[s][k] = po
        lhs = jnp.concatenate([lc_ref[steps_of(s * length + c * T), :] for s in range(nseq)], axis=0)
        parts = []
        for l in range(0, NL, 2):
            rhs = jnp.concatenate(
                [
                    jnp.concatenate([hbv[k, s, l], hbv[k, s, l + 1]], axis=1)
                    for k in range(T) for s in range(nseq)
                ],
                axis=0,
            )
            parts.append(jnp.dot(lhs, rhs, preferred_element_type=f32))
        sc_all = jnp.concatenate(parts, axis=1)
        for s in range(nseq):
            og = rows_dot(ones, jnp.concatenate(pov[s], axis=0))
            outg_ref[pl.ds(s * nch + c, 1), :] += og[:1]
            at = steps_of(s * length + c * T)
            x = joined(x_ref, at).astype(f32)
            gx = joined(g_ref, at) * x
            d = joined(dl_ref, at)
            bc = jnp.concatenate([bc_ref[at, :]] * NL, axis=1)
            mo = sc_all[s * T : (s + 1) * T] + (d * bc + skip) * x
            gu = gx * d
            gu_ref[at, :] += sum(gu[:, lane(l)] for l in range(NL))
            gated_ref[at, :] = (mo * joined(ga_ref, at)).astype(bf16)
            ggr_ref[at, :] = (mo * joined(gs_ref, at)).astype(bf16)
            acc = acc + gx
        return acc

    def step(i, carry):
        h, acc = carry
        h = [list(v) for v in h]
        @pl.when(step_at > 0)
        def _():
            for s in range(nseq):
                leaving(step_at - 1, i, s).wait()

        for p in range(unroll):
            acc = chunk(i * unroll + p, p, i, h, acc)
        for s in range(nseq):
            leaving(step_at, i, s).start()
        return tuple(tuple(v) for v in h), acc

    h0 = tuple(tuple(hin_ref[s, :, lane(l)] for l in range(NL)) for s in range(nseq))
    _, acc = lax.fori_loop(0, nch // unroll, step, (h0, jnp.zeros((T, WIDTH), f32)))
    sk_ref[...] = jnp.broadcast_to(jnp.sum(acc, axis=0, keepdims=True), sk_ref.shape)

    @pl.when(step_at == last_step)
    def _():
        for q in range(nch // unroll):
            for s in range(nseq):
                leaving(step_at, q, s).wait()


def backward_kernel(
    dl_ref, u_ref, g_ref, x_ref, skip_ref, cb_ref, lb_ref, ls_ref, log_ref, lin_ref, hb_ref,
    rl_ref, cp_ref, ing_ref, dlog_ref, rb_ref, a2_ref, held_ref, sems, *, nseq, length, unroll,
):
    a2_ref[...] = rates_of(log_ref) * LOG2E
    nch = length // T
    abf = rates_of(log_ref).astype(bf16)
    skip = skip_ref[...]
    ones = jnp.ones((8, 128), bf16)

    @pl.when(pl.program_id(0) == 0)
    def _():
        ing_ref[...] = jnp.zeros_like(ing_ref)

    step_at, last_step = pl.program_id(0), pl.num_programs(0) - 1
    groups = nch // unroll

    def arriving(at, q, s):
        return state_copy(hb_ref, held_ref, sems, at, q, s, length, unroll, False)

    @pl.when(step_at == 0)
    def _():
        for q in reversed(range(groups)):
            for s in range(nseq):
                arriving(0, q, s).start()

    def chunk(c, p, group, lam, dlog, rb):
        pov = [[None] * T for _ in range(nseq)]
        dacc = [None] * NL
        vals = {}
        for k in reversed(range(T)):
            for s in range(nseq):
                t = s * length + c * T + k
                ct = cb_ref[t]
                po = None
                for l in range(NL):
                    d = jnp.broadcast_to(dl_ref[l, pl.ds(t, 1), :], (N, 128))
                    u = jnp.broadcast_to(u_ref[l, pl.ds(t, 1), :], (N, 128)).astype(bf16)
                    a = g_ref[l, pl.ds(t, 1), :] * ct + lam[s][l]
                    lam[s][l] = jnp.exp2(d * a2_ref[:, lane(l)]) * a
                    ab = a.astype(bf16)
                    q = ab * held_ref[s, group, (p * T + k) * N : (p * T + k + 1) * N, lane(l)] * abf[:, lane(l)]
                    qd = q * d.astype(bf16)
                    vals[k, s, l] = (ab, q)
                    dacc[l] = qd if dacc[l] is None else dacc[l] + qd
                    po = ab * u if po is None else po + ab * u
                pov[s][k] = po
            if k % 8 == 0:
                for l in range(NL):
                    dlog[l] = dlog[l] + dacc[l].astype(f32)
                    dacc[l] = None
        lhs = jnp.concatenate(
            [lb_ref[steps_of(s * length + c * T), :] for s in range(nseq)] + [ls_ref[...]], axis=0
        )
        parts = []
        for l in range(0, NL, 2):
            rhs = jnp.concatenate(
                [
                    jnp.concatenate([vals[k, s, l][y], vals[k, s, l + 1][y]], axis=1)
                    for k in reversed(range(T)) for s in range(nseq) for y in range(2)
                ],
                axis=0,
            )
            parts.append(jnp.dot(lhs, rhs, preferred_element_type=f32))
        both = jnp.concatenate(parts, axis=1)
        for s in range(nseq):
            w = both[s * T : (s + 1) * T]
            qs = both[(nseq + s) * T : (nseq + s + 1) * T]
            ig = rows_dot(ones, jnp.concatenate(pov[s], axis=0))
            ing_ref[pl.ds(s * nch + c, 1), :] += ig[:1]
            at = steps_of(s * length + c * T)
            d = joined(dl_ref, at)
            rg = (qs + w * joined(x_ref, at).astype(f32)) * (1.0 - jnp.exp(-d))
            rb = rb + rg
            rl_ref[at, :] = rg.astype(bf16)
            cp_ref[at, :] = w * d + skip * joined(g_ref, at)
        return rb

    def step(m, carry):
        lam, dlog, rb = carry
        lam = [list(v) for v in lam]
        dlog = list(dlog)
        q = groups - 1 - m
        for s in range(nseq):
            arriving(step_at, q, s).wait()
        for p in reversed(range(unroll)):
            rb = chunk(q * unroll + p, p, q, lam, dlog, rb)

        @pl.when(step_at < last_step)
        def _():
            for s in range(nseq):
                arriving(step_at + 1, q, s).start()

        return tuple(tuple(v) for v in lam), tuple(dlog), rb

    l0 = tuple(tuple(lin_ref[s, :, lane(l)] for l in range(NL)) for s in range(nseq))
    z = jnp.zeros((N, 128), f32)
    _, dlog, rb = lax.fori_loop(0, nch // unroll, step, (l0, (z,) * NL, jnp.zeros((T, WIDTH), f32)))
    for l in range(NL):
        dlog_ref[:, lane(l)] = dlog[l]
    rb_ref[...] = jnp.broadcast_to(jnp.sum(rb, axis=0, keepdims=True), rb_ref.shape)


def block_of(rows):
    return pl.BlockSpec((rows, WIDTH), lambda j: (0, j))


def tiles_of(rows):
    return pl.BlockSpec((NL, rows, 128), lambda j: (j, 0, 0))


def states_of(nseq):
    return pl.BlockSpec((nseq, N, WIDTH), lambda j: (0, 0, j))


def whole(a):
    return pl.BlockSpec(a.shape, lambda j: (0,) * a.ndim, pipeline_mode=pl.Buffered(1))


def kernel_call(body, name, channels, operands, specs, out_specs, outs, flops, scratch=(), **options):
    moved = sum(a.size * a.dtype.itemsize for a in operands) + sum(
        math.prod(o.shape) * o.dtype.itemsize for o in outs
    )
    return pl.pallas_call(
        functools.partial(body, **options),
        grid=(channels // WIDTH,),
        in_specs=specs,
        out_specs=out_specs,
        out_shape=outs,
        scratch_shapes=scratch,
        compiler_params=pltpu.CompilerParams(vmem_limit_bytes=VMEM, dimension_semantics=("arbitrary",)),
        cost_estimate=pl.CostEstimate(flops=flops, bytes_accessed=moved, transcendentals=0),
        name=name,
    )(*operands)


def spread(values, nseq, length, kinds, reverse):
    mask = own_column(nseq * length, length, nseq, kinds, 0, reverse)
    width = mask.shape[1]
    pick = (np.arange(width)[None, :] % N == np.arange(N)[:, None]).astype(ml_dtypes.bfloat16)
    wide = jnp.dot(values.astype(bf16), pick, preferred_element_type=f32)
    return wide.astype(bf16) * mask


def own_column(rows, length, nseq, kinds, kind, reverse):
    column = np.arange(T * nseq * kinds * N)[None, :]
    row = np.arange(rows)[:, None]
    step = column // (nseq * kinds * N)
    if reverse:
        step = T - 1 - step
    own = (step == row % T) & ((column // (kinds * N)) % nseq == row // length) & ((column // N) % kinds == kind)
    return own.astype(ml_dtypes.bfloat16)


def block_rows(nseq):
    return -(-nseq * (N + 2) // 16) * 16


def state_end(proj, rate_weight, rate_bias, x, log, bb, nseq, length):
    tiles, rows, _ = x.shape
    ch = tiles * 128
    o = jax.ShapeDtypeStruct
    return kernel_call(
        state_end_kernel, "state_end", ch,
        (proj, rate_weight, rate_bias, x, log, bb),
        [whole(proj), block_of(rate_weight.shape[0]), block_of(1), tiles_of(rows), block_of(N), whole(bb)],
        [block_of(block_rows(nseq)), tiles_of(rows), tiles_of(rows)],
        (o((block_rows(nseq), ch), bf16), o(x.shape, f32), o(x.shape, f32)),
        2 * 10**10, nseq=nseq, length=length,
        scratch=[pltpu.VMEM((N, WIDTH), f32), pltpu.VMEM((rows, WIDTH), f32)],
    )


def adjoint_end(dl, g, log, cb, nseq, length):
    tiles, rows, _ = dl.shape
    ch = tiles * 128
    return kernel_call(
        adjoint_end_kernel, "adjoint_end", ch,
        (dl, g, log, cb),
        [tiles_of(rows), tiles_of(rows), block_of(N), whole(cb)],
        [block_of(nseq * N)],
        (jax.ShapeDtypeStruct((nseq * N, ch), bf16),),
        2 * 10**10, nseq=nseq, length=length, scratch=[pltpu.VMEM((N, WIDTH), f32)],
    )[0]


def forward(dl, u, g, ga, gs, x, skip, bb, bc, lc, log, hin, nseq, length, unroll=1):
    tiles, rows, _ = dl.shape
    ch = tiles * 128
    o = jax.ShapeDtypeStruct
    t = tiles_of(rows)
    return kernel_call(
        forward_kernel, "forward", ch,
        (dl, u, g, ga, gs, x, skip, bb, bc, lc, log, hin),
        [t, t, t, t, t, t, block_of(1), whole(bb), whole(bc), whole(lc), block_of(N), states_of(nseq)],
        [
            pl.BlockSpec(memory_space=pl.ANY), block_of(rows), block_of(rows), pl.BlockSpec((rows // T, T * N), lambda j: (0, 0)),
            pl.BlockSpec((rows, 128), lambda j: (0, 0)), block_of(8),
        ],
        (
            o((rows * N, ch), bf16), o((rows, ch), bf16), o((rows, ch), bf16), o((rows // T, T * N), f32),
            o((rows, 128), f32), o((8, ch), f32),
        ),
        3 * 10**10, nseq=nseq, length=length, unroll=unroll, scratch=state_scratch(nseq, length, unroll),
    )


def backward(dl, u, g, x, skip, cb, lb, ls, log, lin, hb, nseq, length, unroll=1):
    tiles, rows, _ = dl.shape
    ch = tiles * 128
    o = jax.ShapeDtypeStruct
    t = tiles_of(rows)
    st = states_of(nseq)
    return kernel_call(
        backward_kernel, "backward", ch,
        (dl, u, g, x, skip, cb, lb, ls, log, lin, hb),
        [t, t, t, t, block_of(1), whole(cb), whole(lb), whole(ls), block_of(N), st, pl.BlockSpec(memory_space=pl.ANY)],
        [block_of(rows), block_of(rows), pl.BlockSpec((rows // T, T * N), lambda j: (0, 0)), block_of(N), block_of(8)],
        (o((rows, ch), bf16), o((rows, ch), f32), o((rows // T, T * N), f32), o((N, ch), f32), o((8, ch), f32)),
        5 * 10**10, nseq=nseq, length=length, unroll=unroll, scratch=state_scratch(nseq, length, unroll),
    )


epsilon = 1e-05
ROWS = 64
PAD = 8


def normalized(tokens, gain):
    wide = tokens.astype(f32)
    return (wide * lax.rsqrt(jnp.mean(wide * wide, axis=1, keepdims=True) + epsilon) * gain).astype(bf16)


def gate_kernel(normed_ref, cot_ref, wg_ref, ow_ref, turned_ref, g_ref, ga_ref, gs_ref, gh_ref, gg_ref):
    rows = normed_ref.shape[0]

    @pl.when(pl.program_id(0) == 0)
    def _():
        turned_ref[...] = normed_ref[...].T

    gh_ref[...] = jnp.dot(normed_ref[...], wg_ref[...], preferred_element_type=f32)
    gg_ref[...] = rows_dot(cot_ref[...], ow_ref[...])

    def mix(i, _):
        at = pl.ds(pl.multiple_of(i * ROWS, ROWS), ROWS)
        gh = gh_ref[at, :]
        gg = gg_ref[at, :]
        sg = sigmoid(gh)
        ga = gh * sg
        gs = gg * (sg * (1.0 + gh * (1.0 - sg)))
        g = gg * ga
        for l in range(NL):
            g_ref[l, at, :] = g[:, lane(l)]
            ga_ref[l, at, :] = ga[:, lane(l)]
            gs_ref[l, at, :] = gs[:, lane(l)]
        return 0

    lax.fori_loop(0, rows // ROWS, mix, 0)


def gate_side(normed, cotangent, in_weight, out_weight):
    rows, model = normed.shape
    inner = out_weight.shape[0]
    first = inner // WIDTH
    tiles = jax.ShapeDtypeStruct((inner // 128, rows, 128), f32)
    return kernel_call(
        gate_kernel, "gate_side", inner,
        (normed, cotangent, in_weight, out_weight),
        [
            whole(normed), whole(cotangent), pl.BlockSpec((model, WIDTH), lambda j: (0, j + first)),
            pl.BlockSpec((WIDTH, model), lambda j: (j, 0)),
        ],
        [pl.BlockSpec((model, rows), lambda j: (0, 0))] + [tiles_of(rows)] * 3,
        (jax.ShapeDtypeStruct((model, rows), bf16), tiles, tiles, tiles),
        4 * rows * model * inner, scratch=[pltpu.VMEM((rows, WIDTH), f32)] * 2,
    )


def filled(weight):
    return jnp.concatenate([weight, jnp.zeros((128 - weight.shape[0], weight.shape[1]), weight.dtype)], axis=0)


def inner_kernel(
    tok_ref, halo_ref, gain_ref, wi_ref, cw_ref, cb_ref, sw_ref,
    normed_ref, inner_ref, before_ref, x_ref, slope_ref, proj_ref, meet_ref, ext_ref, flat_ref, *, nseq, length, rank,
):
    @pl.when(pl.program_id(0) == 0)
    def _():
        def norm(i, _):
            at = pl.ds(pl.multiple_of(i * ROWS, ROWS), ROWS)
            normed_ref[at, :] = normalized(tok_ref[at, :], gain_ref[...])
            return 0

        lax.fori_loop(0, nseq * length // ROWS, norm, 0)

    part = jnp.dot(normed_ref[...], wi_ref[...], preferred_element_type=f32).astype(bf16)
    inner_ref[...] = part
    for s in range(nseq):
        for l in range(NL):
            ext_ref[s, l, PAD:, :] = part[s * length : (s + 1) * length, lane(l)].astype(f32)
    before = jnp.dot(
        normalized(halo_ref[...], gain_ref[...]), wi_ref[...], preferred_element_type=f32
    ).astype(bf16)
    before_ref[...] = before
    for s in range(nseq):
        for l in range(NL):
            ext_ref[s, l, :PAD, :] = before[s * PAD : (s + 1) * PAD, lane(l)].astype(f32)

    @pl.when(pl.program_id(0) == 0)
    def _():
        proj_ref[...] = jnp.zeros_like(proj_ref)

    taps = cw_ref.shape[0]
    for s in range(nseq):

        def mix(i, _):
            r = pl.multiple_of(i * ROWS, ROWS)
            at = pl.ds(pl.multiple_of(s * length + r, ROWS), ROWS)
            for l in range(NL):
                pre = cb_ref[:, lane(l)]
                for k in range(taps):
                    pre = pre + cw_ref[k : k + 1, lane(l)] * ext_ref[s, l, pl.ds(r + PAD - taps + 1 + k, ROWS), :]
                sg = sigmoid(pre)
                x = (pre * sg).astype(bf16)
                slope_ref[at, lane(l)] = sg * (1.0 + pre * (1.0 - sg))
                x_ref[l, at, :] = x
                flat_ref[at, lane(l)] = x
            return 0

        lax.fori_loop(0, length // ROWS, mix, 0)
    proj_ref[...] += rows_dot(flat_ref[...], filled(sw_ref[...]))

    @pl.when(pl.program_id(0) == pl.num_programs(0) - 1)
    def _():
        values = proj_ref[...]
        lanes = lax.broadcasted_iota(jnp.int32, values.shape, 1)
        products = values * pltpu.roll(values, 128 - N, 1)
        own = (lanes >= rank) & (lanes < rank + N)
        total = jnp.sum(jnp.where(own, products, 0.0), axis=1, keepdims=True)
        meet_ref[...] = jnp.broadcast_to(total, meet_ref.shape)


def inner_side(tokens, halo, gain, in_weight, conv_weight, conv_bias, select_weight, nseq, length, rank):
    rows, model = tokens.shape
    picks, inner = select_weight.shape
    o = jax.ShapeDtypeStruct
    operands = (tokens, halo, gain, in_weight, conv_weight, conv_bias, select_weight)
    specs = [
        whole(tokens), whole(halo), whole(gain), block_of(model), block_of(conv_weight.shape[0]), block_of(1),
        block_of(picks),
    ]
    square = pl.BlockSpec((rows, 128), lambda j: (0, 0))
    return pl.pallas_call(
        functools.partial(inner_kernel, nseq=nseq, length=length, rank=rank),
        grid=(inner // WIDTH,),
        in_specs=specs,
        out_specs=[
            pl.BlockSpec((rows, model), lambda j: (0, 0)), block_of(rows), block_of(halo.shape[0]), tiles_of(rows), block_of(rows),
            square, square,
        ],
        out_shape=(
            o((rows, model), bf16), o((rows, inner), bf16), o((halo.shape[0], inner), bf16), o((inner // 128, rows, 128), bf16),
            o((rows, inner), f32), o((rows, 128), f32), o((rows, 128), f32),
        ),
        scratch_shapes=[pltpu.VMEM((nseq, NL, PAD + length, 128), f32), pltpu.VMEM((rows, WIDTH), bf16)],
        compiler_params=pltpu.CompilerParams(vmem_limit_bytes=VMEM, dimension_semantics=("arbitrary",)),
        cost_estimate=pl.CostEstimate(flops=2 * rows * model * inner, bytes_accessed=14 * 2**20, transcendentals=0),
        name="inner_side",
    )(*operands)


def input_grad_kernel(
    place_ref, cp_ref, inner_ref, before_ref, x_ref, slope_ref, pg_ref, sw_ref, cw_ref, turned_ref, halo_ref, gain_ref,
    rl_ref, proj_ref, dlog_ref, rb_ref, sk_ref, *refs, nseq, length, part, rank, grp, last,
):
    if last:
        early_ref, kept_ref, sent_ref, igr_ref, tail_ref, head_ref, pre_ref, back_ref, vec_ref = refs
    else:
        early_ref, (kept_ref, sent_ref, igr_ref, tail_ref, head_ref, small_ref, pre_ref, back_ref, vec_ref) = None, refs
    taps = cw_ref.shape[0]
    j = pl.program_id(0)
    wide = pg_ref.shape[1]
    back_ref[...] = cp_ref[...] + jnp.dot(
        pg_ref[:, wide // 2 :], filled(sw_ref[...]), preferred_element_type=f32
    )
    vec_ref[...] = jnp.zeros_like(vec_ref)
    small_step = 32
    for s in range(nseq):
        pre_ref[s, :, :PAD, :] = jnp.zeros((NL, PAD, 128), f32)
        pre_ref[s, :, PAD + length :, :] = jnp.zeros((NL, PAD, 128), f32)

        def first(i, total):
            r = pl.multiple_of(i * small_step, small_step)
            at = pl.ds(pl.multiple_of(s * length + r, small_step), small_step)
            back = back_ref[at, :] * slope_ref[at, :]
            for l in range(NL):
                pre_ref[s, l, pl.ds(pl.multiple_of(r + PAD, PAD), small_step), :] = back[:, lane(l)]
            return total + sum(back[q * 8 : (q + 1) * 8] for q in range(small_step // 8))

        total = lax.fori_loop(0, length // small_step, first, jnp.zeros((8, WIDTH), f32))
        vec_ref[taps : taps + 1, :] += jnp.sum(total, axis=0, keepdims=True)

        def second(i, totals):
            r = pl.multiple_of(i * small_step, small_step)
            at = pl.ds(pl.multiple_of(s * length + r, small_step), small_step)
            sums = []
            for l in range(NL):
                inner = inner_ref[at, lane(l)].astype(f32)
                result = jnp.zeros((small_step, 128), f32)
                for k in range(taps):
                    later = pre_ref[s, l, pl.ds(r + PAD + taps - 1 - k, small_step), :]
                    result = result + cw_ref[k : k + 1, lane(l)] * later
                    product = inner * later
                    sums.append(
                        totals[l * taps + k] + sum(product[q * 8 : (q + 1) * 8] for q in range(small_step // 8))
                    )
                igr_ref[at, lane(l)] = result.astype(bf16)
            return tuple(sums)

        totals = lax.fori_loop(0, length // small_step, second, (jnp.zeros((8, 128), f32),) * (taps * NL))
        head_rows = lax.broadcasted_iota(jnp.int32, (PAD, 128), 0) < taps - 1
        for l in range(NL):
            late = pre_ref[s, l, length:, :]
            tail_ref[s * PAD : (s + 1) * PAD, lane(l)] = sum(
                cw_ref[k : k + 1, lane(l)] * late[taps - 1 - k : taps - 1 - k + PAD] for k in range(taps)
            )
            lead = pre_ref[s, l, : 2 * PAD, :]
            before = before_ref[s * PAD : (s + 1) * PAD, lane(l)].astype(f32)
            before = jnp.concatenate([before[PAD - taps + 1 :], jnp.zeros((PAD - taps + 1, 128), f32)], axis=0)
            head = jnp.zeros((PAD, 128), f32)
            for k in range(taps):
                early = jnp.where(head_rows, lead[PAD - k : 2 * PAD - k], 0.0)
                head = head + cw_ref[k : k + 1, lane(l)] * early
                vec_ref[k : k + 1, lane(l)] += jnp.sum(totals[l * taps + k] + before * early, axis=0, keepdims=True)
            head_ref[s * PAD : (s + 1) * PAD, lane(l)] = head

    vec_ref[taps + 1 : taps + 2, :] = rb_ref[0:1, :]
    vec_ref[taps + 2 : taps + 3, :] = sk_ref[0:1, :]
    vec_ref[8:, :] = dlog_ref[...]
    count = place_ref.shape[0] - 1
    rows_each = turned_ref.shape[0] // count
    rows_pad = padded(rows_each)
    before_normed = normalized(halo_ref[...], gain_ref[...])
    products = []
    for b in range(WIDTH // wide):
        cols = slice(b * wide, (b + 1) * wide)
        shifted = jnp.concatenate(
            [
                jnp.concatenate(
                    [jnp.zeros((PAD - taps + 1, wide), f32), head_ref[s * PAD : s * PAD + taps - 1, cols]], axis=0
                )
                for s in range(nseq)
            ],
            axis=0,
        )
        product = jnp.dot(turned_ref[...], igr_ref[:, cols], preferred_element_type=f32) + contract_rows(
            before_normed, shifted.astype(bf16)
        )
        products.append(product.astype(bf16) if rows_each == rows_pad else product)
    eye = (
        lax.broadcasted_iota(jnp.int32, (vec_ref.shape[0], wide), 0) + rank
        == lax.broadcasted_iota(jnp.int32, (vec_ref.shape[0], wide), 1)
    ).astype(bf16)
    low = jnp.concatenate([proj_ref[...], jnp.zeros((proj_ref.shape[0], wide - proj_ref.shape[1]), f32)], axis=1)
    low = jnp.where(lax.broadcasted_iota(jnp.int32, low.shape, 1) < rank, low, 0.0).astype(bf16)
    small = (
        contract_rows(joined(x_ref, slice(None)), pg_ref[...])
        + contract_rows(rl_ref[...], low)
        + contract_rows(vec_ref[...].astype(bf16), eye)
    )
    def store(flag):
        half = count // 2
        for q in range(count):
            ref = kept_ref if (q // grp) % 2 == flag else sent_ref
            spot = lax.rem(place_ref[q], half)
            for b, product in enumerate(products):
                at = pl.ds(pl.multiple_of((j * len(products) + b) * rows_pad, rows_pad), rows_pad)
                ref[spot, at, :] = share_rows(product, q, rows_each)

    core = place_ref[count]
    for flag in range(2):
        pl.when(core == flag)(functools.partial(store, flag))
    if not last:
        small_ref[...] = small.astype(small_ref.dtype)
        return
    base = kept_ref.shape[1] - padded(part)

    def place_small(values, first):
        for q in range(WIDTH // part):
            share = place_ref[first + q]
            rows = share_rows(values, q, part)

            @pl.when(share < count // 2)
            def _():
                kept_ref[share, base : base + padded(part), :] = rows

            @pl.when(share >= count // 2)
            def _():
                sent_ref[share - count // 2, base : base + padded(part), :] = rows

    steps = pl.num_programs(0)
    place_small(early_ref[...], j * (WIDTH // part))
    place_small(small, (steps + j) * (WIDTH // part))


def input_grads(
    place, cp, inner, before, x, slope, pg, select_weight, conv_weight, turned, halo, gain, rate_low, proj,
    decay_grad, rate_bias_grad, skip_grad, early, nseq, length, part, rank, grp,
):
    rows, width = cp.shape
    width = width // 2
    last = early is not None
    first = width // WIDTH if last else 0
    wide = pg.shape[1]
    count = place.shape[0] - 1
    model = turned.shape[0]
    packed_rows = (width // wide) * padded(model // count) + (padded(part) if last else 0)
    o = jax.ShapeDtypeStruct

    def drop(spec, first=0):
        return pl.BlockSpec(
            spec.block_shape, lambda j, _, f=spec.index_map: f(j + first), pipeline_mode=spec.pipeline_mode
        )

    specs = [
        block_of(rows), block_of(rows), block_of(before.shape[0]), tiles_of(rows), block_of(rows), whole(pg),
        block_of(select_weight.shape[0]), block_of(conv_weight.shape[0]), whole(turned),
        whole(halo), whole(gain), block_of(rows), whole(proj), block_of(N), block_of(8), block_of(8),
    ]
    packed = pl.BlockSpec((count // 2, packed_rows, wide), lambda j: (0, 0, 0))
    out_specs = [packed, packed, block_of(rows), block_of(nseq * PAD), block_of(nseq * PAD)]
    outs = [
        o((count // 2, packed_rows, wide), bf16), o((count // 2, packed_rows, wide), bf16), o((rows, width), bf16),
        o((nseq * PAD, width), f32), o((nseq * PAD, width), f32),
    ]
    operands = [
        place, cp, inner, before, x, slope, pg, select_weight, conv_weight, turned, halo, gain, rate_low, proj,
        decay_grad, rate_bias_grad, skip_grad,
    ]
    in_specs = [drop(s, first) for s in specs]
    block = pl.BlockSpec((WIDTH, wide), lambda j: (j, 0))
    if last:
        operands.append(early)
        in_specs.append(drop(block))
    else:
        out_specs.append(block)
        outs.append(o((width, wide), f32 if part < 16 else bf16))
    return pl.pallas_call(
        functools.partial(input_grad_kernel, nseq=nseq, length=length, part=part, rank=rank, grp=grp, last=last),
        grid_spec=pltpu.PrefetchScalarGridSpec(
            num_scalar_prefetch=1,
            grid=(width // WIDTH,),
            in_specs=in_specs,
            out_specs=[drop(s) for s in out_specs],
            scratch_shapes=[
                pltpu.VMEM((nseq, NL, PAD + length + PAD, 128), f32), pltpu.VMEM((rows, WIDTH), f32),
                pltpu.VMEM((8 + N, WIDTH), f32),
            ],
        ),
        out_shape=outs,
        compiler_params=pltpu.CompilerParams(vmem_limit_bytes=VMEM, dimension_semantics=("arbitrary",)),
        cost_estimate=pl.CostEstimate(flops=24 * rows * width * model, bytes_accessed=16 * 2**20, transcendentals=0),
        name="input_grads",
    )(*operands)


def padded(rows):
    return max(rows, 16)


def share_rows(values, share, rows):
    taken = values[share * rows : (share + 1) * rows]
    if rows < padded(rows):
        taken = jnp.concatenate([taken, jnp.zeros((padded(rows) - rows, values.shape[1]), values.dtype)], axis=0)
    return taken.astype(bf16)


def weight_grad_kernel(gated_ref, gate_ref, cot_ref, turned_ref, packed_ref, *, part):
    j = pl.program_id(0)
    count = packed_ref.shape[0]
    model = cot_ref.shape[1]
    rows_each = model // count
    rows_pad = padded(rows_each)
    product = contract_rows(gated_ref[...], cot_ref[...])
    for q in range(WIDTH // part):
        packed_ref[j * (WIDTH // part) + q, : padded(part), :] = share_rows(product, q, part)
    product = jnp.dot(turned_ref[...], gate_ref[...], preferred_element_type=f32)
    each = model // WIDTH
    at = pl.ds(pl.multiple_of(padded(part) + (j // each) * rows_pad, 16), rows_pad)
    cols = pl.ds(pl.multiple_of((j % each) * WIDTH, WIDTH), WIDTH)
    for q in range(count):
        packed_ref[q, at, cols] = share_rows(product, q, rows_each)


def weight_grads(gated, gate_grad, cot, turned, part):
    rows, width = gated.shape
    model = cot.shape[1]
    count = width // part
    packed_rows = padded(part) + (width // model) * padded(model // count)
    return pl.pallas_call(
        functools.partial(weight_grad_kernel, part=part),
        grid=(width // WIDTH,),
        in_specs=[block_of(rows), block_of(rows), whole(cot), whole(turned)],
        out_specs=pl.BlockSpec((count, packed_rows, model), lambda j: (0, 0, 0)),
        out_shape=jax.ShapeDtypeStruct((count, packed_rows, model), bf16),
        compiler_params=pltpu.CompilerParams(vmem_limit_bytes=VMEM, dimension_semantics=("arbitrary",)),
        cost_estimate=pl.CostEstimate(flops=4 * rows * width * model, bytes_accessed=14 * 2**20, transcendentals=0),
        name="weight_grads",
    )(gated, gate_grad, cot, turned)


def share_kernel(place_ref, *refs, count, rank, taps, part, part_rows, picks):
    first, second = refs[:count], refs[count : 2 * count]
    summed_ref, weight_ref, gain_ref = refs[2 * count : 2 * count + 3]
    in_ref, out_ref, conv_ref, bias_ref, select_ref, rate_ref, rate_bias_ref, decay_ref, skip_ref, norm_ref = refs[
        2 * count + 3 :
    ]
    pad = padded(part_rows)
    wide = first[0].shape[2]
    model = summed_ref.shape[1]
    each = first[0].shape[1] // pad

    def total(held, at, rows):
        return sum(h[0, at : at + rows, :].astype(f32) for h in held)

    for half, held in enumerate((first, second)):
        for b in range(each):
            at = (half * each + b) * wide
            in_ref[:, at : at + wide] = total(held, b * pad, pad)[:part_rows]
    gate_at = 2 * each * wide
    for b in range((in_ref.shape[1] - gate_at) // model):
        at = padded(part) + b * pad
        in_ref[:, gate_at + b * model : gate_at + (b + 1) * model] = summed_ref[at : at + pad, :][:part_rows].astype(f32)
    out_ref[...] = summed_ref[: padded(part), :][:part].astype(f32)
    gain = jnp.sum(weight_ref[...].astype(f32) * in_ref[...], axis=1, keepdims=True)
    gain = jnp.broadcast_to(gain, (part_rows, 128))
    if part_rows < 8:
        gain = jnp.concatenate([gain, jnp.zeros((8 - part_rows, 128), f32)], axis=0)
    gains = gain_ref[...]
    gains = pltpu.roll(gains, gains.shape[1] - place_ref[0] * part_rows, 1)
    norm_ref[...] = gain.T[:1, :part_rows] / gains[:, :part_rows]
    small = total(second, each * pad, padded(part))[:part]
    turned = small[:, : wide // 2].T
    rate_ref[...] = turned[:rank]
    conv_ref[...] = turned[rank : rank + taps]
    bias_ref[...] = turned[rank + taps : rank + taps + 1]
    rate_bias_ref[...] = turned[rank + taps + 1 : rank + taps + 2]
    skip_ref[...] = turned[rank + taps + 2 : rank + taps + 3]
    decay_ref[...] = turned[rank + 8 : rank + 8 + N]
    select_ref[...] = small[:, wide // 2 : wide // 2 + picks]


def shares_of(first, second, summed, in_weight, gain, place, rank, taps, part, part_rows, picks):
    width = in_weight.shape[1]
    model = summed.shape[1]
    o = lambda *shape: jax.ShapeDtypeStruct(shape, f32)
    own = pl.BlockSpec((part_rows, width), lambda i, s: (s[0], 0))
    if part_rows % 16:
        in_weight = lax.dynamic_slice_in_dim(in_weight, place * part_rows, part_rows, 0)
        own = pl.BlockSpec((part_rows, width), lambda i, s: (0, 0))
    fixed = lambda shape: pl.BlockSpec(shape, lambda i, s: (0,) * len(shape))
    arrays = (*first, *second, summed, in_weight, gain)
    specs = [fixed(a.shape) for a in arrays]
    specs[-2] = own
    outs = (
        o(part_rows, width), o(part, model), o(taps, part), o(1, part), o(part, picks), o(rank, part), o(1, part),
        o(N, part), o(1, part), o(1, part_rows),
    )
    return pl.pallas_call(
        functools.partial(
            share_kernel, count=len(first), rank=rank, taps=taps, part=part, part_rows=part_rows, picks=picks
        ),
        grid_spec=pltpu.PrefetchScalarGridSpec(
            num_scalar_prefetch=1, grid=(1,), in_specs=specs, out_specs=[fixed(out.shape) for out in outs],
        ),
        out_shape=outs,
        compiler_params=pltpu.CompilerParams(vmem_limit_bytes=VMEM, dimension_semantics=("arbitrary",)),
        name="shares",
    )(place[None].astype(jnp.int32), *arrays)


def flip_bit(axis, bit):
    return [(i, i ^ bit) for i in range(lax.axis_size(axis))]


def bits_of(axis):
    size = lax.axis_size(axis)
    return [(axis, 1 << k) for k in range(size.bit_length() - 1)]


def places(order):
    grp = lax.axis_size("grp")
    other = jnp.arange(lax.axis_size("seq") * grp) ^ (lax.axis_index("seq") * grp + lax.axis_index("grp"))
    position = jnp.zeros_like(other)
    for axis, bit in order:
        position = 2 * position + (other // (bit * grp if axis == "seq" else bit)) % 2
    return position.astype(jnp.int32)


def pairs_of(bits):
    return [bits[i : i + 2] for i in range(0, len(bits), 2)]


def round_parts(held, bits):
    count = 1 << len(bits)
    size = held[0].shape[0] // count
    parts = [sum(h[i * size : (i + 1) * size].astype(f32) for h in held) for i in range(count)]
    return parts[:1] + [part.astype(bf16) for part in parts[1:]]


def round_trade(parts, bits):
    held = parts[:1]
    for i in range(1, len(parts)):
        flip = sum(bit for at, (axis, bit) in enumerate(bits) if (i >> (len(bits) - 1 - at)) & 1)
        held.append(lax.ppermute(parts[i], bits[0][0], flip_bit(bits[0][0], flip)))
    return held


def sum_packed(kept, sent, rounds, later):
    axis, bit = rounds[0][0]
    held = [kept, lax.ppermute(sent, axis, flip_bit(axis, bit))]
    for bits in rounds[1:]:
        parts = round_parts(held, bits)
        if later is not None:
            *parts, later = lax.optimization_barrier((*parts, later))
        held = round_trade(parts, bits)
    return held, later


def remaining_rounds(held, rounds, later):
    for bits in rounds:
        parts = round_parts(held, bits)
        if later is not None and bits is rounds[-1]:
            *parts, later = lax.optimization_barrier((*parts, later))
        held = round_trade(parts, bits)
    return held, later


def carried(block, shape, rates, backward, after=None, spans=None):
    count, mine = lax.axis_size("seq"), lax.axis_index("seq")
    blocks = lax.all_gather(block, "seq")
    if after is not None:
        blocks, after = lax.optimization_barrier((blocks, after))
    rows = shape[0] * shape[1]
    entering = jnp.zeros(shape, f32)
    for turn in range(count - 1):
        j = count - 1 - turn if backward else turn
        theirs = blocks[j].astype(f32)
        span = (theirs if spans is None else spans[j].astype(f32))[rows : rows + 2 * shape[0]]
        span = span[: shape[0]] + span[shape[0] :]
        longer = jnp.exp(span[:, None, :] * rates) * entering + theirs[:rows].reshape(shape)
        entering = jnp.where(mine < j if backward else j < mine, longer, entering)
    return entering, after, blocks


def contract_rows(left, right, kind=f32):
    return lax.dot_general(left, right, (((0,), (0,)), ((), ())), preferred_element_type=f32).astype(kind)


def shards(
    tokens,
    cotangent,
    norm_gain,
    in_weight,
    conv_weight,
    conv_bias,
    select_weight,
    rate_weight,
    rate_bias,
    decay_log,
    skip_gain,
    out_weight,
):
    nseq, length, model = tokens.shape
    inner_width = out_weight.shape[0]
    rank = rate_weight.shape[0]
    taps = conv_weight.shape[0]
    rows = nseq * length
    share_count = lax.axis_size("seq") * lax.axis_size("grp")
    tok = tokens.reshape(rows, model)
    cot = cotangent.reshape(rows, model)
    gain, skip, bias = norm_gain[None], skip_gain[None], conv_bias[None]
    pieces, grp = lax.axis_size("seq"), lax.axis_size("grp")
    halo = lax.ppermute(tokens[:, length - PAD :], "seq", [(i, i + 1) for i in range(pieces - 1)])
    halo = halo.reshape(nseq * PAD, model)
    picks, wide = rank + 2 * N, 256
    select_weight = select_weight.T
    normed, inner, before, x, slope, proj, bc = inner_side(
        tok, halo, gain, in_weight, conv_weight, bias, select_weight, nseq, length, rank
    )
    in_gate, out_gate = proj[:, rank : rank + N], proj[:, rank + N : picks]
    log = decay_log.T
    rates = -jnp.exp(log)
    bb = jnp.broadcast_to(in_gate[:, :, None], (rows, N, 128))
    ahead, dl, u = state_end(proj, rate_weight, rate_bias[None], x, log, bb, nseq, length)
    ahead, cot = lax.optimization_barrier((ahead, cot))
    turned, g, ga, gs = gate_side(normed, cot, in_weight, out_weight)
    state_shape = (nseq, N, inner_width)
    entering, _, spans = carried(ahead, state_shape, rates, False)
    cb = jnp.broadcast_to(out_gate[:, :, None], (rows, N, 128))
    sent_back = adjoint_end(dl, g, log, cb, nseq, length)
    lc = spread(out_gate, nseq, length, 1, False)
    lb = spread(in_gate, nseq, length, 2, True)
    ls = jnp.asarray(own_column(nseq * T, T, nseq, 2, 1, True))
    behind, lb, ls, u = lax.optimization_barrier((sent_back, lb, ls, u))
    states, gated, gate_grad, out_grad, shift, skip_grad = forward(
        dl, u, g, ga, gs, x, skip, bb, bc, lc, log, entering, nseq, length, 4
    )
    part, part_rows = inner_width // share_count, model // share_count
    weight_packed = weight_grads(gated, gate_grad, cot, turned, part)
    leaving, weight_packed, _ = carried(behind, state_shape, rates, True, weight_packed, spans)
    weight_sum = lax.psum_scatter(weight_packed, "seq", scatter_dimension=0, tiled=True)
    rate_low, conv_part, in_grad, decay_grad, rate_bias_grad = backward(
        dl, u, g, x, skip, cb, lb, ls, log, leaving, states, nseq, length, 4
    )
    out_grad = out_grad.reshape(rows, N) + in_gate * jnp.sum(shift, axis=1, keepdims=True)
    rank_grad = rows_dot(rate_low, rate_weight)
    pg = jnp.concatenate(
        [
            jnp.zeros((rows, wide // 2), bf16),
            rank_grad.astype(bf16),
            in_grad.reshape(rows, N).astype(bf16),
            out_grad.astype(bf16),
            jnp.zeros((rows, wide // 2 - picks), bf16),
        ],
        axis=1,
    )
    seq_bits, grp_bits = bits_of("seq"), bits_of("grp")
    order = seq_bits + grp_bits
    place = jnp.concatenate([places(order), (lax.axis_index("seq") % 2)[None].astype(jnp.int32)])
    rounds = [seq_bits[:1]] + pairs_of(seq_bits[1:]) + pairs_of(grp_bits)
    half_width = inner_width // 2

    def half(conv_part, early):
        return input_grads(
            place, conv_part, inner, before, x, slope, pg, select_weight, conv_weight, turned, halo, gain, rate_low,
            proj, decay_grad, rate_bias_grad, skip_grad, early, nseq, length, part, rank, grp,
        )

    kept, sent, first_grad, first_tail, first_head, early = half(conv_part, None)
    sent, gated = lax.optimization_barrier((sent, gated))
    wide_tok = tok.astype(f32)
    block_out = wide_tok + jnp.dot(gated, out_weight, preferred_element_type=f32)
    first_held, (conv_part, block_out) = sum_packed(kept, sent, rounds[:2], (conv_part, block_out))
    kept, sent, second_grad, second_tail, second_head = half(conv_part, early)
    head = jnp.concatenate([first_head, second_head], axis=1)
    *first_held, sent, head, weight_sum = lax.optimization_barrier((*first_held, sent, head, weight_sum))
    head = head.reshape(nseq, PAD, inner_width)[:, : taps - 1].astype(bf16)
    returned = lax.ppermute(head, "seq", [(i + 1, i) for i in range(pieces - 1)]).astype(f32)
    held, (gate_grad, *first_held) = sum_packed(kept, sent, rounds[:2], (gate_grad, *first_held))
    normed_grad = rows_dot(gate_grad, in_weight[:, inner_width:])
    *first_held, normed_grad = lax.optimization_barrier((*first_held, normed_grad))
    first_held, _ = remaining_rounds(first_held, rounds[2:], None)
    held, (returned, second_grad, normed_grad, second_tail) = remaining_rounds(
        held, rounds[2:], (returned, second_grad, normed_grad, second_tail)
    )
    weight_share = lax.psum_scatter(weight_sum, "grp", scatter_dimension=0, tiled=True)[0]
    in_share, out_share, conv_share, bias_share, select_share, rate_share, rate_bias_share, decay_share, skip_share, (
        gain_share
    ) = shares_of(
        first_held, held, weight_share, in_weight, gain, lax.axis_index("seq") * grp + lax.axis_index("grp"), rank,
        taps, part, part_rows, picks,
    )
    tail = jnp.concatenate([first_tail, second_tail], axis=1)
    fixed = (tail.reshape(nseq, PAD, inner_width)[:, PAD - taps + 1 :] + returned).astype(bf16)

    def patched(grad, at):
        rows_of = grad.reshape(nseq, length, half_width)
        rows_of = rows_of.at[:, length - taps + 1 :].set(fixed[:, :, at : at + half_width])
        return rows_of.reshape(rows, half_width)

    normed_grad = (
        normed_grad
        + rows_dot(patched(first_grad, 0), in_weight[:, :half_width])
        + rows_dot(patched(second_grad, half_width), in_weight[:, half_width:inner_width])
    )
    scale = lax.rsqrt(jnp.mean(wide_tok * wide_tok, axis=1, keepdims=True) + epsilon)
    lifted = normed_grad * norm_gain
    dots = jnp.mean(lifted * wide_tok, axis=1, keepdims=True)
    tokens_grad = cot.astype(f32) + scale * lifted - wide_tok * (scale * scale * scale) * dots
    return (
        block_out.astype(bf16).reshape(tokens.shape),
        tokens_grad.astype(bf16).reshape(tokens.shape),
        gain_share[0],
        in_share,
        conv_share,
        bias_share[0],
        select_share,
        rate_share,
        rate_bias_share[0],
        decay_share.T,
        skip_share[0],
        out_share,
    )


def solution(mesh):
    sharded = P("grp", "seq", None)
    shares = ("seq", "grp")
    return jax.shard_map(
        shards,
        mesh=mesh,
        in_specs=(sharded, sharded) + (P(),) * 10,
        out_specs=(
            sharded,
            sharded,
            P(shares),
            P(shares, None),
            P(None, shares),
            P(shares),
            P(shares, None),
            P(None, shares),
            P(shares),
            P(shares, None),
            P(shares),
            P(shares, None),
        ),
        check_vma=False,
    )
```

```python
import functools
import math

import jax
import jax.numpy as jnp
import ml_dtypes
import numpy as np
from jax import lax
from jax.experimental import pallas as pl
from jax.experimental.pallas import tpu as pltpu
from jax.sharding import PartitionSpec as P

f32 = jnp.float32
bf16 = jnp.bfloat16
LOG2E = 1.4426950408889634
N = 16
T = 16
WIDTH = 512
NL = WIDTH // 128
VMEM = 60 * 2**20


def lane(l):
    return slice(l * 128, (l + 1) * 128)


def sigmoid(v):
    return pltpu.reciprocal(1.0 + jnp.exp2(v * -LOG2E), approx=True)


def joined(ref, rows):
    return jnp.concatenate([ref[l, rows, :] for l in range(NL)], axis=1)


def steps_of(rows):
    return pl.ds(pl.multiple_of(rows, T), T)


def rows_dot(left, right):
    return lax.dot_general(left, right, (((1,), (1,)), ((), ())), preferred_element_type=f32)


def rates_of(log_ref):
    return -jnp.exp(log_ref[...])


def state_end_kernel(
    proj_ref, rw_ref, rb_ref, x_ref, log_ref, bb_ref, block_ref, dl_ref, u_ref, a2_ref, pre_ref, *, nseq, length,
):
    rows = nseq * length
    a2_ref[...] = rates_of(log_ref) * LOG2E
    low = proj_ref[:, : rw_ref.shape[0]].astype(bf16)
    pre_ref[...] = jnp.dot(low, rw_ref[...], preferred_element_type=f32) + rb_ref[...]

    def steps(i, _):
        r = pl.multiple_of(i * 64, 64)
        at = pl.ds(r, 64)
        pre = pre_ref[at, :]
        d = jnp.maximum(pre, 0.0) + jnp.log(1.0 + jnp.exp(-jnp.abs(pre)))
        for l in range(NL):
            dl_ref[l, at, :] = d[:, lane(l)]
            u_ref[l, at, :] = d[:, lane(l)] * x_ref[l, at, :].astype(f32)
        return 0

    lax.fori_loop(0, rows // 64, steps, 0)
    fill = block_ref.shape[0] - nseq * (N + 2)
    for l in range(NL):
        spans = [
            jnp.sum(dl_ref[l, s * length : (s + 1) * length, :], axis=0, keepdims=True) for s in range(nseq)
        ]
        highs = [span.astype(bf16).astype(f32) for span in spans]
        lows = [span - high for span, high in zip(spans, highs)]
        rows_of = jnp.concatenate(highs + lows + [jnp.zeros((fill, 128), f32)], axis=0)
        block_ref[nseq * N :, lane(l)] = rows_of.astype(bf16)

    def step(c, h):
        h = [list(v) for v in h]
        for k in range(T):
            for s in range(nseq):
                t = s * length + c * T + k
                bt = bb_ref[t]
                for l in range(NL):
                    f = jnp.exp2(dl_ref[l, pl.ds(t, 1), :] * a2_ref[:, lane(l)])
                    h[s][l] = f * h[s][l] + u_ref[l, pl.ds(t, 1), :] * bt
        return tuple(tuple(v) for v in h)

    z = jnp.zeros((N, 128), f32)
    h = lax.fori_loop(0, length // T, step, ((z,) * NL,) * nseq)
    for s in range(nseq):
        for l in range(NL):
            block_ref[s * N : (s + 1) * N, lane(l)] = h[s][l].astype(bf16)


def adjoint_end_kernel(dl_ref, g_ref, log_ref, cb_ref, sb_ref, a2_ref, *, nseq, length):
    a2_ref[...] = rates_of(log_ref) * LOG2E
    nch = length // T

    def step(m, lam):
        lam = [list(v) for v in lam]
        c = nch - 1 - m
        for k in reversed(range(T)):
            for s in range(nseq):
                t = s * length + c * T + k
                ct = cb_ref[t]
                for l in range(NL):
                    f = jnp.exp2(dl_ref[l, pl.ds(t, 1), :] * a2_ref[:, lane(l)])
                    lam[s][l] = f * (lam[s][l] + g_ref[l, pl.ds(t, 1), :] * ct)
        return tuple(tuple(v) for v in lam)

    z = jnp.zeros((N, 128), f32)
    lam = lax.fori_loop(0, nch, step, ((z,) * NL,) * nseq)
    for s in range(nseq):
        for l in range(NL):
            sb_ref[s * N : (s + 1) * N, lane(l)] = lam[s][l].astype(bf16)


def state_copy(states_ref, held_ref, sems, at, q, s, length, unroll, out):
    size = unroll * T * N
    rows = pl.ds(pl.multiple_of(s * length * N + q * size, size), size)
    far = states_ref.at[rows, pl.ds(pl.multiple_of(at * WIDTH, WIDTH), WIDTH)]
    near = held_ref.at[s, q]
    return pltpu.make_async_copy(near, far, sems.at[s, q]) if out else pltpu.make_async_copy(far, near, sems.at[s, q])


def state_scratch(nseq, length, unroll):
    groups = length // (T * unroll)
    return [
        pltpu.VMEM((N, WIDTH), f32), pltpu.VMEM((nseq, groups, unroll * T * N, WIDTH), bf16),
        pltpu.SemaphoreType.DMA((nseq, groups)),
    ]


def forward_kernel(
    dl_ref, u_ref, g_ref, ga_ref, gs_ref, x_ref, skip_ref, bb_ref, bc_ref, lc_ref, log_ref, hin_ref,
    hb_ref, gated_ref, ggr_ref, outg_ref, gu_ref, sk_ref, a2_ref, held_ref, sems, *, nseq, length, unroll,
):
    a2_ref[...] = rates_of(log_ref) * LOG2E
    nch = length // T
    skip = skip_ref[...]
    ones = jnp.ones((8, 128), bf16)

    @pl.when(pl.program_id(0) == 0)
    def _():
        outg_ref[...] = jnp.zeros_like(outg_ref)
        gu_ref[...] = jnp.zeros_like(gu_ref)

    step_at, last_step = pl.program_id(0), pl.num_programs(0) - 1

    def leaving(at, q, s):
        return state_copy(hb_ref, held_ref, sems, at, q, s, length, unroll, True)

    def chunk(c, p, q, h, acc):
        hbv, pov = {}, [[None] * T for _ in range(nseq)]
        for k in range(T):
            for s in range(nseq):
                t = s * length + c * T + k
                bt = bb_ref[t]
                po = None
                for l in range(NL):
                    g = jnp.broadcast_to(g_ref[l, pl.ds(t, 1), :], (N, 128)).astype(bf16)
                    f = jnp.exp2(dl_ref[l, pl.ds(t, 1), :] * a2_ref[:, lane(l)])
                    held = f * h[s][l]
                    h[s][l] = held + u_ref[l, pl.ds(t, 1), :] * bt
                    hb = held.astype(bf16)
                    held_ref[s, q, (p * T + k) * N : (p * T + k + 1) * N, lane(l)] = hb
                    hbv[k, s, l] = hb
                    po = hb * g if po is None else po + hb * g
                pov[s][k] = po
        lhs = jnp.concatenate([lc_ref[steps_of(s * length + c * T), :] for s in range(nseq)], axis=0)
        parts = []
        for l in range(0, NL, 2):
            rhs = jnp.concatenate(
                [
                    jnp.concatenate([hbv[k, s, l], hbv[k, s, l + 1]], axis=1)
                    for k in range(T) for s in range(nseq)
                ],
                axis=0,
            )
            parts.append(jnp.dot(lhs, rhs, preferred_element_type=f32))
        sc_all = jnp.concatenate(parts, axis=1)
        for s in range(nseq):
            og = rows_dot(ones, jnp.concatenate(pov[s], axis=0))
            outg_ref[pl.ds(s * nch + c, 1), :] += og[:1]
            at = steps_of(s * length + c * T)
            x = joined(x_ref, at).astype(f32)
            gx = joined(g_ref, at) * x
            d = joined(dl_ref, at)
            bc = jnp.concatenate([bc_ref[at, :]] * NL, axis=1)
            mo = sc_all[s * T : (s + 1) * T] + (d * bc + skip) * x
            gu = gx * d
            gu_ref[at, :] += sum(gu[:, lane(l)] for l in range(NL))
            gated_ref[at, :] = (mo * joined(ga_ref, at).astype(f32)).astype(bf16)
            ggr_ref[at, :] = (mo * joined(gs_ref, at).astype(f32)).astype(bf16)
            acc = acc + gx
        return acc

    def step(i, carry):
        h, acc = carry
        h = [list(v) for v in h]
        @pl.when(step_at > 0)
        def _():
            for s in range(nseq):
                leaving(step_at - 1, i, s).wait()

        for p in range(unroll):
            acc = chunk(i * unroll + p, p, i, h, acc)
        for s in range(nseq):
            leaving(step_at, i, s).start()
        return tuple(tuple(v) for v in h), acc

    h0 = tuple(tuple(hin_ref[s, :, lane(l)] for l in range(NL)) for s in range(nseq))
    _, acc = lax.fori_loop(0, nch // unroll, step, (h0, jnp.zeros((T, WIDTH), f32)))
    sk_ref[...] = jnp.broadcast_to(jnp.sum(acc, axis=0, keepdims=True), sk_ref.shape)

    @pl.when(step_at == last_step)
    def _():
        for q in range(nch // unroll):
            for s in range(nseq):
                leaving(step_at, q, s).wait()


def backward_kernel(
    dl_ref, u_ref, g_ref, x_ref, skip_ref, cb_ref, lb_ref, ls_ref, log_ref, lin_ref, hb_ref,
    rl_ref, cp_ref, ing_ref, dlog_ref, rb_ref, a2_ref, held_ref, sems, *, nseq, length, unroll,
):
    a2_ref[...] = rates_of(log_ref) * LOG2E
    nch = length // T
    abf = rates_of(log_ref).astype(bf16)
    skip = skip_ref[...]
    ones = jnp.ones((8, 128), bf16)

    @pl.when(pl.program_id(0) == 0)
    def _():
        ing_ref[...] = jnp.zeros_like(ing_ref)

    step_at, last_step = pl.program_id(0), pl.num_programs(0) - 1
    groups = nch // unroll

    def arriving(at, q, s):
        return state_copy(hb_ref, held_ref, sems, at, q, s, length, unroll, False)

    @pl.when(step_at == 0)
    def _():
        for q in reversed(range(groups)):
            for s in range(nseq):
                arriving(0, q, s).start()

    def chunk(c, p, group, lam, dlog, rb):
        pov = [[None] * T for _ in range(nseq)]
        dacc = [None] * NL
        vals = {}
        for k in reversed(range(T)):
            for s in range(nseq):
                t = s * length + c * T + k
                ct = cb_ref[t]
                po = None
                for l in range(NL):
                    d = jnp.broadcast_to(dl_ref[l, pl.ds(t, 1), :], (N, 128))
                    u = jnp.broadcast_to(u_ref[l, pl.ds(t, 1), :], (N, 128)).astype(bf16)
                    a = g_ref[l, pl.ds(t, 1), :] * ct + lam[s][l]
                    lam[s][l] = jnp.exp2(d * a2_ref[:, lane(l)]) * a
                    ab = a.astype(bf16)
                    q = ab * held_ref[s, group, (p * T + k) * N : (p * T + k + 1) * N, lane(l)] * abf[:, lane(l)]
                    qd = q * d.astype(bf16)
                    vals[k, s, l] = (ab, q)
                    dacc[l] = qd if dacc[l] is None else dacc[l] + qd
                    po = ab * u if po is None else po + ab * u
                pov[s][k] = po
            if k % 8 == 0:
                for l in range(NL):
                    dlog[l] = dlog[l] + dacc[l].astype(f32)
                    dacc[l] = None
        lhs = jnp.concatenate(
            [lb_ref[steps_of(s * length + c * T), :] for s in range(nseq)] + [ls_ref[...]], axis=0
        )
        parts = []
        for l in range(0, NL, 2):
            rhs = jnp.concatenate(
                [
                    jnp.concatenate([vals[k, s, l][y], vals[k, s, l + 1][y]], axis=1)
                    for k in reversed(range(T)) for s in range(nseq) for y in range(2)
                ],
                axis=0,
            )
            parts.append(jnp.dot(lhs, rhs, preferred_element_type=f32))
        both = jnp.concatenate(parts, axis=1)
        for s in range(nseq):
            w = both[s * T : (s + 1) * T]
            qs = both[(nseq + s) * T : (nseq + s + 1) * T]
            ig = rows_dot(ones, jnp.concatenate(pov[s], axis=0))
            ing_ref[pl.ds(s * nch + c, 1), :] += ig[:1]
            at = steps_of(s * length + c * T)
            d = joined(dl_ref, at)
            rg = (qs + w * joined(x_ref, at).astype(f32)) * (1.0 - jnp.exp(-d))
            rb = rb + rg
            rl_ref[at, :] = rg.astype(bf16)
            cp_ref[at, :] = w * d + skip * joined(g_ref, at)
        return rb

    def step(m, carry):
        lam, dlog, rb = carry
        lam = [list(v) for v in lam]
        dlog = list(dlog)
        q = groups - 1 - m
        for s in range(nseq):
            arriving(step_at, q, s).wait()
        for p in reversed(range(unroll)):
            rb = chunk(q * unroll + p, p, q, lam, dlog, rb)

        @pl.when(step_at < last_step)
        def _():
            for s in range(nseq):
                arriving(step_at + 1, q, s).start()

        return tuple(tuple(v) for v in lam), tuple(dlog), rb

    l0 = tuple(tuple(lin_ref[s, :, lane(l)] for l in range(NL)) for s in range(nseq))
    z = jnp.zeros((N, 128), f32)
    _, dlog, rb = lax.fori_loop(0, nch // unroll, step, (l0, (z,) * NL, jnp.zeros((T, WIDTH), f32)))
    for l in range(NL):
        dlog_ref[:, lane(l)] = dlog[l]
    rb_ref[...] = jnp.broadcast_to(jnp.sum(rb, axis=0, keepdims=True), rb_ref.shape)


def block_of(rows):
    return pl.BlockSpec((rows, WIDTH), lambda j: (0, j))


def tiles_of(rows):
    return pl.BlockSpec((NL, rows, 128), lambda j: (j, 0, 0))


def states_of(nseq):
    return pl.BlockSpec((nseq, N, WIDTH), lambda j: (0, 0, j))


def whole(a):
    return pl.BlockSpec(a.shape, lambda j: (0,) * a.ndim, pipeline_mode=pl.Buffered(1))


def kernel_call(body, name, channels, operands, specs, out_specs, outs, flops, scratch=(), **options):
    moved = sum(a.size * a.dtype.itemsize for a in operands) + sum(
        math.prod(o.shape) * o.dtype.itemsize for o in outs
    )
    return pl.pallas_call(
        functools.partial(body, **options),
        grid=(channels // WIDTH,),
        in_specs=specs,
        out_specs=out_specs,
        out_shape=outs,
        scratch_shapes=scratch,
        compiler_params=pltpu.CompilerParams(vmem_limit_bytes=VMEM, dimension_semantics=("arbitrary",)),
        cost_estimate=pl.CostEstimate(flops=flops, bytes_accessed=moved, transcendentals=0),
        name=name,
    )(*operands)


def spread(values, nseq, length, kinds, reverse):
    mask = own_column(nseq * length, length, nseq, kinds, 0, reverse)
    width = mask.shape[1]
    pick = (np.arange(width)[None, :] % N == np.arange(N)[:, None]).astype(ml_dtypes.bfloat16)
    wide = jnp.dot(values.astype(bf16), pick, preferred_element_type=f32)
    return wide.astype(bf16) * mask


def own_column(rows, length, nseq, kinds, kind, reverse):
    column = np.arange(T * nseq * kinds * N)[None, :]
    row = np.arange(rows)[:, None]
    step = column // (nseq * kinds * N)
    if reverse:
        step = T - 1 - step
    own = (step == row % T) & ((column // (kinds * N)) % nseq == row // length) & ((column // N) % kinds == kind)
    return own.astype(ml_dtypes.bfloat16)


def block_rows(nseq):
    return -(-nseq * (N + 2) // 16) * 16


def state_end(proj, rate_weight, rate_bias, x, log, bb, nseq, length):
    tiles, rows, _ = x.shape
    ch = tiles * 128
    o = jax.ShapeDtypeStruct
    return kernel_call(
        state_end_kernel, "state_end", ch,
        (proj, rate_weight, rate_bias, x, log, bb),
        [whole(proj), block_of(rate_weight.shape[0]), block_of(1), tiles_of(rows), block_of(N), whole(bb)],
        [block_of(block_rows(nseq)), tiles_of(rows), tiles_of(rows)],
        (o((block_rows(nseq), ch), bf16), o(x.shape, f32), o(x.shape, f32)),
        2 * 10**10, nseq=nseq, length=length,
        scratch=[pltpu.VMEM((N, WIDTH), f32), pltpu.VMEM((rows, WIDTH), f32)],
    )


def adjoint_end(dl, g, log, cb, nseq, length):
    tiles, rows, _ = dl.shape
    ch = tiles * 128
    return kernel_call(
        adjoint_end_kernel, "adjoint_end", ch,
        (dl, g, log, cb),
        [tiles_of(rows), tiles_of(rows), block_of(N), whole(cb)],
        [block_of(nseq * N)],
        (jax.ShapeDtypeStruct((nseq * N, ch), bf16),),
        2 * 10**10, nseq=nseq, length=length, scratch=[pltpu.VMEM((N, WIDTH), f32)],
    )[0]


def forward(dl, u, g, ga, gs, x, skip, bb, bc, lc, log, hin, nseq, length, unroll=1):
    tiles, rows, _ = dl.shape
    ch = tiles * 128
    o = jax.ShapeDtypeStruct
    t = tiles_of(rows)
    return kernel_call(
        forward_kernel, "forward", ch,
        (dl, u, g, ga, gs, x, skip, bb, bc, lc, log, hin),
        [t, t, t, t, t, t, block_of(1), whole(bb), whole(bc), whole(lc), block_of(N), states_of(nseq)],
        [
            pl.BlockSpec(memory_space=pl.ANY), block_of(rows), block_of(rows), pl.BlockSpec((rows // T, T * N), lambda j: (0, 0)),
            pl.BlockSpec((rows, 128), lambda j: (0, 0)), block_of(8),
        ],
        (
            o((rows * N, ch), bf16), o((rows, ch), bf16), o((rows, ch), bf16), o((rows // T, T * N), f32),
            o((rows, 128), f32), o((8, ch), f32),
        ),
        3 * 10**10, nseq=nseq, length=length, unroll=unroll, scratch=state_scratch(nseq, length, unroll),
    )


def backward(dl, u, g, x, skip, cb, lb, ls, log, lin, hb, nseq, length, unroll=1):
    tiles, rows, _ = dl.shape
    ch = tiles * 128
    o = jax.ShapeDtypeStruct
    t = tiles_of(rows)
    st = states_of(nseq)
    return kernel_call(
        backward_kernel, "backward", ch,
        (dl, u, g, x, skip, cb, lb, ls, log, lin, hb),
        [t, t, t, t, block_of(1), whole(cb), whole(lb), whole(ls), block_of(N), st, pl.BlockSpec(memory_space=pl.ANY)],
        [block_of(rows), block_of(rows), pl.BlockSpec((rows // T, T * N), lambda j: (0, 0)), block_of(N), block_of(8)],
        (o((rows, ch), bf16), o((rows, ch), f32), o((rows // T, T * N), f32), o((N, ch), f32), o((8, ch), f32)),
        5 * 10**10, nseq=nseq, length=length, unroll=unroll, scratch=state_scratch(nseq, length, unroll),
    )


epsilon = 1e-05
ROWS = 64
PAD = 8


def normalized(tokens, gain):
    wide = tokens.astype(f32)
    return (wide * lax.rsqrt(jnp.mean(wide * wide, axis=1, keepdims=True) + epsilon) * gain).astype(bf16)


def gate_kernel(normed_ref, cot_ref, wg_ref, ow_ref, turned_ref, g_ref, ga_ref, gs_ref, gh_ref, gg_ref):
    rows = normed_ref.shape[0]

    @pl.when(pl.program_id(0) == 0)
    def _():
        turned_ref[...] = normed_ref[...].T

    gh_ref[...] = jnp.dot(normed_ref[...], wg_ref[...], preferred_element_type=f32)
    gg_ref[...] = rows_dot(cot_ref[...], ow_ref[...])

    def mix(i, _):
        at = pl.ds(pl.multiple_of(i * ROWS, ROWS), ROWS)
        gh = gh_ref[at, :]
        gg = gg_ref[at, :]
        sg = sigmoid(gh)
        ga = gh * sg
        gs = gg * (sg * (1.0 + gh * (1.0 - sg)))
        g = gg * ga
        for l in range(NL):
            g_ref[l, at, :] = g[:, lane(l)]
            ga_ref[l, at, :] = ga[:, lane(l)].astype(bf16)
            gs_ref[l, at, :] = gs[:, lane(l)].astype(bf16)
        return 0

    lax.fori_loop(0, rows // ROWS, mix, 0)


def gate_side(normed, cotangent, in_weight, out_weight):
    rows, model = normed.shape
    inner = out_weight.shape[0]
    first = inner // WIDTH
    tiles = jax.ShapeDtypeStruct((inner // 128, rows, 128), f32)
    narrow = jax.ShapeDtypeStruct(tiles.shape, bf16)
    return kernel_call(
        gate_kernel, "gate_side", inner,
        (normed, cotangent, in_weight, out_weight),
        [
            whole(normed), whole(cotangent), pl.BlockSpec((model, WIDTH), lambda j: (0, j + first)),
            pl.BlockSpec((WIDTH, model), lambda j: (j, 0)),
        ],
        [pl.BlockSpec((model, rows), lambda j: (0, 0))] + [tiles_of(rows)] * 3,
        (jax.ShapeDtypeStruct((model, rows), bf16), tiles, narrow, narrow),
        4 * rows * model * inner, scratch=[pltpu.VMEM((rows, WIDTH), f32)] * 2,
    )


def filled(weight):
    return jnp.concatenate([weight, jnp.zeros((128 - weight.shape[0], weight.shape[1]), weight.dtype)], axis=0)


def inner_kernel(
    tok_ref, halo_ref, gain_ref, wi_ref, cw_ref, cb_ref, sw_ref,
    normed_ref, inner_ref, before_ref, x_ref, slope_ref, proj_ref, meet_ref, ext_ref, flat_ref, *, nseq, length, rank,
):
    @pl.when(pl.program_id(0) == 0)
    def _():
        def norm(i, _):
            at = pl.ds(pl.multiple_of(i * ROWS, ROWS), ROWS)
            normed_ref[at, :] = normalized(tok_ref[at, :], gain_ref[...])
            return 0

        lax.fori_loop(0, nseq * length // ROWS, norm, 0)

    part = jnp.dot(normed_ref[...], wi_ref[...], preferred_element_type=f32).astype(bf16)
    inner_ref[...] = part
    for s in range(nseq):
        for l in range(NL):
            ext_ref[s, l, PAD:, :] = part[s * length : (s + 1) * length, lane(l)].astype(f32)
    before = jnp.dot(
        normalized(halo_ref[...], gain_ref[...]), wi_ref[...], preferred_element_type=f32
    ).astype(bf16)
    before_ref[...] = before
    for s in range(nseq):
        for l in range(NL):
            ext_ref[s, l, :PAD, :] = before[s * PAD : (s + 1) * PAD, lane(l)].astype(f32)

    @pl.when(pl.program_id(0) == 0)
    def _():
        proj_ref[...] = jnp.zeros_like(proj_ref)

    taps = cw_ref.shape[0]
    for s in range(nseq):

        def mix(i, _):
            r = pl.multiple_of(i * ROWS, ROWS)
            at = pl.ds(pl.multiple_of(s * length + r, ROWS), ROWS)
            for l in range(NL):
                pre = cb_ref[:, lane(l)]
                for k in range(taps):
                    pre = pre + cw_ref[k : k + 1, lane(l)] * ext_ref[s, l, pl.ds(r + PAD - taps + 1 + k, ROWS), :]
                sg = sigmoid(pre)
                x = (pre * sg).astype(bf16)
                slope_ref[at, lane(l)] = (sg * (1.0 + pre * (1.0 - sg))).astype(bf16)
                x_ref[l, at, :] = x
                flat_ref[at, lane(l)] = x
            return 0

        lax.fori_loop(0, length // ROWS, mix, 0)
    proj_ref[...] += rows_dot(flat_ref[...], filled(sw_ref[...]))

    @pl.when(pl.program_id(0) == pl.num_programs(0) - 1)
    def _():
        values = proj_ref[...]
        lanes = lax.broadcasted_iota(jnp.int32, values.shape, 1)
        products = values * pltpu.roll(values, 128 - N, 1)
        own = (lanes >= rank) & (lanes < rank + N)
        total = jnp.sum(jnp.where(own, products, 0.0), axis=1, keepdims=True)
        meet_ref[...] = jnp.broadcast_to(total, meet_ref.shape)


def inner_side(tokens, halo, gain, in_weight, conv_weight, conv_bias, select_weight, nseq, length, rank):
    rows, model = tokens.shape
    picks, inner = select_weight.shape
    o = jax.ShapeDtypeStruct
    operands = (tokens, halo, gain, in_weight, conv_weight, conv_bias, select_weight)
    specs = [
        whole(tokens), whole(halo), whole(gain), block_of(model), block_of(conv_weight.shape[0]), block_of(1),
        block_of(picks),
    ]
    square = pl.BlockSpec((rows, 128), lambda j: (0, 0))
    return pl.pallas_call(
        functools.partial(inner_kernel, nseq=nseq, length=length, rank=rank),
        grid=(inner // WIDTH,),
        in_specs=specs,
        out_specs=[
            pl.BlockSpec((rows, model), lambda j: (0, 0)), block_of(rows), block_of(halo.shape[0]), tiles_of(rows), block_of(rows),
            square, square,
        ],
        out_shape=(
            o((rows, model), bf16), o((rows, inner), bf16), o((halo.shape[0], inner), bf16), o((inner // 128, rows, 128), bf16),
            o((rows, inner), bf16), o((rows, 128), f32), o((rows, 128), f32),
        ),
        scratch_shapes=[pltpu.VMEM((nseq, NL, PAD + length, 128), f32), pltpu.VMEM((rows, WIDTH), bf16)],
        compiler_params=pltpu.CompilerParams(vmem_limit_bytes=VMEM, dimension_semantics=("arbitrary",)),
        cost_estimate=pl.CostEstimate(flops=2 * rows * model * inner, bytes_accessed=14 * 2**20, transcendentals=0),
        name="inner_side",
    )(*operands)


def input_grad_kernel(
    place_ref, cp_ref, inner_ref, before_ref, x_ref, slope_ref, pg_ref, sw_ref, cw_ref, turned_ref, halo_ref, gain_ref,
    rl_ref, proj_ref, dlog_ref, rb_ref, sk_ref, *refs, nseq, length, part, rank, grp, last,
):
    if last:
        early_ref, kept_ref, sent_ref, igr_ref, tail_ref, head_ref, pre_ref, back_ref, vec_ref = refs
    else:
        early_ref, (kept_ref, sent_ref, igr_ref, tail_ref, head_ref, small_ref, pre_ref, back_ref, vec_ref) = None, refs
    taps = cw_ref.shape[0]
    j = pl.program_id(0)
    wide = pg_ref.shape[1]
    back_ref[...] = cp_ref[...] + jnp.dot(
        pg_ref[:, wide // 2 :], filled(sw_ref[...]), preferred_element_type=f32
    )
    vec_ref[...] = jnp.zeros_like(vec_ref)
    small_step = 32
    for s in range(nseq):
        pre_ref[s, :, :PAD, :] = jnp.zeros((NL, PAD, 128), f32)
        pre_ref[s, :, PAD + length :, :] = jnp.zeros((NL, PAD, 128), f32)

        def first(i, total):
            r = pl.multiple_of(i * small_step, small_step)
            at = pl.ds(pl.multiple_of(s * length + r, small_step), small_step)
            back = back_ref[at, :] * slope_ref[at, :].astype(f32)
            for l in range(NL):
                pre_ref[s, l, pl.ds(pl.multiple_of(r + PAD, PAD), small_step), :] = back[:, lane(l)]
            return total + sum(back[q * 8 : (q + 1) * 8] for q in range(small_step // 8))

        total = lax.fori_loop(0, length // small_step, first, jnp.zeros((8, WIDTH), f32))
        vec_ref[taps : taps + 1, :] += jnp.sum(total, axis=0, keepdims=True)

        def second(i, totals):
            r = pl.multiple_of(i * small_step, small_step)
            at = pl.ds(pl.multiple_of(s * length + r, small_step), small_step)
            sums = []
            for l in range(NL):
                inner = inner_ref[at, lane(l)].astype(f32)
                result = jnp.zeros((small_step, 128), f32)
                for k in range(taps):
                    later = pre_ref[s, l, pl.ds(r + PAD + taps - 1 - k, small_step), :]
                    result = result + cw_ref[k : k + 1, lane(l)] * later
                    product = inner * later
                    sums.append(
                        totals[l * taps + k] + sum(product[q * 8 : (q + 1) * 8] for q in range(small_step // 8))
                    )
                igr_ref[at, lane(l)] = result.astype(bf16)
            return tuple(sums)

        totals = lax.fori_loop(0, length // small_step, second, (jnp.zeros((8, 128), f32),) * (taps * NL))
        head_rows = lax.broadcasted_iota(jnp.int32, (PAD, 128), 0) < taps - 1
        for l in range(NL):
            late = pre_ref[s, l, length:, :]
            tail_ref[s * PAD : (s + 1) * PAD, lane(l)] = sum(
                cw_ref[k : k + 1, lane(l)] * late[taps - 1 - k : taps - 1 - k + PAD] for k in range(taps)
            )
            lead = pre_ref[s, l, : 2 * PAD, :]
            before = before_ref[s * PAD : (s + 1) * PAD, lane(l)].astype(f32)
            before = jnp.concatenate([before[PAD - taps + 1 :], jnp.zeros((PAD - taps + 1, 128), f32)], axis=0)
            head = jnp.zeros((PAD, 128), f32)
            for k in range(taps):
                early = jnp.where(head_rows, lead[PAD - k : 2 * PAD - k], 0.0)
                head = head + cw_ref[k : k + 1, lane(l)] * early
                vec_ref[k : k + 1, lane(l)] += jnp.sum(totals[l * taps + k] + before * early, axis=0, keepdims=True)
            head_ref[s * PAD : (s + 1) * PAD, lane(l)] = head

    vec_ref[taps + 1 : taps + 2, :] = rb_ref[0:1, :]
    vec_ref[taps + 2 : taps + 3, :] = sk_ref[0:1, :]
    vec_ref[8:, :] = dlog_ref[...]
    count = place_ref.shape[0] - 1
    rows_each = turned_ref.shape[0] // count
    rows_pad = padded(rows_each)
    before_normed = normalized(halo_ref[...], gain_ref[...])
    products = []
    for b in range(WIDTH // wide):
        cols = slice(b * wide, (b + 1) * wide)
        shifted = jnp.concatenate(
            [
                jnp.concatenate(
                    [jnp.zeros((PAD - taps + 1, wide), f32), head_ref[s * PAD : s * PAD + taps - 1, cols]], axis=0
                )
                for s in range(nseq)
            ],
            axis=0,
        )
        product = jnp.dot(turned_ref[...], igr_ref[:, cols], preferred_element_type=f32) + contract_rows(
            before_normed, shifted.astype(bf16)
        )
        products.append(product.astype(bf16) if rows_each == rows_pad else product)
    eye = (
        lax.broadcasted_iota(jnp.int32, (vec_ref.shape[0], wide), 0) + rank
        == lax.broadcasted_iota(jnp.int32, (vec_ref.shape[0], wide), 1)
    ).astype(bf16)
    low = jnp.concatenate([proj_ref[...], jnp.zeros((proj_ref.shape[0], wide - proj_ref.shape[1]), f32)], axis=1)
    low = jnp.where(lax.broadcasted_iota(jnp.int32, low.shape, 1) < rank, low, 0.0).astype(bf16)
    small = (
        contract_rows(joined(x_ref, slice(None)), pg_ref[...])
        + contract_rows(rl_ref[...], low)
        + contract_rows(vec_ref[...].astype(bf16), eye)
    )
    def store(flag):
        half = count // 2
        for q in range(count):
            ref = kept_ref if (q // grp) % 2 == flag else sent_ref
            spot = lax.rem(place_ref[q], half)
            for b, product in enumerate(products):
                at = pl.ds(pl.multiple_of((j * len(products) + b) * rows_pad, rows_pad), rows_pad)
                ref[spot, at, :] = share_rows(product, q, rows_each)

    core = place_ref[count]
    for flag in range(2):
        pl.when(core == flag)(functools.partial(store, flag))
    if not last:
        small_ref[...] = small.astype(small_ref.dtype)
        return
    base = kept_ref.shape[1] - padded(part)

    def place_small(values, first):
        for q in range(WIDTH // part):
            share = place_ref[first + q]
            rows = share_rows(values, q, part)

            @pl.when(share < count // 2)
            def _():
                kept_ref[share, base : base + padded(part), :] = rows

            @pl.when(share >= count // 2)
            def _():
                sent_ref[share - count // 2, base : base + padded(part), :] = rows

    steps = pl.num_programs(0)
    place_small(early_ref[...], j * (WIDTH // part))
    place_small(small, (steps + j) * (WIDTH // part))


def input_grads(
    place, cp, inner, before, x, slope, pg, select_weight, conv_weight, turned, halo, gain, rate_low, proj,
    decay_grad, rate_bias_grad, skip_grad, early, nseq, length, part, rank, grp,
):
    rows, width = cp.shape
    width = width // 2
    last = early is not None
    first = width // WIDTH if last else 0
    wide = pg.shape[1]
    count = place.shape[0] - 1
    model = turned.shape[0]
    packed_rows = (width // wide) * padded(model // count) + (padded(part) if last else 0)
    o = jax.ShapeDtypeStruct

    def drop(spec, first=0):
        return pl.BlockSpec(
            spec.block_shape, lambda j, _, f=spec.index_map: f(j + first), pipeline_mode=spec.pipeline_mode
        )

    specs = [
        block_of(rows), block_of(rows), block_of(before.shape[0]), tiles_of(rows), block_of(rows), whole(pg),
        block_of(select_weight.shape[0]), block_of(conv_weight.shape[0]), whole(turned),
        whole(halo), whole(gain), block_of(rows), whole(proj), block_of(N), block_of(8), block_of(8),
    ]
    packed = pl.BlockSpec((count // 2, packed_rows, wide), lambda j: (0, 0, 0))
    out_specs = [packed, packed, block_of(rows), block_of(nseq * PAD), block_of(nseq * PAD)]
    outs = [
        o((count // 2, packed_rows, wide), bf16), o((count // 2, packed_rows, wide), bf16), o((rows, width), bf16),
        o((nseq * PAD, width), f32), o((nseq * PAD, width), f32),
    ]
    operands = [
        place, cp, inner, before, x, slope, pg, select_weight, conv_weight, turned, halo, gain, rate_low, proj,
        decay_grad, rate_bias_grad, skip_grad,
    ]
    in_specs = [drop(s, first) for s in specs]
    block = pl.BlockSpec((WIDTH, wide), lambda j: (j, 0))
    if last:
        operands.append(early)
        in_specs.append(drop(block))
    else:
        out_specs.append(block)
        outs.append(o((width, wide), f32 if part < 16 else bf16))
    return pl.pallas_call(
        functools.partial(input_grad_kernel, nseq=nseq, length=length, part=part, rank=rank, grp=grp, last=last),
        grid_spec=pltpu.PrefetchScalarGridSpec(
            num_scalar_prefetch=1,
            grid=(width // WIDTH,),
            in_specs=in_specs,
            out_specs=[drop(s) for s in out_specs],
            scratch_shapes=[
                pltpu.VMEM((nseq, NL, PAD + length + PAD, 128), f32), pltpu.VMEM((rows, WIDTH), f32),
                pltpu.VMEM((8 + N, WIDTH), f32),
            ],
        ),
        out_shape=outs,
        compiler_params=pltpu.CompilerParams(vmem_limit_bytes=VMEM, dimension_semantics=("arbitrary",)),
        cost_estimate=pl.CostEstimate(flops=24 * rows * width * model, bytes_accessed=16 * 2**20, transcendentals=0),
        name="input_grads",
    )(*operands)


def padded(rows):
    return max(rows, 16)


def share_rows(values, share, rows):
    taken = values[share * rows : (share + 1) * rows]
    if rows < padded(rows):
        taken = jnp.concatenate([taken, jnp.zeros((padded(rows) - rows, values.shape[1]), values.dtype)], axis=0)
    return taken.astype(bf16)


def weight_grad_kernel(gated_ref, gate_ref, cot_ref, turned_ref, packed_ref, *, part):
    j = pl.program_id(0)
    count = packed_ref.shape[0]
    model = cot_ref.shape[1]
    rows_each = model // count
    rows_pad = padded(rows_each)
    product = contract_rows(gated_ref[...], cot_ref[...])
    for q in range(WIDTH // part):
        packed_ref[j * (WIDTH // part) + q, : padded(part), :] = share_rows(product, q, part)
    product = jnp.dot(turned_ref[...], gate_ref[...], preferred_element_type=f32)
    each = model // WIDTH
    at = pl.ds(pl.multiple_of(padded(part) + (j // each) * rows_pad, 16), rows_pad)
    cols = pl.ds(pl.multiple_of((j % each) * WIDTH, WIDTH), WIDTH)
    for q in range(count):
        packed_ref[q, at, cols] = share_rows(product, q, rows_each)


def weight_grads(gated, gate_grad, cot, turned, part):
    rows, width = gated.shape
    model = cot.shape[1]
    count = width // part
    packed_rows = padded(part) + (width // model) * padded(model // count)
    return pl.pallas_call(
        functools.partial(weight_grad_kernel, part=part),
        grid=(width // WIDTH,),
        in_specs=[block_of(rows), block_of(rows), whole(cot), whole(turned)],
        out_specs=pl.BlockSpec((count, packed_rows, model), lambda j: (0, 0, 0)),
        out_shape=jax.ShapeDtypeStruct((count, packed_rows, model), bf16),
        compiler_params=pltpu.CompilerParams(vmem_limit_bytes=VMEM, dimension_semantics=("arbitrary",)),
        cost_estimate=pl.CostEstimate(flops=4 * rows * width * model, bytes_accessed=14 * 2**20, transcendentals=0),
        name="weight_grads",
    )(gated, gate_grad, cot, turned)


def share_kernel(place_ref, *refs, count, rank, taps, part, part_rows, picks):
    first, second = refs[:count], refs[count : 2 * count]
    summed_ref, weight_ref, gain_ref = refs[2 * count : 2 * count + 3]
    in_ref, out_ref, conv_ref, bias_ref, select_ref, rate_ref, rate_bias_ref, decay_ref, skip_ref, norm_ref = refs[
        2 * count + 3 :
    ]
    pad = padded(part_rows)
    wide = first[0].shape[2]
    model = summed_ref.shape[1]
    each = first[0].shape[1] // pad

    def total(held, at, rows):
        return sum(h[0, at : at + rows, :].astype(f32) for h in held)

    for half, held in enumerate((first, second)):
        for b in range(each):
            at = (half * each + b) * wide
            in_ref[:, at : at + wide] = total(held, b * pad, pad)[:part_rows]
    gate_at = 2 * each * wide
    for b in range((in_ref.shape[1] - gate_at) // model):
        at = padded(part) + b * pad
        in_ref[:, gate_at + b * model : gate_at + (b + 1) * model] = summed_ref[at : at + pad, :][:part_rows].astype(f32)
    out_ref[...] = summed_ref[: padded(part), :][:part].astype(f32)
    gain = jnp.sum(weight_ref[...].astype(f32) * in_ref[...], axis=1, keepdims=True)
    gain = jnp.broadcast_to(gain, (part_rows, 128))
    if part_rows < 8:
        gain = jnp.concatenate([gain, jnp.zeros((8 - part_rows, 128), f32)], axis=0)
    gains = gain_ref[...]
    gains = pltpu.roll(gains, gains.shape[1] - place_ref[0] * part_rows, 1)
    norm_ref[...] = gain.T[:1, :part_rows] / gains[:, :part_rows]
    small = total(second, each * pad, padded(part))[:part]
    turned = small[:, : wide // 2].T
    rate_ref[...] = turned[:rank]
    conv_ref[...] = turned[rank : rank + taps]
    bias_ref[...] = turned[rank + taps : rank + taps + 1]
    rate_bias_ref[...] = turned[rank + taps + 1 : rank + taps + 2]
    skip_ref[...] = turned[rank + taps + 2 : rank + taps + 3]
    decay_ref[...] = turned[rank + 8 : rank + 8 + N]
    select_ref[...] = small[:, wide // 2 : wide // 2 + picks]


def shares_of(first, second, summed, in_weight, gain, place, rank, taps, part, part_rows, picks):
    width = in_weight.shape[1]
    model = summed.shape[1]
    o = lambda *shape: jax.ShapeDtypeStruct(shape, f32)
    own = pl.BlockSpec((part_rows, width), lambda i, s: (s[0], 0))
    if part_rows % 16:
        in_weight = lax.dynamic_slice_in_dim(in_weight, place * part_rows, part_rows, 0)
        own = pl.BlockSpec((part_rows, width), lambda i, s: (0, 0))
    fixed = lambda shape: pl.BlockSpec(shape, lambda i, s: (0,) * len(shape))
    arrays = (*first, *second, summed, in_weight, gain)
    specs = [fixed(a.shape) for a in arrays]
    specs[-2] = own
    outs = (
        o(part_rows, width), o(part, model), o(taps, part), o(1, part), o(part, picks), o(rank, part), o(1, part),
        o(N, part), o(1, part), o(1, part_rows),
    )
    return pl.pallas_call(
        functools.partial(
            share_kernel, count=len(first), rank=rank, taps=taps, part=part, part_rows=part_rows, picks=picks
        ),
        grid_spec=pltpu.PrefetchScalarGridSpec(
            num_scalar_prefetch=1, grid=(1,), in_specs=specs, out_specs=[fixed(out.shape) for out in outs],
        ),
        out_shape=outs,
        compiler_params=pltpu.CompilerParams(vmem_limit_bytes=VMEM, dimension_semantics=("arbitrary",)),
        name="shares",
    )(place[None].astype(jnp.int32), *arrays)


def flip_bit(axis, bit):
    return [(i, i ^ bit) for i in range(lax.axis_size(axis))]


def bits_of(axis):
    size = lax.axis_size(axis)
    return [(axis, 1 << k) for k in range(size.bit_length() - 1)]


def places(order):
    grp = lax.axis_size("grp")
    other = jnp.arange(lax.axis_size("seq") * grp) ^ (lax.axis_index("seq") * grp + lax.axis_index("grp"))
    position = jnp.zeros_like(other)
    for axis, bit in order:
        position = 2 * position + (other // (bit * grp if axis == "seq" else bit)) % 2
    return position.astype(jnp.int32)


def pairs_of(bits):
    return [bits[i : i + 2] for i in range(0, len(bits), 2)]


def round_parts(held, bits):
    count = 1 << len(bits)
    size = held[0].shape[0] // count
    parts = [sum(h[i * size : (i + 1) * size].astype(f32) for h in held) for i in range(count)]
    return parts[:1] + [part.astype(bf16) for part in parts[1:]]


def round_trade(parts, bits):
    held = parts[:1]
    for i in range(1, len(parts)):
        flip = sum(bit for at, (axis, bit) in enumerate(bits) if (i >> (len(bits) - 1 - at)) & 1)
        held.append(lax.ppermute(parts[i], bits[0][0], flip_bit(bits[0][0], flip)))
    return held


def sum_packed(kept, sent, rounds, later):
    axis, bit = rounds[0][0]
    held = [kept, lax.ppermute(sent, axis, flip_bit(axis, bit))]
    for bits in rounds[1:]:
        parts = round_parts(held, bits)
        if later is not None:
            *parts, later = lax.optimization_barrier((*parts, later))
        held = round_trade(parts, bits)
    return held, later


def remaining_rounds(held, rounds, later):
    for bits in rounds:
        parts = round_parts(held, bits)
        if later is not None and bits is rounds[-1]:
            *parts, later = lax.optimization_barrier((*parts, later))
        held = round_trade(parts, bits)
    return held, later


def carried(block, shape, rates, backward, after=None, spans=None):
    count, mine = lax.axis_size("seq"), lax.axis_index("seq")
    blocks = lax.all_gather(block, "seq")
    if after is not None:
        blocks, after = lax.optimization_barrier((blocks, after))
    rows = shape[0] * shape[1]
    entering = jnp.zeros(shape, f32)
    for turn in range(count - 1):
        j = count - 1 - turn if backward else turn
        theirs = blocks[j].astype(f32)
        span = (theirs if spans is None else spans[j].astype(f32))[rows : rows + 2 * shape[0]]
        span = span[: shape[0]] + span[shape[0] :]
        longer = jnp.exp(span[:, None, :] * rates) * entering + theirs[:rows].reshape(shape)
        entering = jnp.where(mine < j if backward else j < mine, longer, entering)
    return entering, after, blocks


def contract_rows(left, right, kind=f32):
    return lax.dot_general(left, right, (((0,), (0,)), ((), ())), preferred_element_type=f32).astype(kind)


def shards(
    tokens,
    cotangent,
    norm_gain,
    in_weight,
    conv_weight,
    conv_bias,
    select_weight,
    rate_weight,
    rate_bias,
    decay_log,
    skip_gain,
    out_weight,
):
    nseq, length, model = tokens.shape
    inner_width = out_weight.shape[0]
    rank = rate_weight.shape[0]
    taps = conv_weight.shape[0]
    rows = nseq * length
    share_count = lax.axis_size("seq") * lax.axis_size("grp")
    tok = tokens.reshape(rows, model)
    cot = cotangent.reshape(rows, model)
    gain, skip, bias = norm_gain[None], skip_gain[None], conv_bias[None]
    pieces, grp = lax.axis_size("seq"), lax.axis_size("grp")
    halo = lax.ppermute(tokens[:, length - PAD :], "seq", [(i, i + 1) for i in range(pieces - 1)])
    halo = halo.reshape(nseq * PAD, model)
    picks, wide = rank + 2 * N, 256
    select_weight = select_weight.T
    normed, inner, before, x, slope, proj, bc = inner_side(
        tok, halo, gain, in_weight, conv_weight, bias, select_weight, nseq, length, rank
    )
    in_gate, out_gate = proj[:, rank : rank + N], proj[:, rank + N : picks]
    log = decay_log.T
    rates = -jnp.exp(log)
    bb = jnp.broadcast_to(in_gate[:, :, None], (rows, N, 128))
    ahead, dl, u = state_end(proj, rate_weight, rate_bias[None], x, log, bb, nseq, length)
    ahead, cot = lax.optimization_barrier((ahead, cot))
    turned, g, ga, gs = gate_side(normed, cot, in_weight, out_weight)
    state_shape = (nseq, N, inner_width)
    entering, _, spans = carried(ahead, state_shape, rates, False)
    cb = jnp.broadcast_to(out_gate[:, :, None], (rows, N, 128))
    sent_back = adjoint_end(dl, g, log, cb, nseq, length)
    lc = spread(out_gate, nseq, length, 1, False)
    lb = spread(in_gate, nseq, length, 2, True)
    ls = jnp.asarray(own_column(nseq * T, T, nseq, 2, 1, True))
    behind, lb, ls, u = lax.optimization_barrier((sent_back, lb, ls, u))
    states, gated, gate_grad, out_grad, shift, skip_grad = forward(
        dl, u, g, ga, gs, x, skip, bb, bc, lc, log, entering, nseq, length, 4
    )
    part, part_rows = inner_width // share_count, model // share_count
    weight_packed = weight_grads(gated, gate_grad, cot, turned, part)
    leaving, weight_packed, _ = carried(behind, state_shape, rates, True, weight_packed, spans)
    weight_sum = lax.psum_scatter(weight_packed, "seq", scatter_dimension=0, tiled=True)
    rate_low, conv_part, in_grad, decay_grad, rate_bias_grad = backward(
        dl, u, g, x, skip, cb, lb, ls, log, leaving, states, nseq, length, 4
    )
    out_grad = out_grad.reshape(rows, N) + in_gate * jnp.sum(shift, axis=1, keepdims=True)
    rank_grad = rows_dot(rate_low, rate_weight)
    pg = jnp.concatenate(
        [
            jnp.zeros((rows, wide // 2), bf16),
            rank_grad.astype(bf16),
            in_grad.reshape(rows, N).astype(bf16),
            out_grad.astype(bf16),
            jnp.zeros((rows, wide // 2 - picks), bf16),
        ],
        axis=1,
    )
    seq_bits, grp_bits = bits_of("seq"), bits_of("grp")
    order = seq_bits + grp_bits
    place = jnp.concatenate([places(order), (lax.axis_index("seq") % 2)[None].astype(jnp.int32)])
    rounds = [seq_bits[:1]] + pairs_of(seq_bits[1:]) + pairs_of(grp_bits)
    half_width = inner_width // 2

    def half(conv_part, early):
        return input_grads(
            place, conv_part, inner, before, x, slope, pg, select_weight, conv_weight, turned, halo, gain, rate_low,
            proj, decay_grad, rate_bias_grad, skip_grad, early, nseq, length, part, rank, grp,
        )

    kept, sent, first_grad, first_tail, first_head, early = half(conv_part, None)
    sent, gated = lax.optimization_barrier((sent, gated))
    wide_tok = tok.astype(f32)
    block_out = wide_tok + jnp.dot(gated, out_weight, preferred_element_type=f32)
    first_held, (conv_part, block_out) = sum_packed(kept, sent, rounds[:2], (conv_part, block_out))
    kept, sent, second_grad, second_tail, second_head = half(conv_part, early)
    head = jnp.concatenate([first_head, second_head], axis=1)
    *first_held, sent, head, weight_sum = lax.optimization_barrier((*first_held, sent, head, weight_sum))
    head = head.reshape(nseq, PAD, inner_width)[:, : taps - 1].astype(bf16)
    returned = lax.ppermute(head, "seq", [(i + 1, i) for i in range(pieces - 1)]).astype(f32)
    held, (gate_grad, *first_held) = sum_packed(kept, sent, rounds[:2], (gate_grad, *first_held))
    normed_grad = rows_dot(gate_grad, in_weight[:, inner_width:])
    *first_held, normed_grad = lax.optimization_barrier((*first_held, normed_grad))
    first_held, _ = remaining_rounds(first_held, rounds[2:], None)
    held, (returned, second_grad, normed_grad, second_tail) = remaining_rounds(
        held, rounds[2:], (returned, second_grad, normed_grad, second_tail)
    )
    weight_share = lax.psum_scatter(weight_sum, "grp", scatter_dimension=0, tiled=True)[0]
    in_share, out_share, conv_share, bias_share, select_share, rate_share, rate_bias_share, decay_share, skip_share, (
        gain_share
    ) = shares_of(
        first_held, held, weight_share, in_weight, gain, lax.axis_index("seq") * grp + lax.axis_index("grp"), rank,
        taps, part, part_rows, picks,
    )
    tail = jnp.concatenate([first_tail, second_tail], axis=1)
    fixed = (tail.reshape(nseq, PAD, inner_width)[:, PAD - taps + 1 :] + returned).astype(bf16)

    def patched(grad, at):
        rows_of = grad.reshape(nseq, length, half_width)
        rows_of = rows_of.at[:, length - taps + 1 :].set(fixed[:, :, at : at + half_width])
        return rows_of.reshape(rows, half_width)

    normed_grad = (
        normed_grad
        + rows_dot(patched(first_grad, 0), in_weight[:, :half_width])
        + rows_dot(patched(second_grad, half_width), in_weight[:, half_width:inner_width])
    )
    scale = lax.rsqrt(jnp.mean(wide_tok * wide_tok, axis=1, keepdims=True) + epsilon)
    lifted = normed_grad * norm_gain
    dots = jnp.mean(lifted * wide_tok, axis=1, keepdims=True)
    tokens_grad = cot.astype(f32) + scale * lifted - wide_tok * (scale * scale * scale) * dots
    return (
        block_out.astype(bf16).reshape(tokens.shape),
        tokens_grad.astype(bf16).reshape(tokens.shape),
        gain_share[0],
        in_share,
        conv_share,
        bias_share[0],
        select_share,
        rate_share,
        rate_bias_share[0],
        decay_share.T,
        skip_share[0],
        out_share,
    )


def solution(mesh):
    sharded = P("grp", "seq", None)
    shares = ("seq", "grp")
    return jax.shard_map(
        shards,
        mesh=mesh,
        in_specs=(sharded, sharded) + (P(),) * 10,
        out_specs=(
            sharded,
            sharded,
            P(shares),
            P(shares, None),
            P(None, shares),
            P(shares),
            P(shares, None),
            P(None, shares),
            P(shares),
            P(shares, None),
            P(shares),
            P(shares, None),
        ),
        check_vma=False,
    )
```
